256 devices in a mesh: loop: 32 (over z, y_hi, core), dp: 8 (over x, y_lo).
Axes of the slice: x: 4, y: 4 (y_hi: 2, y_lo: 2; y = y_hi * 2 + y_lo), z: 8, core: 2. Of those that a mesh axis runs over, the one named last changes fastest.
Arguments:
- sensor_feats: bfloat16 [8, 4096, 1152], P('dp', 'loop'), may hold values from -6 to 6
- text_embeds: bfloat16 [8, 4096, 1024], P('dp', 'loop'), may hold values from -6 to 6
- proj_weight: bfloat16 [1152, 1024], replicated, may hold values from -0.1875 to 0.1875
- matches: int32 [8, 4096], P('dp', 'loop'), may hold values from 0 to 4095, each once within a row
- log_scale: float32 [], replicated, may hold values from 2 to 2.6
- logit_bias: float32 [], replicated, may hold values from -3 to -1
Outputs:
- sensor_grad: bfloat16 [8, 4096, 1152], P('dp', 'loop')
- text_grad: float32 [8, 4096, 1024], P('dp', 'loop')
- weight_grad: float32 [1152, 1024], P('loop')
The draws below stay inside these ranges and needn't reach their ends.
Inputs may be any that keep to these rules, and one draw needn't show every extreme that they name: `matches`: within each group every index appears exactly once.
All inputs are finite; a program needn't handle non-finite values.
Results may differ from the reference program's by a relative error of at most 0.0068.
Values may be sent and summed in bfloat16 or wider, within the bound.
No kernel may reach another device: no remote copies, remote signals or barrier semaphores. Data moves between devices by JAX's collectives and lax.ppermute only.
A program may use at most 64 MiB of HBM per device.

```python
import jax
import jax.numpy as jnp
from jax import lax

D = 1024
FEAT = 1152
PAIRS = 4096
GROUPS = 8


def with_spikes(entries, own_key, source, target, shards_of, factor):
    def block_of(position):
        return (jnp.arange(entries.shape[position]) // (entries.shape[position] // shards_of)).reshape((-1,) + (1,) * (entries.ndim - 1 - position))

    near = jax.random.permutation(own_key, shards_of)[block_of(target)]
    second = (block_of(target) + shards_of // 2) % shards_of
    return jnp.where((block_of(source) == near) | (block_of(source) == second), factor * entries, entries)


def steps_of(stream_key, shape, shards, low, largest):
    gain, own = 1.0, jax.random.fold_in(stream_key, 6)
    for dim, blocks in shards:
        draws = jnp.exp(jax.random.uniform(jax.random.fold_in(own, dim), (blocks,), jnp.float32, low / len(shards), largest / len(shards)))
        gain = gain * jnp.repeat(draws, shape[dim] // blocks).reshape([-1 if axis == dim else 1 for axis in range(len(shape))])
    return gain


def scatter_about(rng, dims, width, most, shards=(), kind=jnp.bfloat16):
    factor_of = steps_of(rng, dims, shards, -0.22, 0.18) if shards else 1.0
    drawn = jax.random.normal(rng, dims, jnp.float32) * width * factor_of
    return jnp.minimum(jnp.maximum(drawn, -most), most).astype(kind)


def bell_draw_with(own_key, shape, spread, bound, shards, heavy, kind=jnp.bfloat16):
    result = spread * jax.random.normal(own_key, shape, jnp.float32)
    if shards:
        result = result * steps_of(own_key, shape, shards, -0.22, 0.18)
    return jnp.clip(with_spikes(result, jax.random.fold_in(own_key, 3), *heavy), -bound, bound).astype(kind)


def setup_inputs(seed: int = 0) -> dict:
    key_of = jax.random.split(jax.random.key(seed), 7)
    sensor_feats = bell_draw_with(key_of[0], (GROUPS, PAIRS, FEAT), 1.0, 6.0, ((0, 8), (1, 32)), (1, 2, 32, 2.75))
    text_embeds = scatter_about(key_of[1], (GROUPS, PAIRS, D), 1.0, 6.0, ((0, 8), (1, 32)))
    proj_weight = scatter_about(key_of[2], (FEAT, D), FEAT ** -0.5, 0.1875)
    matches = jax.vmap(lambda own: jax.random.permutation(own, PAIRS))(jax.random.split(key_of[3], GROUPS)).reshape((GROUPS, PAIRS)).astype(jnp.int32)
    log_scale = jnp.clip(jax.random.uniform(key_of[4], (), jnp.float32, 2.0, 2.6), 2.0, 2.6)
    logit_bias = jnp.clip(jax.random.uniform(key_of[5], (), jnp.float32, -3.0, -1.0), -3.0, -1.0)
    return {"sensor_feats": sensor_feats, "text_embeds": text_embeds, "proj_weight": proj_weight, "matches": matches, "log_scale": log_scale, "logit_bias": logit_bias}


def group_grads(sensor, texts, matched, proj_weight, log_scale, logit_bias):
    projected = jnp.dot(sensor, proj_weight, preferred_element_type=jnp.float32)
    image_inv = lax.rsqrt(lax.optimization_barrier(jnp.sum(projected * projected, -1, keepdims=True)) + 1e-06)
    image_unit = projected * image_inv
    image_emb = image_unit.astype(jnp.bfloat16)
    text_wide = texts.astype(jnp.float32)
    text_inv = lax.rsqrt(lax.optimization_barrier(jnp.sum(text_wide * text_wide, -1, keepdims=True)) + 1e-06)
    text_unit = text_wide * text_inv
    text_emb = text_unit.astype(jnp.bfloat16)
    block = min(512, PAIRS)
    count_blocks = PAIRS // block
    image_blocks = image_emb.astype(jnp.float32).reshape(count_blocks, block, D)
    match_blocks = matched.reshape(count_blocks, block)
    text_float = text_emb.astype(jnp.float32)
    columns = jnp.arange(PAIRS, dtype=jnp.int32)
    logit_scale = jnp.exp(log_scale)

    def step(carry, inputs):
        image_block, match_block = inputs
        logits = logit_scale * jnp.dot(image_block, text_float.T) + logit_bias
        positive = (match_block[:, None] == columns[None, :]).astype(jnp.float32)
        rounded = (jax.nn.sigmoid(logits) - positive).astype(jnp.bfloat16)
        rounded = lax.optimization_barrier(rounded)
        grads = rounded.astype(jnp.float32)
        image_part = jnp.dot(grads, text_float)
        return (carry + jnp.dot(grads.T, image_block), image_part)
    text_acc, image_parts = lax.scan(step, jnp.zeros((PAIRS, D), jnp.float32), (image_blocks, match_blocks))
    image_grad = logit_scale * image_parts.reshape(PAIRS, D)
    text_acc = logit_scale * text_acc
    proj_grad = ((image_grad - image_unit * lax.optimization_barrier(jnp.sum(image_unit * image_grad, -1, keepdims=True))) * image_inv).astype(jnp.bfloat16)
    text_grad = (text_acc - text_unit * lax.optimization_barrier(jnp.sum(text_unit * text_acc, -1, keepdims=True))) * text_inv
    sensor_grad = jnp.dot(proj_grad, proj_weight.T, preferred_element_type=jnp.float32).astype(jnp.bfloat16)
    weight_part = jnp.dot(sensor.T, proj_grad, preferred_element_type=jnp.float32)
    return (sensor_grad, text_grad, weight_part)

def reference(sensor_feats, text_embeds, proj_weight, matches, log_scale, logit_bias):

    def one_group(items):
        return group_grads(items[0], items[1], items[2], proj_weight, log_scale, logit_bias)
    sensor_grad, text_grad, weight_parts = lax.map(one_group, (sensor_feats, text_embeds, matches))
    return (sensor_grad, text_grad, lax.optimization_barrier(jnp.sum(weight_parts, 0)) / GROUPS)
```

```python
import jax
import jax.numpy as jnp
from jax import lax
from jax.sharding import PartitionSpec as P

Z, YH, CORE = 8, 2, 2
LOOP = Z * YH * CORE
DP = 8
BF16 = jnp.bfloat16
F32 = jnp.float32


def route(move):
    pairs = []
    for z in range(Z):
        for y in range(YH):
            for c in range(CORE):
                to_z, to_y, to_c = move(z, y, c)
                source = (z * YH + y) * CORE + c
                pairs.append((source, ((to_z % Z) * YH + to_y) * CORE + to_c))
    return pairs


def shift_z(block, distance):
    return lax.ppermute(block, "loop", route(lambda z, y, c: (z + distance, y, c)))


def swap_core(block):
    return lax.ppermute(block, "loop", route(lambda z, y, c: (z, y, 1 - c)))


def swap_yh(block):
    return lax.ppermute(block, "loop", route(lambda z, y, c: (z, 1 - y, c)))


def inner_rows(left, right):
    return lax.dot_general(left, right, (((1,), (1,)), ((), ())), preferred_element_type=F32)


def inner_cols(left, right):
    return lax.dot_general(left, right, (((0,), (0,)), ((), ())), preferred_element_type=F32)


def part_of(array, index, parts):
    width = array.shape[-1] // parts
    return lax.dynamic_slice_in_dim(array, index * width, width, array.ndim - 1)


def swap_blocks(array, bit, rows):
    count = array.shape[0] // rows
    blocks = [array[(s ^ bit) * rows : ((s ^ bit) + 1) * rows] for s in range(count)]
    return jnp.concatenate(blocks, 0)


def on_device(sensor_feats, text_embeds, proj_weight, matches, log_scale, logit_bias):
    sensor = sensor_feats[0]
    texts = text_embeds[0]
    rows = sensor.shape[0]
    feat, width = proj_weight.shape
    loop_index = lax.axis_index("loop")
    z = loop_index // (YH * CORE)
    yh = (loop_index // CORE) % YH
    core = loop_index % CORE
    logit_scale = jnp.exp(log_scale)

    text_wide = texts.astype(F32)
    text_inv = lax.rsqrt(jnp.sum(text_wide * text_wide, -1, keepdims=True) + 1e-06)
    text_unit = text_wide * text_inv
    text_emb = text_unit.astype(BF16)
    half = rows // 2
    slot = {0: text_emb}
    slot[1] = shift_z(text_emb, -1)
    slot[-1] = shift_z(text_emb, 1)
    slot[2] = shift_z(text_emb, -2)
    slot[-2] = shift_z(text_emb, 2)

    sensor_yh = swap_yh(sensor)
    sensor_rows = jnp.concatenate([sensor, swap_core(sensor), sensor_yh, swap_core(sensor_yh)], 0)
    match = matches.reshape(1, rows)
    match_pair = jnp.concatenate([match, swap_core(match)], 1)
    match_rows = jnp.concatenate([match_pair, swap_yh(match_pair)], 1).reshape(4 * rows, 1)

    slot[3] = shift_z(slot[2], -1)
    slot[-3] = shift_z(slot[-2], 1)
    slot[4] = jnp.concatenate([shift_z(slot[2][:half], -2), shift_z(slot[-2][half:], 2)], 0)

    projected = jnp.dot(sensor_rows, proj_weight, preferred_element_type=F32)
    image_inv = lax.rsqrt(jnp.sum(projected * projected, -1, keepdims=True) + 1e-06)
    image_unit = projected * image_inv
    image_emb = image_unit.astype(BF16)

    def grads_of(keys):
        piece = jnp.concatenate([slot[k] for k in keys], 0)
        logits = logit_scale * inner_rows(image_emb, piece) + logit_bias
        own = jnp.arange(rows, dtype=jnp.int32)
        columns = jnp.concatenate(
            [own + (((z + k) % Z) * YH * CORE + yh * CORE + core) * rows for k in keys]
        )
        positive = (match_rows == columns[None, :]).astype(F32)
        grads = (jax.nn.sigmoid(logits) - positive).astype(BF16)
        image_part = jnp.dot(grads, piece, preferred_element_type=F32)
        text_part = inner_cols(grads, image_emb)
        return image_part, {k: text_part[n * rows : (n + 1) * rows] for n, k in enumerate(keys)}

    image_near, text_acc = grads_of((-2, -1, 0, 1, 2))
    image_far, text_far = grads_of((-3, 3, 4))
    image_acc = logit_scale * (image_near + image_far)

    text_far = {k: v.astype(BF16) for k, v in text_far.items()}
    from_below = shift_z(text_far[3], 1)
    from_above = shift_z(text_far[-3], -1)
    far_below = shift_z(text_far[4][:half], 2)
    far_above = shift_z(text_far[4][half:], -2)
    beside_below = shift_z(text_acc[1].astype(BF16), 1)
    beside_above = shift_z(text_acc[-1].astype(BF16), -1)
    nil = jnp.zeros((half, width), F32)
    up = text_acc[2] + from_below.astype(F32) + jnp.concatenate([far_below.astype(F32), nil], 0)
    down = text_acc[-2] + from_above.astype(F32) + jnp.concatenate([nil, far_above.astype(F32)], 0)
    up = shift_z(up.astype(BF16), 2)
    down = shift_z(down.astype(BF16), -2)

    dot = jnp.sum(image_unit * image_acc, -1).reshape(4, rows)
    sent = part_of(image_acc, 1 - core, 2).astype(BF16)
    kept = part_of(image_acc, core, 2)
    kept = kept + swap_blocks(swap_core(sent), 1, rows).astype(F32)
    dot = dot + swap_blocks(swap_core(dot), 1, 1)
    sent = part_of(kept, 1 - yh, 2).astype(BF16)
    kept = part_of(kept, yh, 2)
    kept = kept + swap_blocks(swap_yh(sent), 2, rows).astype(F32)
    dot = dot + swap_blocks(swap_yh(dot), 2, 1)
    quarter = core * 2 + yh
    unit_part = part_of(image_unit, quarter, 4)
    proj_grad = ((kept - unit_part * dot.reshape(4 * rows, 1)) * image_inv).astype(BF16)

    per_loop = feat // LOOP
    strip = per_loop // 4
    place = jnp.arange(feat, dtype=jnp.int32)
    rest = place % (feat // 4)
    wanted = (rest // strip) * per_loop + (place // (feat // 4)) * strip + rest % strip
    permutation = (jnp.arange(feat, dtype=jnp.int32)[:, None] == wanted[None, :]).astype(BF16)
    sensor_sorted = jnp.dot(sensor_rows, permutation, preferred_element_type=F32).astype(BF16)
    weight_part = inner_cols(sensor_sorted, proj_grad).astype(BF16)
    lanes = width // 8
    weight_part = weight_part.reshape(4, feat // 4, 2, lanes).transpose(0, 2, 1, 3)
    weight_part = lax.all_to_all(weight_part.reshape(DP, feat // 4, lanes), "dp", 0, 0, tiled=True)
    weight_part = jnp.sum(weight_part.astype(F32), 0).astype(BF16)
    weight_part = weight_part.reshape(LOOP, strip, lanes)
    weight_part = lax.all_to_all(weight_part, "loop", 0, 0, tiled=True)
    weight_part = jnp.sum(weight_part.reshape(Z, YH * CORE, strip, lanes).astype(F32), 0)
    weight_part = weight_part * (1.0 / DP)
    shares = jnp.broadcast_to(weight_part[None], (DP,) + weight_part.shape)
    shares = lax.all_to_all(shares, "dp", 0, 0, tiled=True)
    shares = shares.reshape(4, 2, YH, CORE, strip, lanes).transpose(0, 4, 3, 2, 1, 5)
    weight_grad = shares.reshape(per_loop, width)

    from_yh = swap_yh(proj_grad[2 * rows :])
    mine = proj_grad[: 2 * rows]
    pair = jnp.where(
        yh == 0, jnp.concatenate([mine, from_yh], 1), jnp.concatenate([from_yh, mine], 1)
    )
    from_core = swap_core(pair[rows:])
    mine = pair[:rows]
    own_grad = jnp.where(
        core == 0, jnp.concatenate([mine, from_core], 1), jnp.concatenate([from_core, mine], 1)
    )
    sensor_grad = inner_rows(own_grad, proj_weight).astype(BF16)

    text_sum = text_acc[0] + beside_below.astype(F32) + beside_above.astype(F32)
    text_sum = logit_scale * (text_sum + up.astype(F32) + down.astype(F32))
    text_grad = (text_sum - text_unit * jnp.sum(text_unit * text_sum, -1, keepdims=True)) * text_inv
    return (sensor_grad[None], text_grad[None], weight_grad)


def solution(mesh):
    placed = (P("dp", "loop", None), P("dp", "loop", None), P(), P("dp", "loop"), P(), P())
    return jax.shard_map(
        on_device,
        mesh=mesh,
        in_specs=placed,
        out_specs=(P("dp", "loop", None), P("dp", "loop", None), P("loop", None)),
        check_vma=False,
    )
```

```python
import jax
import jax.numpy as jnp
from jax import lax
from jax.sharding import PartitionSpec as P

Z, YH, CORE = 8, 2, 2
LOOP = Z * YH * CORE
DP = 8
BF16 = jnp.bfloat16
F32 = jnp.float32


def route(move):
    pairs = []
    for z in range(Z):
        for y in range(YH):
            for c in range(CORE):
                to_z, to_y, to_c = move(z, y, c)
                source = (z * YH + y) * CORE + c
                pairs.append((source, ((to_z % Z) * YH + to_y) * CORE + to_c))
    return pairs


def shift_z(block, distance):
    return lax.ppermute(block, "loop", route(lambda z, y, c: (z + distance, y, c)))


def swap_core(block):
    return lax.ppermute(block, "loop", route(lambda z, y, c: (z, y, 1 - c)))


def swap_yh(block):
    return lax.ppermute(block, "loop", route(lambda z, y, c: (z, 1 - y, c)))


def inner_rows(left, right):
    return lax.dot_general(left, right, (((1,), (1,)), ((), ())), preferred_element_type=F32)


def inner_cols(left, right):
    return lax.dot_general(left, right, (((0,), (0,)), ((), ())), preferred_element_type=F32)


def part_of(array, index, parts):
    width = array.shape[-1] // parts
    return lax.dynamic_slice_in_dim(array, index * width, width, array.ndim - 1)


def swap_blocks(array, bit, rows):
    count = array.shape[0] // rows
    blocks = [array[(s ^ bit) * rows : ((s ^ bit) + 1) * rows] for s in range(count)]
    return jnp.concatenate(blocks, 0)


def on_device(sensor_feats, text_embeds, proj_weight, matches, log_scale, logit_bias):
    sensor = sensor_feats[0]
    texts = text_embeds[0]
    rows = sensor.shape[0]
    feat, width = proj_weight.shape
    loop_index = lax.axis_index("loop")
    z = loop_index // (YH * CORE)
    yh = (loop_index // CORE) % YH
    core = loop_index % CORE
    logit_scale = jnp.exp(log_scale)

    text_wide = texts.astype(F32)
    text_inv = lax.rsqrt(jnp.sum(text_wide * text_wide, -1, keepdims=True) + 1e-06)
    text_unit = text_wide * text_inv
    text_emb = text_unit.astype(BF16)
    half = rows // 2
    slot = {0: text_emb}
    for k in (1, 2, 3):
        slot[k] = shift_z(slot[k - 1], -1)
        slot[-k] = shift_z(slot[1 - k], 1)
    slot[4] = jnp.concatenate([shift_z(slot[3][:half], -1), shift_z(slot[-3][half:], 1)], 0)

    match = matches.reshape(1, rows)
    digits = jnp.concatenate([match // 64, match % 64], 0).astype(BF16)
    digits = jnp.pad(digits, ((0, 14), (0, feat - rows)))
    packet = jnp.concatenate([sensor, digits], 0)
    packet = jnp.concatenate([packet, swap_yh(packet)], 0)
    packets = jnp.stack([packet.reshape(2, rows + 16, feat), swap_core(packet).reshape(2, rows + 16, feat)], 1)
    sensor_rows = packets[:, :, :rows].reshape(4 * rows, feat)
    digits = packets[:, :, rows : rows + 2, :rows].astype(F32)
    match_rows = (digits[:, :, 0] * 64.0 + digits[:, :, 1]).reshape(4 * rows, 1)

    projected = jnp.dot(sensor_rows, proj_weight, preferred_element_type=F32)
    image_inv = lax.rsqrt(jnp.sum(projected * projected, -1, keepdims=True) + 1e-06)
    image_unit = projected * image_inv
    image_emb = image_unit.astype(BF16)

    def grads_of(keys):
        piece = jnp.concatenate([slot[k] for k in keys], 0)
        logits = logit_scale * inner_rows(image_emb, piece) + logit_bias
        own = jnp.arange(rows, dtype=jnp.int32)
        columns = jnp.concatenate(
            [own + (((z + k) % Z) * YH * CORE + yh * CORE + core) * rows for k in keys]
        )
        positive = (match_rows == columns[None, :].astype(F32)).astype(F32)
        grads = (jax.nn.sigmoid(logits) - positive).astype(BF16)
        image_part = jnp.dot(grads, piece, preferred_element_type=F32)
        text_part = inner_cols(grads, image_emb).astype(BF16)
        return image_part, {k: text_part[n * rows : (n + 1) * rows] for n, k in enumerate(keys)}

    image_acc, text_part = 0.0, {}
    for keys in ((-1, 0, 1), (-2, 2), (-3, 3), (4,)):
        image_part, parts = grads_of(keys)
        image_acc = image_acc + image_part
        text_part.update(parts)
    image_acc = logit_scale * image_acc

    turned = jnp.concatenate([text_part[k] for k in (0, 1, 2, 3, 4, -3, -2, -1)] * 2, 0)
    turned = lax.dynamic_slice_in_dim(turned, ((Z - z) % Z) * rows, Z * rows, 0)
    columns_of_z = [[(n * YH + y) * CORE + c for n in range(Z)] for y in range(YH) for c in range(CORE)]
    text_sum = lax.psum_scatter(
        turned, "loop", scatter_dimension=0, axis_index_groups=columns_of_z, tiled=True
    )

    def with_dot(block, dot):
        high = lax.reduce_precision(dot, 8, 7)
        digits = jnp.stack([high, dot - high]).astype(BF16).reshape(-1, block.shape[1])
        digits = jnp.pad(digits, ((0, 16 - digits.shape[0]), (0, 0)))
        return jnp.concatenate([block.astype(BF16), digits], 0)

    def taken(packet):
        block = packet[: 4 * rows].astype(F32)
        digits = packet[4 * rows : 4 * rows + 8 * rows // packet.shape[1]].astype(F32)
        digits = digits.reshape(2, 4, rows)
        return block, digits[0] + digits[1]

    dot = jnp.sum(image_unit * image_acc, -1).reshape(4, rows)
    other, other_dot = taken(swap_core(with_dot(part_of(image_acc, 1 - core, 2), dot)))
    kept = part_of(image_acc, core, 2) + swap_blocks(other, 1, rows)
    dot = dot + swap_blocks(other_dot, 1, 1)
    other, other_dot = taken(swap_yh(with_dot(part_of(kept, 1 - yh, 2), dot)))
    kept = part_of(kept, yh, 2) + swap_blocks(other, 2, rows)
    dot = dot + swap_blocks(other_dot, 2, 1)
    quarter = core * 2 + yh
    unit_part = part_of(image_unit, quarter, 4)
    proj_grad = ((kept - unit_part * dot.reshape(4 * rows, 1)) * image_inv).astype(BF16)

    per_loop = feat // LOOP
    strip = per_loop // 4
    place = jnp.arange(feat, dtype=jnp.int32)
    rest = place % (feat // 4)
    wanted = (rest // strip) * per_loop + (place // (feat // 4)) * strip + rest % strip
    permutation = (jnp.arange(feat, dtype=jnp.int32)[:, None] == wanted[None, :]).astype(BF16)
    sensor_sorted = jnp.dot(sensor_rows, permutation, preferred_element_type=F32).astype(BF16)
    weight_part = inner_cols(sensor_sorted, proj_grad).astype(BF16)
    lanes = width // 8
    weight_part = weight_part.reshape(4, feat // 4, 2, lanes).transpose(0, 2, 1, 3)
    weight_part = lax.all_to_all(weight_part.reshape(DP, feat // 4, lanes), "dp", 0, 0, tiled=True)
    weight_part = jnp.sum(weight_part.astype(F32), 0).astype(BF16)
    proj_grad, weight_part = lax.optimization_barrier((proj_grad, weight_part))
    weight_part = weight_part.reshape(LOOP, strip, lanes)
    weight_part = lax.all_to_all(weight_part, "loop", 0, 0, tiled=True)
    weight_part = jnp.sum(weight_part.reshape(Z, YH * CORE, strip, lanes).astype(F32), 0)
    weight_part = weight_part * (1.0 / DP)
    shares = jnp.broadcast_to(weight_part[None], (DP,) + weight_part.shape)
    shares = lax.all_to_all(shares, "dp", 0, 0, tiled=True)
    shares = shares.reshape(4, 2, YH, CORE, strip, lanes).transpose(0, 4, 3, 2, 1, 5)
    weight_grad = shares.reshape(per_loop, width)

    from_yh = swap_yh(proj_grad[2 * rows :])
    mine = proj_grad[: 2 * rows]
    pair = jnp.where(
        yh == 0, jnp.concatenate([mine, from_yh], 1), jnp.concatenate([from_yh, mine], 1)
    )
    from_core = swap_core(pair[rows:])
    mine = pair[:rows]
    own_grad = jnp.where(
        core == 0, jnp.concatenate([mine, from_core], 1), jnp.concatenate([from_core, mine], 1)
    )
    sensor_grad = inner_rows(own_grad, proj_weight).astype(BF16)

    text_sum = logit_scale * text_sum.astype(F32)
    text_grad = (text_sum - text_unit * jnp.sum(text_unit * text_sum, -1, keepdims=True)) * text_inv
    return (sensor_grad[None], text_grad[None], weight_grad)


def solution(mesh):
    placed = (P("dp", "loop", None), P("dp", "loop", None), P(), P("dp", "loop"), P(), P())
    return jax.shard_map(
        on_device,
        mesh=mesh,
        in_specs=placed,
        out_specs=(P("dp", "loop", None), P("dp", "loop", None), P("loop", None)),
        check_vma=False,
    )
```

```python
import functools

import jax
import jax.numpy as jnp
from jax import lax
from jax.experimental import pallas as pl
from jax.experimental.pallas import tpu as pltpu
from jax.sharding import PartitionSpec as P

Z, YH, CORE = 8, 2, 2
LOOP = Z * YH * CORE
DP = 8
BF16 = jnp.bfloat16
F32 = jnp.float32
VMEM = pl.BlockSpec(memory_space=pltpu.VMEM)
SMEM = pl.BlockSpec(memory_space=pltpu.SMEM)


def route(move):
    pairs = []
    for z in range(Z):
        for y in range(YH):
            for c in range(CORE):
                to_z, to_y, to_c = move(z, y, c)
                source = (z * YH + y) * CORE + c
                pairs.append((source, ((to_z % Z) * YH + to_y) * CORE + to_c))
    return pairs


def shift_z(block, distance):
    return lax.ppermute(block, "loop", route(lambda z, y, c: (z + distance, y, c)))


def swap_core(block):
    return lax.ppermute(block, "loop", route(lambda z, y, c: (z, y, 1 - c)))


def swap_yh(block):
    return lax.ppermute(block, "loop", route(lambda z, y, c: (z, 1 - y, c)))


def inner_rows(left, right):
    return lax.dot_general(left, right, (((1,), (1,)), ((), ())), preferred_element_type=F32)


def inner_cols(left, right):
    return lax.dot_general(left, right, (((0,), (0,)), ((), ())), preferred_element_type=F32)


def call(kernel, out, aliases, *operands):
    return pl.pallas_call(
        kernel,
        out_shape=out,
        in_specs=[SMEM if o.ndim == 1 else VMEM for o in operands],
        out_specs=[VMEM] * len(out),
        input_output_aliases=aliases,
        cost_estimate=pl.CostEstimate(flops=1, bytes_accessed=1, transcendentals=0),
        compiler_params=pltpu.CompilerParams(vmem_limit_bytes=40 << 20),
    )(*operands)


def block_grads(numbers, start, image_emb, match, text):
    wide = text.astype(F32)
    inv = lax.rsqrt(jnp.sum(wide * wide, -1, keepdims=True) + 1e-06)
    emb = (wide * inv).astype(BF16)
    logits = numbers[0] * inner_rows(image_emb, emb) + numbers[1]
    column = lax.broadcasted_iota(jnp.int32, logits.shape, 1) + start
    positive = (match == column.astype(F32)).astype(F32)
    return emb, (jax.nn.sigmoid(logits) - positive).astype(BF16)


def pairs_kernel(count, first, numbers, starts, image_emb, match, *refs):
    texts, refs = refs[:count], refs[count:]
    if not first:
        acc_in, refs = refs[0], refs[1:]
    acc_out, text_out = refs[0], refs[1:]
    image = image_emb[...]
    embs, grads = [], []
    for n in range(count):
        emb, grad = block_grads(numbers, starts[n], image, match[...], texts[n][...])
        embs.append(emb)
        grads.append(grad)
    emb, grad = jnp.concatenate(embs, 0), jnp.concatenate(grads, 1)
    part = jnp.dot(grad, emb, preferred_element_type=F32)
    acc_out[...] = part if first else acc_in[...] + part
    text_part = inner_cols(grad, image)
    rows = texts[0].shape[0]
    for n in range(count):
        text_out[n][...] = text_part[n * rows : (n + 1) * rows].astype(text_out[n].dtype)


def last_kernel(numbers, starts, image_emb, match, low, high, acc_in, unit, acc_out, dot_out, packet, low_out, high_out):
    image = image_emb[...]
    text = jnp.concatenate([low[...], high[...]], 0)
    emb, grad = block_grads(numbers, starts[0], image, match[...], text)
    acc = numbers[0] * (acc_in[...] + jnp.dot(grad, emb, preferred_element_type=F32))
    acc_out[...] = acc
    dot = jnp.sum(unit[...] * acc, -1, keepdims=True)
    dot_out[...] = dot
    rows, width = acc.shape
    half, quarter, block = width // 2, width // 4, rows // 4
    own = pl.multiple_of(starts[1] * half, half)
    other = pl.multiple_of((1 - starts[1]) * half, half)
    packet[:, :half] = acc_out[:, pl.ds(other, half)].astype(BF16)
    top = dot.astype(BF16).astype(F32)
    lane = lax.broadcasted_iota(jnp.int32, (rows, 128), 1)
    digits = jnp.where(lane == 0, top, jnp.where(lane == 1, dot - top, 0.0))
    packet[:, half : half + 128] = digits.astype(BF16)
    for side in range(2):
        lanes = pl.ds(pl.multiple_of(own + side * quarter, quarter), quarter)
        for n, slot in enumerate((1, 3)):
            at = (2 * side + n) * block
            packet[at : at + block, half + 128 :] = acc_out[slot * block : (slot + 1) * block, lanes].astype(BF16)
    text_part = inner_cols(grad, image).astype(BF16)
    middle = low.shape[0]
    low_out[...] = text_part[:middle]
    high_out[...] = text_part[middle:]


def weight_kernel(starts, got, acc, dot, unit, inv, sensor_sorted, weight, row_send, row_keep):
    rows, width = acc.shape
    half, quarter, block = width // 2, width // 4, rows // 4
    own = pl.ds(pl.multiple_of(starts[1] * half, half), half)
    projs = []
    for slot in range(4):
        mine = slice(slot * block, (slot + 1) * block)
        theirs = slice((slot ^ 1) * block, ((slot ^ 1) + 1) * block)
        kept = acc[mine, own] + got[theirs, :half].astype(F32)
        digits = got[theirs, half : half + 128].astype(F32)
        whole_dot = dot[mine, :] + digits[:, 0:1] + digits[:, 1:2]
        projs.append(((kept - unit[mine, own] * whole_dot) * inv[mine, :]).astype(BF16))
        if slot in (0, 2):
            target = (row_keep, row_send)[slot // 2]
            target[:, own] = kept.astype(target.dtype)
            for side in range(2):
                first = pl.multiple_of((1 - starts[1]) * half + side * quarter, quarter)
                lanes = pl.ds(first, quarter)
                at = (2 * side + slot // 2) * block
                extra = got[at : at + block, half + 128 :].astype(F32)
                target[:, lanes] = (acc[mine, lanes] + extra).astype(target.dtype)
    proj = jnp.concatenate(projs, 0)
    chunk_rows, chunk_cols = weight.shape[1:]
    for x in range(4):
        left = sensor_sorted[x * chunk_rows : (x + 1) * chunk_rows, :]
        product = jnp.dot(left, proj, preferred_element_type=F32).astype(BF16)
        for y in range(2):
            weight[2 * x + y] = product[:, y * chunk_cols : (y + 1) * chunk_cols]


def on_device(sensor_feats, text_embeds, proj_weight, matches, log_scale, logit_bias):
    sensor = sensor_feats[0]
    texts = text_embeds[0]
    rows = sensor.shape[0]
    feat, width = proj_weight.shape
    loop_index = lax.axis_index("loop")
    z = loop_index // (YH * CORE)
    core = loop_index % CORE
    logit_scale = jnp.exp(log_scale)
    numbers = jnp.stack([logit_scale, logit_bias])

    slot = {0: texts}
    for k in (1, 2, 3):
        slot[k] = shift_z(slot[k - 1], -1)
        slot[-k] = shift_z(slot[1 - k], 1)

    match = matches.reshape(1, rows)
    digits = jnp.concatenate([match // 64, match % 64], 0).astype(BF16)
    digits = jnp.pad(digits, ((0, 14), (0, feat - rows)))
    packet = jnp.concatenate([sensor, digits], 0)
    packet = jnp.concatenate([packet, swap_yh(packet)], 0)
    packets = jnp.stack([packet.reshape(2, rows + 16, feat), swap_core(packet).reshape(2, rows + 16, feat)], 1)
    sensor_rows = packets[:, :, :rows].reshape(4 * rows, feat)
    digits = packets[:, :, rows : rows + 2, :rows].astype(F32)
    match_rows = (digits[:, :, 0] * 64.0 + digits[:, :, 1]).reshape(4 * rows, 1)

    projected = jnp.dot(sensor_rows, proj_weight, preferred_element_type=F32)
    image_inv = lax.rsqrt(jnp.sum(projected * projected, -1, keepdims=True) + 1e-06)
    image_unit = projected * image_inv
    image_emb = image_unit.astype(BF16)

    per_loop = feat // LOOP
    strip = per_loop // 4
    place = jnp.arange(feat, dtype=jnp.int32)
    rest = place % (feat // 4)
    wanted = (rest // strip) * per_loop + (place // (feat // 4)) * strip + rest % strip
    permutation = (wanted[:, None] == jnp.arange(feat, dtype=jnp.int32)[None, :]).astype(BF16)
    permutation = lax.optimization_barrier(permutation)
    sensor_sorted = inner_rows(permutation, sensor_rows).astype(BF16)

    def starts_of(keys):
        return [(loop_index + k * YH * CORE) % LOOP * rows for k in keys]

    def pairs(keys, dtypes, acc):
        operands = [numbers, jnp.stack(starts_of(keys)), image_emb, match_rows, *(slot[k] for k in keys)]
        out = [jax.ShapeDtypeStruct((4 * rows, width), F32)]
        out += [jax.ShapeDtypeStruct((rows, width), d) for d in dtypes]
        aliases = {}
        if acc is not None:
            aliases = {len(operands): 0}
            operands.append(acc)
        kernel = functools.partial(pairs_kernel, len(keys), acc is None)
        return call(kernel, out, aliases, *operands)

    acc, text_0, text_1, text_m1 = pairs((0, 1, -1), (F32, BF16, BF16), None)
    acc, text_2, text_m2 = pairs((2, -2), (F32, F32), acc)
    half = rows // 2
    end_low, end_high = shift_z(slot[3][:half], -1), shift_z(slot[-3][half:], 1)
    acc, text_3, text_m3 = pairs((3, -3), (BF16, BF16), acc)
    starts = jnp.stack(starts_of((4,)) + [core])
    shapes = [((4 * rows, width), F32), ((4 * rows, 1), F32), ((4 * rows, width // 8 * 7), BF16)]
    shapes += [((half, width), BF16)] * 2
    acc, dot, packet, text_low, text_high = call(
        last_kernel,
        [jax.ShapeDtypeStruct(*s) for s in shapes],
        {6: 0},
        numbers, starts, image_emb, match_rows, end_low, end_high, acc, image_unit,
    )

    shapes = [((DP, feat // 4, width // 4), BF16), ((rows, width), BF16), ((rows, width), F32)]
    weight_part, row_send, row_keep = call(
        weight_kernel,
        [jax.ShapeDtypeStruct(*s) for s in shapes],
        {},
        starts, swap_core(packet), acc, dot, image_unit, image_inv, sensor_sorted,
    )
    weight_part = lax.all_to_all(weight_part, "dp", 0, 0, tiled=True)
    weight_part = jnp.sum(weight_part.astype(F32), 0).astype(BF16)
    weight_part = weight_part.reshape(LOOP, strip, width // 4)
    weight_part = lax.all_to_all(weight_part, "loop", 0, 0, tiled=True)
    weight_part = jnp.sum(weight_part.reshape(Z * YH, CORE, strip, width // 4).astype(F32), 0)
    weight_part = weight_part * (1.0 / DP)
    shares = jnp.broadcast_to(weight_part[None], (DP,) + weight_part.shape)
    shares = lax.all_to_all(shares, "dp", 0, 0, tiled=True)
    shares = shares.reshape(4, 2, CORE, strip, width // 4).transpose(0, 3, 2, 1, 4)
    weight_grad = shares.reshape(per_loop, width)

    text_3, text_m3, text_low, text_high, text_1, text_m1, row_send = lax.optimization_barrier(
        (text_3, text_m3, text_low, text_high, text_1, text_m1, row_send)
    )
    row_got = swap_yh(row_send)
    from_below, from_above = shift_z(text_3, 1), shift_z(text_m3, -1)
    far_below, far_above = shift_z(text_low, 2), shift_z(text_high, -2)
    near_below, near_above = shift_z(text_1, 1), shift_z(text_m1, -1)
    nil = jnp.zeros((half, width), F32)
    up = text_2 + from_below.astype(F32) + jnp.concatenate([far_below.astype(F32), nil], 0)
    down = text_m2 + from_above.astype(F32) + jnp.concatenate([nil, far_above.astype(F32)], 0)
    up, down = shift_z(up.astype(BF16), 2), shift_z(down.astype(BF16), -2)
    text_sum = text_0 + near_below.astype(F32) + near_above.astype(F32)
    text_sum = logit_scale * (text_sum + up.astype(F32) + down.astype(F32))
    text_wide = texts.astype(F32)
    text_inv = lax.rsqrt(jnp.sum(text_wide * text_wide, -1, keepdims=True) + 1e-06)
    text_unit = text_wide * text_inv
    text_grad = (text_sum - text_unit * jnp.sum(text_unit * text_sum, -1, keepdims=True)) * text_inv

    image_grad = row_keep + row_got.astype(F32)
    own_unit = image_unit[:rows]
    own_dot = jnp.sum(own_unit * image_grad, -1, keepdims=True)
    proj_grad = ((image_grad - own_unit * own_dot) * image_inv[:rows]).astype(BF16)
    sensor_grad = inner_rows(proj_grad, proj_weight).astype(BF16)
    return (sensor_grad[None], text_grad[None], weight_grad)


def solution(mesh):
    placed = (P("dp", "loop", None), P("dp", "loop", None), P(), P("dp", "loop"), P(), P())
    return jax.shard_map(
        on_device,
        mesh=mesh,
        in_specs=placed,
        out_specs=(P("dp", "loop", None), P("dp", "loop", None), P("loop", None)),
        check_vma=False,
    )
```

```python
import functools

import jax
import jax.numpy as jnp
from jax import lax
from jax.experimental import pallas as pl
from jax.experimental.pallas import tpu as pltpu
from jax.sharding import PartitionSpec as P

Z, YH, CORE = 8, 2, 2
LOOP = Z * YH * CORE
DP = 8
BF16 = jnp.bfloat16
F32 = jnp.float32
VMEM = pl.BlockSpec(memory_space=pltpu.VMEM)
SMEM = pl.BlockSpec(memory_space=pltpu.SMEM)


def route(move):
    pairs = []
    for z in range(Z):
        for y in range(YH):
            for c in range(CORE):
                to_z, to_y, to_c = move(z, y, c)
                source = (z * YH + y) * CORE + c
                pairs.append((source, ((to_z % Z) * YH + to_y) * CORE + to_c))
    return pairs


def shift_z(block, distance):
    return lax.ppermute(block, "loop", route(lambda z, y, c: (z + (1 - 2 * c) * distance, y, c)))


def swap_core(block):
    return lax.ppermute(block, "loop", route(lambda z, y, c: (z, y, 1 - c)))


def swap_yh(block):
    return lax.ppermute(block, "loop", route(lambda z, y, c: (z, 1 - y, c)))


def inner_rows(left, right):
    return lax.dot_general(left, right, (((1,), (1,)), ((), ())), preferred_element_type=F32)


def inner_cols(left, right):
    return lax.dot_general(left, right, (((0,), (0,)), ((), ())), preferred_element_type=F32)


def call(kernel, out, aliases, *operands):
    return pl.pallas_call(
        kernel,
        out_shape=out,
        in_specs=[SMEM if o.ndim == 1 else VMEM for o in operands],
        out_specs=[VMEM] * len(out),
        input_output_aliases=aliases,
        cost_estimate=pl.CostEstimate(flops=1, bytes_accessed=1, transcendentals=0),
        compiler_params=pltpu.CompilerParams(vmem_limit_bytes=20 << 20),
    )(*operands)


def block_grads(numbers, start, image_emb, match, text):
    wide = text.astype(F32)
    inv = lax.rsqrt(jnp.sum(wide * wide, -1, keepdims=True) + 1e-06)
    emb = (wide * inv).astype(BF16)
    logits = numbers[0] * inner_rows(image_emb, emb) + numbers[1]
    column = lax.broadcasted_iota(jnp.int32, logits.shape, 1) + start
    positive = (match == column.astype(F32)).astype(F32)
    return emb, (jax.nn.sigmoid(logits) - positive).astype(BF16)


def pairs_kernel(count, first, numbers, starts, image_emb, match, *refs):
    texts, refs = refs[:count], refs[count:]
    if not first:
        acc_in, refs = refs[0], refs[1:]
    acc_out, text_out = refs[0], refs[1:]
    image = image_emb[...]
    embs, grads = [], []
    for n in range(count):
        emb, grad = block_grads(numbers, starts[n], image, match[...], texts[n][...])
        embs.append(emb)
        grads.append(grad)
    emb, grad = jnp.concatenate(embs, 0), jnp.concatenate(grads, 1)
    part = jnp.dot(grad, emb, preferred_element_type=F32)
    acc_out[...] = part if first else acc_in[...] + part
    text_part = inner_cols(grad, image)
    rows = texts[0].shape[0]
    for n in range(count):
        text_out[n][...] = text_part[n * rows : (n + 1) * rows].astype(text_out[n].dtype)


def project_kernel(own, core, yh, both, proj_weight, *refs):
    matches, (unit, emb, inv_out, match_out) = refs[:4], refs[4:]
    rows = own.shape[0]
    for n, sensor in enumerate((own, core, yh, both)):
        here = slice(n * rows, (n + 1) * rows)
        projected = jnp.dot(sensor[...], proj_weight[...], preferred_element_type=F32)
        inv = lax.rsqrt(jnp.sum(projected * projected, -1, keepdims=True) + 1e-06)
        scaled = projected * inv
        unit[here, :] = scaled
        emb[here, :] = scaled.astype(BF16)
        inv_out[here, :] = inv
        match = jnp.broadcast_to(matches[n][...].astype(F32), (rows, rows))
        match_out[here, :] = match.T[:, 0:1]


def last_kernel(numbers, starts, image_emb, match, text, acc_in, unit, acc_out, dot_out, packet, grad_out):
    emb, grad = block_grads(numbers, starts[0], image_emb[...], match[...], text[...])
    grad_out[...] = grad
    acc = numbers[0] * (acc_in[...] + jnp.dot(grad, emb, preferred_element_type=F32))
    acc_out[...] = acc
    dot = jnp.sum(unit[...] * acc, -1, keepdims=True)
    dot_out[...] = dot
    rows, width = acc.shape
    half, quarter, block = width // 2, width // 4, rows // 4
    own = pl.multiple_of(starts[1] * half, half)
    other = pl.multiple_of((1 - starts[1]) * half, half)
    packet[:, :half] = acc_out[:, pl.ds(other, half)].astype(BF16)
    top = dot.astype(BF16).astype(F32)
    lane = lax.broadcasted_iota(jnp.int32, (rows, 128), 1)
    digits = jnp.where(lane == 0, top, jnp.where(lane == 1, dot - top, 0.0))
    packet[:, half : half + 128] = digits.astype(BF16)
    for side in range(2):
        lanes = pl.ds(pl.multiple_of(own + side * quarter, quarter), quarter)
        for n, slot in enumerate((1, 3)):
            at = (2 * side + n) * block
            packet[at : at + block, half + 128 :] = acc_out[slot * block : (slot + 1) * block, lanes].astype(BF16)


def last_text_kernel(grad, image_emb, out):
    out[...] = inner_cols(grad[...], image_emb[...]).astype(out.dtype)


def weight_kernel(starts, got, acc, dot, unit, inv, own_rows, core_rows, yh_rows, both_rows, weight, row_send, row_keep):
    rows, width = acc.shape
    half, quarter, block = width // 2, width // 4, rows // 4
    own = pl.ds(pl.multiple_of(starts[1] * half, half), half)
    projs = []
    for slot in range(4):
        mine = slice(slot * block, (slot + 1) * block)
        theirs = slice((slot ^ 1) * block, ((slot ^ 1) + 1) * block)
        kept = acc[mine, own] + got[theirs, :half].astype(F32)
        digits = got[theirs, half : half + 128].astype(F32)
        whole_dot = dot[mine, :] + digits[:, 0:1] + digits[:, 1:2]
        projs.append(((kept - unit[mine, own] * whole_dot) * inv[mine, :]).astype(BF16))
        if slot in (0, 2):
            target = (row_keep, row_send)[slot // 2]
            target[:, own] = kept.astype(target.dtype)
            for side in range(2):
                first = pl.multiple_of((1 - starts[1]) * half + side * quarter, quarter)
                lanes = pl.ds(first, quarter)
                at = (2 * side + slot // 2) * block
                extra = got[at : at + block, half + 128 :].astype(F32)
                target[:, lanes] = (acc[mine, lanes] + extra).astype(target.dtype)
    proj = jnp.concatenate(projs, 0)
    sensor = jnp.concatenate([own_rows[...], core_rows[...], yh_rows[...], both_rows[...]], 0)
    chunk = weight.shape[1]
    for n in range(half // 128):
        product = inner_cols(proj[:, n * 128 : (n + 1) * 128], sensor).astype(BF16)
        for m in range(128 // chunk):
            weight[n * (128 // chunk) + m] = product[m * chunk : (m + 1) * chunk]


def chunk_kernel(parts, out):
    total = parts[0].astype(F32)
    for n in range(1, parts.shape[0]):
        total = total + parts[n].astype(F32)
    turned = total.T
    count, rows, lanes = out.shape
    for n in range(count):
        at = 2 * rows * n
        out[n] = jnp.concatenate([turned[at : at + rows], turned[at + rows : at + 2 * rows]], 1).astype(BF16)


def share_kernel(parts, out):
    for core in range(CORE):
        total = parts[core].astype(F32)
        for n in range(1, Z * YH):
            total = total + parts[n * CORE + core].astype(F32)
        total = total * (1.0 / DP)
        for n in range(DP):
            out[n, core] = total


def layout_kernel(shares, out):
    rows, lanes = shares.shape[2:]
    cols = lanes // 2
    for core in range(CORE):
        for pair in range(DP // 2):
            left, right = shares[2 * pair, core], shares[2 * pair + 1, core]
            at = core * DP * cols + pair * lanes
            out[:rows, at : at + lanes] = jnp.concatenate([left[:, :cols], right[:, :cols]], 1)
            out[rows:, at : at + lanes] = jnp.concatenate([left[:, cols:], right[:, cols:]], 1)


def on_device(sensor_feats, text_embeds, proj_weight, matches, log_scale, logit_bias):
    sensor = sensor_feats[0]
    texts = text_embeds[0]
    rows = sensor.shape[0]
    feat, width = proj_weight.shape
    loop_index = lax.axis_index("loop")
    z = loop_index // (YH * CORE)
    core = loop_index % CORE
    logit_scale = jnp.exp(log_scale)
    numbers = jnp.stack([logit_scale, logit_bias])

    slot = {0: texts}
    for k in (1, 2, 3):
        slot[k] = shift_z(slot[k - 1], -1)
        slot[-k] = shift_z(slot[1 - k], 1)
    slot[4] = shift_z(slot[-3], 1)

    sensor_yh = swap_yh(sensor)
    sensors = [sensor, swap_core(sensor), sensor_yh, swap_core(sensor_yh)]
    match = matches.reshape(1, rows)
    match_yh = swap_yh(match)
    match_both = swap_core(jnp.concatenate([match, match_yh], 0))
    match = [match, match_both[:1], match_yh, match_both[1:]]
    shapes = [((4 * rows, width), F32), ((4 * rows, width), BF16), ((4 * rows, 1), F32), ((4 * rows, 1), F32)]
    image_unit, image_emb, image_inv, match_rows = call(
        project_kernel, [jax.ShapeDtypeStruct(*s) for s in shapes], {}, *sensors, proj_weight, *match
    )

    def starts_of(keys):
        step = (1 - 2 * core) * YH * CORE
        return [(loop_index + k * step + LOOP) % LOOP * rows for k in keys]

    def pairs(keys, dtypes, acc):
        operands = [numbers, jnp.stack(starts_of(keys)), image_emb, match_rows, *(slot[k] for k in keys)]
        out = [jax.ShapeDtypeStruct((4 * rows, width), F32)]
        out += [jax.ShapeDtypeStruct((rows, width), d) for d in dtypes]
        aliases = {}
        if acc is not None:
            aliases = {len(operands): 0}
            operands.append(acc)
        kernel = functools.partial(pairs_kernel, len(keys), acc is None)
        return call(kernel, out, aliases, *operands)

    acc, text_0, text_1, text_m1, text_2, text_m2 = pairs((0, 1, -1, 2, -2), (F32, BF16, BF16, F32, F32), None)
    acc, text_3, text_m3 = pairs((3, -3), (BF16, BF16), acc)
    starts = jnp.stack(starts_of((4,)) + [core])
    shapes = [((4 * rows, width), F32), ((4 * rows, 1), F32), ((4 * rows, width // 8 * 7), BF16), ((4 * rows, rows), BF16)]
    acc, dot, packet, last_grad = call(
        last_kernel,
        [jax.ShapeDtypeStruct(*s) for s in shapes],
        {5: 0},
        numbers, starts, image_emb, match_rows, slot[4], acc, image_unit,
    )
    (text_4,) = call(last_text_kernel, [jax.ShapeDtypeStruct((rows, width), BF16)], {}, last_grad, image_emb)

    shapes = [((DP, width // 16, feat), BF16), ((rows, width), BF16), ((rows, width), F32)]
    weight_part, row_send, row_keep = call(
        weight_kernel,
        [jax.ShapeDtypeStruct(*s) for s in shapes],
        {},
        starts, swap_core(packet), acc, dot, image_unit, image_inv, *sensors,
    )
    weight_part = lax.all_to_all(weight_part, "dp", 0, 0, tiled=True)
    per_loop = feat // LOOP
    block = (per_loop // 2, width // 8)
    (weight_part,) = call(chunk_kernel, [jax.ShapeDtypeStruct((LOOP,) + block, BF16)], {}, weight_part)
    text_2, text_m2, weight_part = lax.optimization_barrier((text_2, text_m2, weight_part))
    weight_part = lax.all_to_all(weight_part, "loop", 0, 0, tiled=True)
    (shares,) = call(share_kernel, [jax.ShapeDtypeStruct((DP, CORE) + block, F32)], {}, weight_part)
    shares = lax.all_to_all(shares, "dp", 0, 0, tiled=True)
    (weight_grad,) = call(layout_kernel, [jax.ShapeDtypeStruct((per_loop, width), F32)], {}, shares)

    text_3, text_m3, text_4, text_1, text_m1, row_send = lax.optimization_barrier(
        (text_3, text_m3, text_4, text_1, text_m1, row_send)
    )
    row_got = swap_yh(row_send)
    from_below, from_above, far = shift_z(text_3, 1), shift_z(text_m3, -1), shift_z(text_4, 2)
    near_below, near_above = shift_z(text_1, 1), shift_z(text_m1, -1)
    up = text_2 + from_below.astype(F32) + far.astype(F32)
    down = text_m2 + from_above.astype(F32)
    up, down = shift_z(up.astype(BF16), 2), shift_z(down.astype(BF16), -2)
    text_sum = text_0 + near_below.astype(F32) + near_above.astype(F32)
    text_sum = logit_scale * (text_sum + up.astype(F32) + down.astype(F32))
    text_wide = texts.astype(F32)
    text_inv = lax.rsqrt(jnp.sum(text_wide * text_wide, -1, keepdims=True) + 1e-06)
    text_unit = text_wide * text_inv
    text_grad = (text_sum - text_unit * jnp.sum(text_unit * text_sum, -1, keepdims=True)) * text_inv

    image_grad = row_keep + row_got.astype(F32)
    own_unit = image_unit[:rows]
    own_dot = jnp.sum(own_unit * image_grad, -1, keepdims=True)
    proj_grad = ((image_grad - own_unit * own_dot) * image_inv[:rows]).astype(BF16)
    sensor_grad = inner_rows(proj_grad, proj_weight).astype(BF16)
    return (sensor_grad[None], text_grad[None], weight_grad)


def solution(mesh):
    placed = (P("dp", "loop", None), P("dp", "loop", None), P(), P("dp", "loop"), P(), P())
    return jax.shard_map(
        on_device,
        mesh=mesh,
        in_specs=placed,
        out_specs=(P("dp", "loop", None), P("dp", "loop", None), P("loop", None)),
        check_vma=False,
    )
```

```python
import functools

import jax
import jax.numpy as jnp
from jax import lax
from jax.experimental import pallas as pl
from jax.experimental.pallas import tpu as pltpu
from jax.sharding import PartitionSpec as P

Z, YH, CORE = 8, 2, 2
LOOP = Z * YH * CORE
DP = 8
BF16 = jnp.bfloat16
F32 = jnp.float32
VMEM = pl.BlockSpec(memory_space=pltpu.VMEM)
HBM = pl.BlockSpec(memory_space=pltpu.HBM)
SMEM = pl.BlockSpec(memory_space=pltpu.SMEM)


def route(move):
    pairs = []
    for z in range(Z):
        for y in range(YH):
            for c in range(CORE):
                to_z, to_y, to_c = move(z, y, c)
                source = (z * YH + y) * CORE + c
                pairs.append((source, ((to_z % Z) * YH + to_y) * CORE + to_c))
    return pairs


def shift_z(block, distance):
    return lax.ppermute(block, "loop", route(lambda z, y, c: (z + (1 - 2 * c) * distance, y, c)))


def swap_core(block):
    return lax.ppermute(block, "loop", route(lambda z, y, c: (z, y, 1 - c)))


def swap_yh(block):
    return lax.ppermute(block, "loop", route(lambda z, y, c: (z, 1 - y, c)))


def inner_rows(left, right):
    return lax.dot_general(left, right, (((1,), (1,)), ((), ())), preferred_element_type=F32)


def inner_cols(left, right):
    return lax.dot_general(left, right, (((0,), (0,)), ((), ())), preferred_element_type=F32)


def call(kernel, out, aliases, *operands, far=(), late=(), far_out=()):
    far, far_out, total = list(far), list(far_out), len(operands)

    def body(*refs):
        ins, outs, scratch = refs[:total], refs[total : total + len(out)], refs[total + len(out) :]
        held, held_out = scratch[: len(far)], scratch[len(far) : len(far) + len(far_out)]
        sems = scratch[len(far) + len(far_out)]
        loads = [pltpu.make_async_copy(ins[n], held[m], sems.at[m]) for m, n in enumerate(far)]
        for load in loads:
            load.start()
        for m, n in enumerate(far):
            if n not in late:
                loads[m].wait()

        def ready():
            for m, n in enumerate(far):
                if n in late:
                    loads[m].wait()

        ins = [held[far.index(n)] if n in far else ref for n, ref in enumerate(ins)]
        local = [held_out[far_out.index(n)] if n in far_out else ref for n, ref in enumerate(outs)]
        kernel(ready, *ins, *local)
        stores = [pltpu.make_async_copy(held_out[m], outs[n], sems.at[len(far) + m]) for m, n in enumerate(far_out)]
        for store in stores:
            store.start()
        for store in stores:
            store.wait()

    in_specs = [SMEM if o.ndim == 1 else HBM if n in far else VMEM for n, o in enumerate(operands)]
    scratch = [pltpu.VMEM(operands[n].shape, operands[n].dtype) for n in far]
    scratch += [pltpu.VMEM(out[n].shape, out[n].dtype) for n in far_out]
    scratch.append(pltpu.SemaphoreType.DMA((max(1, len(far) + len(far_out)),)))
    operands = [pltpu.with_memory_space_constraint(o, pltpu.HBM) if n in far else o for n, o in enumerate(operands)]
    return pl.pallas_call(
        body,
        out_shape=[pltpu.HBM(o.shape, o.dtype) if n in far_out else o for n, o in enumerate(out)],
        in_specs=in_specs,
        out_specs=[HBM if n in far_out else VMEM for n in range(len(out))],
        scratch_shapes=scratch,
        input_output_aliases=aliases,
        cost_estimate=pl.CostEstimate(flops=1, bytes_accessed=1, transcendentals=0),
        compiler_params=pltpu.CompilerParams(vmem_limit_bytes=20 << 20),
    )(*operands)


def block_grads(numbers, start, image_emb, match, text):
    wide = text.astype(F32)
    inv = lax.rsqrt(jnp.sum(wide * wide, -1, keepdims=True) + 1e-06)
    emb = (wide * inv).astype(BF16)
    logits = numbers[0] * inner_rows(image_emb, emb) + numbers[1]
    column = lax.broadcasted_iota(jnp.int32, logits.shape, 1) + start
    positive = (match == column.astype(F32)).astype(F32)
    return emb, (jax.nn.sigmoid(logits) - positive).astype(BF16)


def pairs_kernel(count, first, ready, numbers, starts, image_emb, match, *refs):
    texts, refs = refs[:count], refs[count:]
    if not first:
        acc_in, refs = refs[0], refs[1:]
    acc_out, text_out = refs[0], refs[1:]
    image = image_emb[...]
    embs, grads = [], []
    for n in range(count):
        emb, grad = block_grads(numbers, starts[n], image, match[...], texts[n][...])
        embs.append(emb)
        grads.append(grad)
    emb, grad = jnp.concatenate(embs, 0), jnp.concatenate(grads, 1)
    part = jnp.dot(grad, emb, preferred_element_type=F32)
    acc_out[...] = part if first else acc_in[...] + part
    text_part = inner_cols(grad, image)
    rows = texts[0].shape[0]
    for n in range(count):
        text_out[n][...] = text_part[n * rows : (n + 1) * rows].astype(text_out[n].dtype)


def project_kernel(ready, own, core, yh, both, proj_weight, *refs):
    matches, (unit, emb, inv_out, match_out) = refs[:4], refs[4:]
    rows = own.shape[0]
    for n, sensor in enumerate((own, core, yh, both)):
        here = slice(n * rows, (n + 1) * rows)
        projected = jnp.dot(sensor[...], proj_weight[...], preferred_element_type=F32)
        inv = lax.rsqrt(jnp.sum(projected * projected, -1, keepdims=True) + 1e-06)
        scaled = projected * inv
        unit[here, :] = scaled
        emb[here, :] = scaled.astype(BF16)
        inv_out[here, :] = inv
        match = jnp.broadcast_to(matches[n][...].astype(F32), (rows, rows))
        match_out[here, :] = match.T[:, 0:1]


def last_kernel(ready, numbers, starts, image_emb, match, text, acc_in, unit, acc_out, dot_out, packet, grad_out):
    emb, grad = block_grads(numbers, starts[0], image_emb[...], match[...], text[...])
    grad_out[...] = grad
    acc = numbers[0] * (acc_in[...] + jnp.dot(grad, emb, preferred_element_type=F32))
    acc_out[...] = acc
    ready()
    dot = jnp.sum(unit[...] * acc, -1, keepdims=True)
    dot_out[...] = dot
    rows, width = acc.shape
    half, quarter, block = width // 2, width // 4, rows // 4
    own = pl.multiple_of(starts[1] * half, half)
    other = pl.multiple_of((1 - starts[1]) * half, half)
    packet[:, :half] = acc_out[:, pl.ds(other, half)].astype(BF16)
    top = dot.astype(BF16).astype(F32)
    lane = lax.broadcasted_iota(jnp.int32, (rows, 128), 1)
    digits = jnp.where(lane == 0, top, jnp.where(lane == 1, dot - top, 0.0))
    packet[:, half : half + 128] = digits.astype(BF16)
    for side in range(2):
        lanes = pl.ds(pl.multiple_of(own + side * quarter, quarter), quarter)
        for n, slot in enumerate((1, 3)):
            at = (2 * side + n) * block
            packet[at : at + block, half + 128 :] = acc_out[slot * block : (slot + 1) * block, lanes].astype(BF16)


def last_text_kernel(ready, grad, image_emb, out):
    out[...] = inner_cols(grad[...], image_emb[...]).astype(out.dtype)


def weight_kernel(ready, starts, got, acc, dot, unit, inv, own_rows, core_rows, yh_rows, both_rows, weight, row_send, row_keep):
    rows, width = acc.shape
    half, quarter, block = width // 2, width // 4, rows // 4
    own = pl.ds(pl.multiple_of(starts[1] * half, half), half)
    projs = []
    for slot in range(4):
        mine = slice(slot * block, (slot + 1) * block)
        theirs = slice((slot ^ 1) * block, ((slot ^ 1) + 1) * block)
        kept = acc[mine, own] + got[theirs, :half].astype(F32)
        digits = got[theirs, half : half + 128].astype(F32)
        whole_dot = dot[mine, :] + digits[:, 0:1] + digits[:, 1:2]
        projs.append(((kept - unit[mine, own] * whole_dot) * inv[mine, :]).astype(BF16))
        if slot in (0, 2):
            target = (row_keep, row_send)[slot // 2]
            target[:, own] = kept.astype(target.dtype)
            for side in range(2):
                first = pl.multiple_of((1 - starts[1]) * half + side * quarter, quarter)
                lanes = pl.ds(first, quarter)
                at = (2 * side + slot // 2) * block
                extra = got[at : at + block, half + 128 :].astype(F32)
                target[:, lanes] = (acc[mine, lanes] + extra).astype(target.dtype)
    proj = jnp.concatenate(projs, 0)
    ready()
    sensor = jnp.concatenate([own_rows[...], core_rows[...], yh_rows[...], both_rows[...]], 0)
    chunk = weight.shape[1]
    for n in range(half // 128):
        product = inner_cols(proj[:, n * 128 : (n + 1) * 128], sensor).astype(BF16)
        for m in range(128 // chunk):
            weight[n * (128 // chunk) + m] = product[m * chunk : (m + 1) * chunk]


def chunk_kernel(ready, parts, out):
    total = parts[0].astype(F32)
    for n in range(1, parts.shape[0]):
        total = total + parts[n].astype(F32)
    turned = total.T
    count, rows, lanes = out.shape
    for n in range(count):
        at = 2 * rows * n
        out[n] = jnp.concatenate([turned[at : at + rows], turned[at + rows : at + 2 * rows]], 1).astype(BF16)


def share_kernel(ready, parts, out):
    rows = parts.shape[1]
    for core in range(CORE):
        total = parts[core].astype(F32)
        for n in range(1, Z * YH):
            total = total + parts[n * CORE + core].astype(F32)
        total = total * (1.0 / DP)
        for n in range(DP):
            out[n, core * rows : (core + 1) * rows] = total


def layout_kernel(ready, shares, out):
    rows, lanes = shares.shape[1] // 2, shares.shape[2]
    cols = lanes // 2
    for core in range(CORE):
        here = slice(core * rows, (core + 1) * rows)
        for pair in range(DP // 2):
            left, right = shares[2 * pair, here], shares[2 * pair + 1, here]
            at = core * DP * cols + pair * lanes
            out[:rows, at : at + lanes] = jnp.concatenate([left[:, :cols], right[:, :cols]], 1)
            out[rows:, at : at + lanes] = jnp.concatenate([left[:, cols:], right[:, cols:]], 1)


def on_device(sensor_feats, text_embeds, proj_weight, matches, log_scale, logit_bias):
    sensor = sensor_feats[0]
    texts = text_embeds[0]
    rows = sensor.shape[0]
    feat, width = proj_weight.shape
    loop_index = lax.axis_index("loop")
    z = loop_index // (YH * CORE)
    core = loop_index % CORE
    logit_scale = jnp.exp(log_scale)
    numbers = jnp.stack([logit_scale, logit_bias])

    slot = {0: texts}
    for k in (1, 2, 3):
        slot[k] = shift_z(slot[k - 1], -1)
        slot[-k] = shift_z(slot[1 - k], 1)

    sensor_yh = swap_yh(sensor)
    sensors = [sensor, swap_core(sensor), sensor_yh, swap_core(sensor_yh)]
    match = matches.reshape(1, rows)
    match_yh = swap_yh(match)
    match_both = swap_core(jnp.concatenate([match, match_yh], 0))
    match = [match, match_both[:1], match_yh, match_both[1:]]
    shapes = [((4 * rows, width), F32), ((4 * rows, width), BF16), ((4 * rows, 1), F32), ((4 * rows, 1), F32)]
    image_unit, image_emb, image_inv, match_rows = call(
        project_kernel, [jax.ShapeDtypeStruct(*s) for s in shapes], {}, *sensors, proj_weight, *match, far=range(5), far_out=(0,)
    )

    def starts_of(keys):
        step = (1 - 2 * core) * YH * CORE
        return [(loop_index + k * step + LOOP) % LOOP * rows for k in keys]

    def pairs(keys, dtypes, acc):
        operands = [numbers, jnp.stack(starts_of(keys)), image_emb, match_rows, *(slot[k] for k in keys)]
        out = [jax.ShapeDtypeStruct((4 * rows, width), F32)]
        out += [jax.ShapeDtypeStruct((rows, width), d) for d in dtypes]
        aliases = {}
        if acc is not None:
            aliases = {len(operands): 0}
            operands.append(acc)
        kernel = functools.partial(pairs_kernel, len(keys), acc is None)
        far = range(4, 4 + len(keys))
        return call(kernel, out, aliases, *operands, far=far, far_out=range(1, len(out)))

    acc, text_0, text_1, text_m1, text_2, text_m2 = pairs((0, 1, -1, 2, -2), (F32, BF16, BF16, F32, F32), None)
    last_text, acc = lax.optimization_barrier((slot[-3], acc))
    last_text = shift_z(last_text, 1)
    acc, text_3, text_m3 = pairs((3, -3), (BF16, BF16), acc)
    starts = jnp.stack(starts_of((4,)) + [core])
    shapes = [((4 * rows, width), F32), ((4 * rows, 1), F32), ((4 * rows, width // 8 * 7), BF16), ((4 * rows, rows), BF16)]
    acc, dot, packet, last_grad = call(
        last_kernel,
        [jax.ShapeDtypeStruct(*s) for s in shapes],
        {5: 0},
        numbers, starts, image_emb, match_rows, last_text, acc, image_unit,
        far=(4, 6),
        late=(6,),
    )
    (text_4,) = call(
        last_text_kernel, [jax.ShapeDtypeStruct((rows, width), BF16)], {}, last_grad, image_emb, far_out=(0,)
    )

    shapes = [((DP, width // 16, feat), BF16), ((rows, width), BF16), ((rows, width), F32)]
    weight_part, row_send, row_keep = call(
        weight_kernel,
        [jax.ShapeDtypeStruct(*s) for s in shapes],
        {},
        starts, swap_core(packet), acc, dot, image_unit, image_inv, *sensors,
        far=(4, *range(6, 10)),
        late=range(6, 10),
        far_out=range(3),
    )
    weight_part = lax.all_to_all(weight_part, "dp", 0, 0, tiled=True)
    per_loop = feat // LOOP
    block = (per_loop // 2, width // 8)
    (weight_part,) = call(
        chunk_kernel, [jax.ShapeDtypeStruct((LOOP,) + block, BF16)], {}, weight_part, far_out=(0,)
    )
    text_2, text_m2, row_send, _ = lax.optimization_barrier((text_2, text_m2, row_send, weight_part))
    weight_part = lax.all_to_all(weight_part, "loop", 0, 0, tiled=True)
    (shares,) = call(
        share_kernel, [jax.ShapeDtypeStruct((DP, per_loop, width // 8), F32)], {}, weight_part, far_out=(0,)
    )

    text_3, text_m3, text_4, text_1, text_m1, _ = lax.optimization_barrier(
        (text_3, text_m3, text_4, text_1, text_m1, row_keep)
    )
    row_got = swap_yh(row_send)
    from_below, from_above, far = shift_z(text_3, 1), shift_z(text_m3, -1), shift_z(text_4, 2)
    near_below, near_above = shift_z(text_1, 1), shift_z(text_m1, -1)
    up = text_2 + from_below.astype(F32) + far.astype(F32)
    down = text_m2 + from_above.astype(F32)
    up, down = shift_z(up.astype(BF16), 2), shift_z(down.astype(BF16), -2)
    up, down, row_got, _ = lax.optimization_barrier((up, down, row_got, shares))
    shares = lax.all_to_all(shares, "dp", 0, 0, tiled=True)
    (weight_grad,) = call(
        layout_kernel, [jax.ShapeDtypeStruct((per_loop, width), F32)], {}, shares, far_out=(0,)
    )
    text_sum = text_0 + near_below.astype(F32) + near_above.astype(F32)
    text_sum = logit_scale * (text_sum + up.astype(F32) + down.astype(F32))
    text_wide = texts.astype(F32)
    text_inv = lax.rsqrt(jnp.sum(text_wide * text_wide, -1, keepdims=True) + 1e-06)
    text_unit = text_wide * text_inv
    text_grad = (text_sum - text_unit * jnp.sum(text_unit * text_sum, -1, keepdims=True)) * text_inv

    image_grad = row_keep + row_got.astype(F32)
    own_unit = image_unit[:rows]
    own_dot = jnp.sum(own_unit * image_grad, -1, keepdims=True)
    proj_grad = ((image_grad - own_unit * own_dot) * image_inv[:rows]).astype(BF16)
    sensor_grad = inner_rows(proj_grad, proj_weight).astype(BF16)
    return (sensor_grad[None], text_grad[None], weight_grad)


def solution(mesh):
    placed = (P("dp", "loop", None), P("dp", "loop", None), P(), P("dp", "loop"), P(), P())
    return jax.shard_map(
        on_device,
        mesh=mesh,
        in_specs=placed,
        out_specs=(P("dp", "loop", None), P("dp", "loop", None), P("loop", None)),
        check_vma=False,
    )
```

```python
import functools

import jax
import jax.numpy as jnp
from jax import lax
from jax.experimental import pallas as pl
from jax.experimental.pallas import tpu as pltpu
from jax.sharding import PartitionSpec as P

Z, YH, CORE = 8, 2, 2
LOOP = Z * YH * CORE
DP = 8
BF16 = jnp.bfloat16
F32 = jnp.float32
VMEM = pl.BlockSpec(memory_space=pltpu.VMEM)
HBM = pl.BlockSpec(memory_space=pltpu.HBM)
SMEM = pl.BlockSpec(memory_space=pltpu.SMEM)


def route(move):
    pairs = []
    for z in range(Z):
        for y in range(YH):
            for c in range(CORE):
                to_z, to_y, to_c = move(z, y, c)
                source = (z * YH + y) * CORE + c
                pairs.append((source, ((to_z % Z) * YH + to_y) * CORE + to_c))
    return pairs


def shift_z(block, distance):
    return lax.ppermute(block, "loop", route(lambda z, y, c: (z + (1 - 2 * c) * distance, y, c)))


def swap_core(block):
    return lax.ppermute(block, "loop", route(lambda z, y, c: (z, y, 1 - c)))


def swap_yh(block):
    return lax.ppermute(block, "loop", route(lambda z, y, c: (z, 1 - y, c)))


def inner_rows(left, right):
    return lax.dot_general(left, right, (((1,), (1,)), ((), ())), preferred_element_type=F32)


def inner_cols(left, right):
    return lax.dot_general(left, right, (((0,), (0,)), ((), ())), preferred_element_type=F32)


class Moves:
    def __init__(self, sems, loads, held, outs):
        self.sems, self.loads, self.held, self.outs, self.sent = sems, loads, held, outs, []

    def need(self, n):
        self.loads[n].wait()

    def send(self, n, part=None):
        source, target = self.held[n], self.outs[n]
        if part is not None:
            source, target = source.at[part], target.at[part]
        copy = pltpu.make_async_copy(source, target, self.sems.at[len(self.loads) + len(self.sent)])
        copy.start()
        self.sent.append(copy)


def call(kernel, out, aliases, *operands, far=(), far_out=(), sends=None):
    far, far_out, total = list(far), list(far_out), len(operands)
    sends = len(far_out) if sends is None else sends

    def body(*refs):
        ins, outs, scratch = refs[:total], refs[total : total + len(out)], refs[total + len(out) :]
        held = dict(zip(far, scratch[: len(far)]))
        held_out = dict(zip(far_out, scratch[len(far) : -1]))
        loads = {n: pltpu.make_async_copy(ins[n], held[n], scratch[-1].at[m]) for m, n in enumerate(far)}
        for load in loads.values():
            load.start()
        moves = Moves(scratch[-1], loads, held_out, outs)
        kernel(moves, *(held.get(n, ref) for n, ref in enumerate(ins)), *(held_out.get(n, ref) for n, ref in enumerate(outs)))
        for copy in moves.sent:
            copy.wait()

    in_specs = [SMEM if o.ndim == 1 else HBM if n in far else VMEM for n, o in enumerate(operands)]
    scratch = [pltpu.VMEM(operands[n].shape, operands[n].dtype) for n in far]
    scratch += [pltpu.VMEM(out[n].shape, out[n].dtype) for n in far_out]
    scratch.append(pltpu.SemaphoreType.DMA((max(1, len(far) + sends),)))
    operands = [pltpu.with_memory_space_constraint(o, pltpu.HBM) if n in far else o for n, o in enumerate(operands)]
    return pl.pallas_call(
        body,
        out_shape=[pltpu.HBM(o.shape, o.dtype) if n in far_out else o for n, o in enumerate(out)],
        in_specs=in_specs,
        out_specs=[HBM if n in far_out else VMEM for n in range(len(out))],
        scratch_shapes=scratch,
        input_output_aliases=aliases,
        cost_estimate=pl.CostEstimate(flops=1, bytes_accessed=1, transcendentals=0),
        compiler_params=pltpu.CompilerParams(vmem_limit_bytes=20 << 20),
    )(*operands)


def block_grads(numbers, start, image_emb, match, text):
    wide = text.astype(F32)
    inv = lax.rsqrt(jnp.sum(wide * wide, -1, keepdims=True) + 1e-06)
    emb = (wide * inv).astype(BF16)
    logits = numbers[0] * inner_rows(image_emb, emb) + numbers[1]
    column = lax.broadcasted_iota(jnp.int32, logits.shape, 1) + start
    positive = (match == column.astype(F32)).astype(F32)
    return emb, (jax.nn.sigmoid(logits) - positive).astype(BF16)


def pairs_kernel(count, first, moves, numbers, starts, image_emb, match, *refs):
    texts, refs = refs[:count], refs[count:]
    if not first:
        acc_in, refs = refs[0], refs[1:]
    acc_out, text_out = refs[0], refs[1:]
    image = image_emb[...]
    embs, grads = [], []
    for n in range(count):
        moves.need(4 + n)
        emb, grad = block_grads(numbers, starts[n], image, match[...], texts[n][...])
        embs.append(emb)
        grads.append(grad)
        text_out[n][...] = inner_cols(grad, image).astype(text_out[n].dtype)
        moves.send(1 + n)
    part = jnp.dot(jnp.concatenate(grads, 1), jnp.concatenate(embs, 0), preferred_element_type=F32)
    acc_out[...] = part if first else acc_in[...] + part


def project_kernel(moves, own, core, yh, both, proj_weight, *refs):
    matches, (emb, inv_out, match_out) = refs[:4], refs[4:]
    rows = own.shape[0]
    moves.need(4)
    for n, sensor in enumerate((own, core, yh, both)):
        here = slice(n * rows, (n + 1) * rows)
        moves.need(n)
        projected = jnp.dot(sensor[...], proj_weight[...], preferred_element_type=F32)
        inv = lax.rsqrt(jnp.sum(projected * projected, -1, keepdims=True) + 1e-06)
        emb[here, :] = (projected * inv).astype(BF16)
        inv_out[here, :] = inv
        match = jnp.broadcast_to(matches[n][...].astype(F32), (rows, rows))
        match_out[here, :] = match.T[:, 0:1]


def last_kernel(moves, numbers, starts, image_emb, match, text, acc_in, acc_out, dot_out, packet, grad_out):
    emb, grad = block_grads(numbers, starts[0], image_emb[...], match[...], text[...])
    grad_out[...] = grad
    acc = numbers[0] * (acc_in[...] + jnp.dot(grad, emb, preferred_element_type=F32))
    acc_out[...] = acc
    dot = jnp.sum(image_emb[...].astype(F32) * acc, -1, keepdims=True)
    dot_out[...] = dot
    rows, width = acc.shape
    half, quarter, block = width // 2, width // 4, rows // 4
    own = pl.multiple_of(starts[1] * half, half)
    other = pl.multiple_of((1 - starts[1]) * half, half)
    packet[:, :half] = acc_out[:, pl.ds(other, half)].astype(BF16)
    top = dot.astype(BF16).astype(F32)
    lane = lax.broadcasted_iota(jnp.int32, (rows, 128), 1)
    digits = jnp.where(lane == 0, top, jnp.where(lane == 1, dot - top, 0.0))
    packet[:, half : half + 128] = digits.astype(BF16)
    for side in range(2):
        lanes = pl.ds(pl.multiple_of(own + side * quarter, quarter), quarter)
        for n, slot in enumerate((1, 3)):
            at = (2 * side + n) * block
            packet[at : at + block, half + 128 :] = acc_out[slot * block : (slot + 1) * block, lanes].astype(BF16)


def last_text_kernel(moves, grad, image_emb, out):
    out[...] = inner_cols(grad[...], image_emb[...]).astype(out.dtype)
    moves.send(0)


def weight_kernel(moves, starts, got, acc, dot, image_emb, inv, own_rows, core_rows, yh_rows, both_rows, weight, row_send, row_keep):
    rows, width = acc.shape
    half, quarter, block = width // 2, width // 4, rows // 4
    own = pl.ds(pl.multiple_of(starts[1] * half, half), half)
    projs = []
    for slot in range(4):
        mine = slice(slot * block, (slot + 1) * block)
        theirs = slice((slot ^ 1) * block, ((slot ^ 1) + 1) * block)
        kept = acc[mine, own] + got[theirs, :half].astype(F32)
        digits = got[theirs, half : half + 128].astype(F32)
        whole_dot = dot[mine, :] + digits[:, 0:1] + digits[:, 1:2]
        unit = image_emb[mine, own].astype(F32)
        projs.append(((kept - unit * whole_dot) * inv[mine, :]).astype(BF16))
        if slot in (0, 2):
            target = (row_keep, row_send)[slot // 2]
            target[:, own] = kept.astype(target.dtype)
            for side in range(2):
                first = pl.multiple_of((1 - starts[1]) * half + side * quarter, quarter)
                lanes = pl.ds(first, quarter)
                at = (2 * side + slot // 2) * block
                extra = got[at : at + block, half + 128 :].astype(F32)
                target[:, lanes] = (acc[mine, lanes] + extra).astype(target.dtype)
            moves.send(2 - slot // 2)
    proj = jnp.concatenate(projs, 0)
    for n in range(6, 10):
        moves.need(n)
    sensor = jnp.concatenate([own_rows[...], core_rows[...], yh_rows[...], both_rows[...]], 0)
    chunk = weight.shape[1]
    for n in range(half // 128):
        product = inner_cols(proj[:, n * 128 : (n + 1) * 128], sensor).astype(BF16)
        for m in range(128 // chunk):
            at = n * (128 // chunk) + m
            weight[at] = product[m * chunk : (m + 1) * chunk]
            moves.send(0, at)


def chunk_kernel(moves, parts, out):
    total = parts[0].astype(F32)
    for n in range(1, parts.shape[0]):
        total = total + parts[n].astype(F32)
    turned = total.T
    count, rows, lanes = out.shape
    for n in range(count):
        at = 2 * rows * n
        out[n] = jnp.concatenate([turned[at : at + rows], turned[at + rows : at + 2 * rows]], 1).astype(BF16)
    moves.send(0)


def share_kernel(moves, parts, out):
    rows = parts.shape[1]
    for core in range(CORE):
        total = parts[core].astype(F32)
        for n in range(1, Z * YH):
            total = total + parts[n * CORE + core].astype(F32)
        total = total * (1.0 / DP)
        for n in range(DP):
            out[n, core * rows : (core + 1) * rows] = total
    moves.send(0)


def layout_kernel(moves, shares, out):
    rows, lanes = shares.shape[1] // 2, shares.shape[2]
    cols = lanes // 2
    for core in range(CORE):
        here = slice(core * rows, (core + 1) * rows)
        for pair in range(DP // 2):
            left, right = shares[2 * pair, here], shares[2 * pair + 1, here]
            at = core * DP * cols + pair * lanes
            out[:rows, at : at + lanes] = jnp.concatenate([left[:, :cols], right[:, :cols]], 1)
            out[rows:, at : at + lanes] = jnp.concatenate([left[:, cols:], right[:, cols:]], 1)
    moves.send(0)


def on_device(sensor_feats, text_embeds, proj_weight, matches, log_scale, logit_bias):
    sensor = sensor_feats[0]
    texts = text_embeds[0]
    rows = sensor.shape[0]
    feat, width = proj_weight.shape
    loop_index = lax.axis_index("loop")
    z = loop_index // (YH * CORE)
    core = loop_index % CORE
    logit_scale = jnp.exp(log_scale)
    numbers = jnp.stack([logit_scale, logit_bias])

    slot = {0: texts}
    for k in (1, 2):
        slot[k] = shift_z(slot[k - 1], -1)
        slot[-k] = shift_z(slot[1 - k], 1)

    sensor_yh = swap_yh(sensor)
    match = matches.reshape(1, rows)
    sensor_later, match_later, _ = lax.optimization_barrier((sensor, match, sensor_yh))
    sensors = [sensor, swap_core(sensor_later), sensor_yh, swap_core(sensor_yh)]
    match_yh = swap_yh(match_later)
    match_both = swap_core(jnp.concatenate([match, match_yh], 0))
    match = [match, match_both[:1], match_yh, match_both[1:]]
    shapes = [((4 * rows, width), BF16), ((4 * rows, 1), F32), ((4 * rows, 1), F32)]
    image_emb, image_inv, match_rows = call(
        project_kernel, [jax.ShapeDtypeStruct(*s) for s in shapes], {}, *sensors, proj_weight, *match, far=range(5)
    )
    up, down, _ = lax.optimization_barrier((slot[2], slot[-2], image_emb))
    slot[3], slot[-3] = shift_z(up, -1), shift_z(down, 1)

    def starts_of(keys):
        step = (1 - 2 * core) * YH * CORE
        return [(loop_index + k * step + LOOP) % LOOP * rows for k in keys]

    def pairs(keys, dtypes, acc):
        operands = [numbers, jnp.stack(starts_of(keys)), image_emb, match_rows, *(slot[k] for k in keys)]
        out = [jax.ShapeDtypeStruct((4 * rows, width), F32)]
        out += [jax.ShapeDtypeStruct((rows, width), d) for d in dtypes]
        aliases = {}
        if acc is not None:
            aliases = {len(operands): 0}
            operands.append(acc)
        kernel = functools.partial(pairs_kernel, len(keys), acc is None)
        far = range(4, 4 + len(keys))
        return call(kernel, out, aliases, *operands, far=far, far_out=range(1, len(out)))

    acc, text_0, text_1, text_m1, text_2, text_m2 = pairs((0, 1, -1, 2, -2), (F32, BF16, BF16, BF16, BF16), None)
    last_text, _ = lax.optimization_barrier((slot[-3], acc))
    last_text = shift_z(last_text, 1)
    acc, text_3, text_m3 = pairs((3, -3), (BF16, BF16), acc)
    starts = jnp.stack(starts_of((4,)) + [core])
    shapes = [((4 * rows, width), F32), ((4 * rows, 1), F32), ((4 * rows, width // 8 * 7), BF16), ((4 * rows, rows), BF16)]
    acc, dot, packet, last_grad = call(
        last_kernel,
        [jax.ShapeDtypeStruct(*s) for s in shapes],
        {5: 0},
        numbers, starts, image_emb, match_rows, last_text, acc,
    )
    (text_4,) = call(
        last_text_kernel, [jax.ShapeDtypeStruct((rows, width), BF16)], {}, last_grad, image_emb, far_out=(0,)
    )

    shapes = [((DP, width // 16, feat), BF16), ((rows, width), BF16), ((rows, width), F32)]
    weight_part, row_send, row_keep = call(
        weight_kernel,
        [jax.ShapeDtypeStruct(*s) for s in shapes],
        {},
        starts, swap_core(packet), acc, dot, image_emb, image_inv, *sensors,
        far=range(6, 10),
        far_out=range(3),
        sends=2 + DP,
    )
    weight_part = lax.all_to_all(weight_part, "dp", 0, 0, tiled=True)
    per_loop = feat // LOOP
    block = (per_loop // 2, width // 8)
    (weight_chunks,) = call(
        chunk_kernel, [jax.ShapeDtypeStruct((LOOP,) + block, BF16)], {}, weight_part, far_out=(0,)
    )
    weight_part = lax.all_to_all(weight_chunks, "loop", 0, 0, tiled=True)
    (shares,) = call(
        share_kernel, [jax.ShapeDtypeStruct((DP, per_loop, width // 8), F32)], {}, weight_part, far_out=(0,)
    )

    text_3, text_m3, text_4, text_1, text_m1, _ = lax.optimization_barrier(
        (text_3, text_m3, text_4, text_1, text_m1, row_keep)
    )
    row_got = swap_yh(row_send)
    from_below, from_above, far = shift_z(text_3, 1), shift_z(text_m3, -1), shift_z(text_4, 2)
    near_below, near_above = shift_z(text_1, 1), shift_z(text_m1, -1)
    from_below, from_above, far, near_below, near_above, row_got, _ = lax.optimization_barrier(
        (from_below, from_above, far, near_below, near_above, row_got, weight_chunks)
    )
    up = text_2.astype(F32) + from_below.astype(F32) + far.astype(F32)
    down = text_m2.astype(F32) + from_above.astype(F32)
    up, down = shift_z(up.astype(BF16), 2), shift_z(down.astype(BF16), -2)
    up, down, row_got, _ = lax.optimization_barrier((up, down, row_got, shares))
    shares = lax.all_to_all(shares, "dp", 0, 0, tiled=True)
    (weight_grad,) = call(
        layout_kernel, [jax.ShapeDtypeStruct((per_loop, width), F32)], {}, shares, far_out=(0,)
    )
    text_sum = text_0 + near_below.astype(F32) + near_above.astype(F32)
    text_sum = logit_scale * (text_sum + up.astype(F32) + down.astype(F32))
    text_wide = texts.astype(F32)
    text_inv = lax.rsqrt(jnp.sum(text_wide * text_wide, -1, keepdims=True) + 1e-06)
    text_unit = text_wide * text_inv
    text_grad = (text_sum - text_unit * jnp.sum(text_unit * text_sum, -1, keepdims=True)) * text_inv

    image_grad = row_keep + row_got.astype(F32)
    own_unit = image_emb[:rows].astype(F32)
    own_dot = jnp.sum(own_unit * image_grad, -1, keepdims=True)
    proj_grad = ((image_grad - own_unit * own_dot) * image_inv[:rows]).astype(BF16)
    sensor_grad = inner_rows(proj_grad, proj_weight).astype(BF16)
    return (sensor_grad[None], text_grad[None], weight_grad)


def solution(mesh):
    placed = (P("dp", "loop", None), P("dp", "loop", None), P(), P("dp", "loop"), P(), P())
    return jax.shard_map(
        on_device,
        mesh=mesh,
        in_specs=placed,
        out_specs=(P("dp", "loop", None), P("dp", "loop", None), P("loop", None)),
        check_vma=False,
    )
```

```python
import functools

import jax
import jax.numpy as jnp
from jax import lax
from jax.experimental import pallas as pl
from jax.experimental.pallas import tpu as pltpu
from jax.sharding import PartitionSpec as P

Z, YH, CORE = 8, 2, 2
LOOP = Z * YH * CORE
DP = 8
CUT = 640
BF16 = jnp.bfloat16
F32 = jnp.float32
VMEM = pl.BlockSpec(memory_space=pltpu.VMEM)
HBM = pl.BlockSpec(memory_space=pltpu.HBM)
SMEM = pl.BlockSpec(memory_space=pltpu.SMEM)


def route(move):
    pairs = []
    for z in range(Z):
        for y in range(YH):
            for c in range(CORE):
                to_z, to_y, to_c = move(z, y, c)
                source = (z * YH + y) * CORE + c
                pairs.append((source, ((to_z % Z) * YH + to_y) * CORE + to_c))
    return pairs


def shift_z(block, distance):
    return lax.ppermute(block, "loop", route(lambda z, y, c: (z + (1 - 2 * c) * distance, y, c)))


def swap_core(block):
    return lax.ppermute(block, "loop", route(lambda z, y, c: (z, y, 1 - c)))


def swap_yh(block):
    return lax.ppermute(block, "loop", route(lambda z, y, c: (z, 1 - y, c)))


def inner_rows(left, right):
    return lax.dot_general(left, right, (((1,), (1,)), ((), ())), preferred_element_type=F32)


def inner_cols(left, right):
    return lax.dot_general(left, right, (((0,), (0,)), ((), ())), preferred_element_type=F32)


class Moves:
    def __init__(self, base, sems, loads, held, outs, pack):
        self.base = base
        self.sems, self.loads, self.held, self.outs, self.pack, self.sent = sems, loads, held, outs, pack, []

    def need(self, n):
        self.loads[n].wait()

    def send(self, n, part=None):
        source, target = self.held[n], self.outs[n]
        if part is not None:
            source, target = source.at[part], target.at[part]
        copy = pltpu.make_async_copy(source, target, self.sems.at[self.base + len(self.sent)])
        copy.start()
        self.sent.append(copy)


def call(kernel, out, aliases, *operands, far=(), packed=(), far_out=(), sends=None, cuts=()):
    cuts = dict(cuts)
    far, packed, far_out, total = list(far), list(packed), list(far_out), len(operands)
    sends = len(far_out) if sends is None else sends

    def body(*refs):
        ins, outs, scratch = refs[:total], refs[total : total + len(out)], refs[total + len(out) :]
        held = dict(zip(far, scratch[: len(far)]))
        held_out = dict(zip(far_out, scratch[len(far) : len(far) + len(far_out)]))
        for m, n in enumerate(packed):
            height = operands[n].shape[0]
            held[n] = scratch[-2].at[pl.ds(m * height, height)]
        whole = [(m, n) for m, n in enumerate(in_hbm) if n not in cuts]
        loads = {n: pltpu.make_async_copy(ins[n], held[n], scratch[-1].at[m]) for m, n in whole}
        for n, cut in cuts.items():
            for m, part in enumerate((pl.ds(0, cut), pl.ds(cut, operands[n].shape[0] - cut))):
                sem = scratch[-1].at[len(in_hbm) + sends] if m else scratch[-1].at[far.index(n)]
                loads[n, m] = pltpu.make_async_copy(ins[n].at[part], held[n].at[part], sem)
        for load in loads.values():
            load.start()
        moves = Moves(len(in_hbm), scratch[-1], loads, held_out, outs, scratch[-2] if packed else None)
        kernel(moves, *(held.get(n, ref) for n, ref in enumerate(ins)), *(held_out.get(n, ref) for n, ref in enumerate(outs)))
        for copy in moves.sent:
            copy.wait()

    in_hbm = far + packed
    in_specs = [SMEM if o.ndim == 1 else HBM if n in in_hbm else VMEM for n, o in enumerate(operands)]
    scratch = [pltpu.VMEM(operands[n].shape, operands[n].dtype) for n in far]
    scratch += [pltpu.VMEM(out[n].shape, out[n].dtype) for n in far_out]
    if packed:
        height, width = operands[packed[0]].shape
        scratch.append(pltpu.VMEM((len(packed) * height, width), operands[packed[0]].dtype))
    scratch.append(pltpu.SemaphoreType.DMA((len(in_hbm) + sends + 1,)))
    operands = [pltpu.with_memory_space_constraint(o, pltpu.HBM) if n in in_hbm else o for n, o in enumerate(operands)]
    return pl.pallas_call(
        body,
        out_shape=[pltpu.HBM(o.shape, o.dtype) if n in far_out else o for n, o in enumerate(out)],
        in_specs=in_specs,
        out_specs=[HBM if n in far_out else VMEM for n in range(len(out))],
        scratch_shapes=scratch,
        input_output_aliases=aliases,
        cost_estimate=pl.CostEstimate(flops=1, bytes_accessed=1, transcendentals=0),
        compiler_params=pltpu.CompilerParams(vmem_limit_bytes=20 << 20),
    )(*operands)


def block_grads(numbers, columns, image_emb, match, text):
    wide = text.astype(F32)
    inv = lax.rsqrt(jnp.sum(wide * wide, -1, keepdims=True) + 1e-06)
    emb = (wide * inv).astype(BF16)
    logits = numbers[0] * inner_rows(image_emb, emb) + numbers[1]
    positive = (match == columns).astype(F32)
    return emb, (jax.nn.sigmoid(logits) - positive).astype(BF16)


def columns_of(start, rows):
    return (lax.broadcasted_iota(jnp.int32, (1, rows), 1) + start).astype(F32)


def pairs_kernel(count, first, moves, numbers, starts, image_emb, match, *refs):
    texts, refs = refs[:count], refs[count:]
    if not first:
        acc_in, refs = refs[0], refs[1:]
    acc_out, text_out = refs[0], refs[1:]
    image = image_emb[...]
    rows = texts[0].shape[0]
    columns = jnp.concatenate([columns_of(starts[n], rows) for n in range(count)], 1)
    for n in range(count):
        moves.need(4 + n)
    emb, grad = block_grads(numbers, columns, image, match[...], moves.pack[...])
    text_part = inner_cols(grad, image)
    for n in range(count):
        text_out[n][...] = text_part[n * rows : (n + 1) * rows].astype(text_out[n].dtype)
        moves.send(1 + n)
    part = jnp.dot(grad, emb, preferred_element_type=F32)
    acc_out[...] = part if first else acc_in[...] + part


def project_kernel(moves, proj_weight, own, core, yh, both, *refs):
    matches, (emb, inv_out, match_out) = refs[:4], refs[4:]
    rows, cut = own.shape[0], CUT
    for n in range(4):
        moves.need(1 + n)
    sensor = moves.pack[...]
    moves.need((0, 0))
    projected = jnp.dot(sensor[:, :cut], proj_weight[:cut], preferred_element_type=F32)
    moves.need((0, 1))
    projected = projected + jnp.dot(sensor[:, cut:], proj_weight[cut:], preferred_element_type=F32)
    inv = lax.rsqrt(jnp.sum(projected * projected, -1, keepdims=True) + 1e-06)
    emb[...] = (projected * inv).astype(BF16)
    inv_out[...] = inv
    for n in range(4):
        match = jnp.broadcast_to(matches[n][...].astype(F32), (rows, rows))
        match_out[n * rows : (n + 1) * rows, :] = match.T[:, 0:1]


def last_kernel(moves, numbers, starts, image_emb, match, text, acc_in, acc_out, dot_out, packet, grad_out):
    columns = columns_of(starts[0], text.shape[0])
    emb, grad = block_grads(numbers, columns, image_emb[...], match[...], text[...])
    grad_out[...] = grad
    acc = numbers[0] * (acc_in[...] + jnp.dot(grad, emb, preferred_element_type=F32))
    acc_out[...] = acc
    dot = jnp.sum(image_emb[...].astype(F32) * acc, -1, keepdims=True)
    dot_out[...] = dot
    rows, width = acc.shape
    half, quarter, block = width // 2, width // 4, rows // 4
    own = pl.multiple_of(starts[1] * half, half)
    other = pl.multiple_of((1 - starts[1]) * half, half)
    packet[:, :half] = acc_out[:, pl.ds(other, half)].astype(BF16)
    top = dot.astype(BF16).astype(F32)
    lane = lax.broadcasted_iota(jnp.int32, (rows, 128), 1)
    digits = jnp.where(lane == 0, top, jnp.where(lane == 1, dot - top, 0.0))
    packet[:, half : half + 128] = digits.astype(BF16)
    for side in range(2):
        lanes = pl.ds(pl.multiple_of(own + side * quarter, quarter), quarter)
        for n, slot in enumerate((1, 3)):
            at = (2 * side + n) * block
            packet[at : at + block, half + 128 :] = acc_out[slot * block : (slot + 1) * block, lanes].astype(BF16)


def last_text_kernel(moves, grad, image_emb, out):
    out[...] = inner_cols(grad[...], image_emb[...]).astype(out.dtype)
    moves.send(0)


def weight_kernel(moves, starts, got, acc, dot, image_emb, inv, own_rows, core_rows, yh_rows, both_rows, weight, row_send, row_keep):
    rows, width = acc.shape
    half, quarter, block = width // 2, width // 4, rows // 4
    own = pl.ds(pl.multiple_of(starts[1] * half, half), half)
    projs = []
    for slot in range(4):
        mine = slice(slot * block, (slot + 1) * block)
        theirs = slice((slot ^ 1) * block, ((slot ^ 1) + 1) * block)
        kept = acc[mine, own] + got[theirs, :half].astype(F32)
        digits = got[theirs, half : half + 128].astype(F32)
        whole_dot = dot[mine, :] + digits[:, 0:1] + digits[:, 1:2]
        unit = image_emb[mine, own].astype(F32)
        projs.append(((kept - unit * whole_dot) * inv[mine, :]).astype(BF16))
        if slot in (0, 2):
            target = (row_keep, row_send)[slot // 2]
            target[:, own] = kept.astype(target.dtype)
            for side in range(2):
                first = pl.multiple_of((1 - starts[1]) * half + side * quarter, quarter)
                lanes = pl.ds(first, quarter)
                at = (2 * side + slot // 2) * block
                extra = got[at : at + block, half + 128 :].astype(F32)
                target[:, lanes] = (acc[mine, lanes] + extra).astype(target.dtype)
            moves.send(2 - slot // 2)
    proj = jnp.concatenate(projs, 0)
    for n in range(6, 10):
        moves.need(n)
    sensor = moves.pack[...]
    chunk = weight.shape[1]
    for side in range(2):
        product = inner_cols(proj[:, side * quarter : (side + 1) * quarter], sensor).astype(BF16)
        for m in range(quarter // chunk):
            at = side * (quarter // chunk) + m
            weight[at] = product[m * chunk : (m + 1) * chunk]
            moves.send(0, at)


def chunk_kernel(moves, parts, out):
    total = parts[0].astype(F32)
    for n in range(1, parts.shape[0]):
        total = total + parts[n].astype(F32)
    turned = total.T
    count, rows, lanes = out.shape
    for n in range(count):
        at = 2 * rows * n
        out[n] = jnp.concatenate([turned[at : at + rows], turned[at + rows : at + 2 * rows]], 1).astype(BF16)
    moves.send(0)


def share_kernel(moves, parts, out):
    rows = parts.shape[1]
    for core in range(CORE):
        total = parts[core].astype(F32)
        for n in range(1, Z * YH):
            total = total + parts[n * CORE + core].astype(F32)
        total = total * (1.0 / DP)
        for n in range(DP):
            out[n, core * rows : (core + 1) * rows] = total
    moves.send(0)


def layout_kernel(moves, shares, out):
    rows, lanes = shares.shape[1] // 2, shares.shape[2]
    cols = lanes // 2
    for core in range(CORE):
        here = slice(core * rows, (core + 1) * rows)
        for pair in range(DP // 2):
            left, right = shares[2 * pair, here], shares[2 * pair + 1, here]
            at = core * DP * cols + pair * lanes
            out[:rows, at : at + lanes] = jnp.concatenate([left[:, :cols], right[:, :cols]], 1)
            out[rows:, at : at + lanes] = jnp.concatenate([left[:, cols:], right[:, cols:]], 1)
    moves.send(0)


def on_device(sensor_feats, text_embeds, proj_weight, matches, log_scale, logit_bias):
    sensor = sensor_feats[0]
    texts = text_embeds[0]
    rows = sensor.shape[0]
    feat, width = proj_weight.shape
    loop_index = lax.axis_index("loop")
    z = loop_index // (YH * CORE)
    core = loop_index % CORE
    logit_scale = jnp.exp(log_scale)
    numbers = jnp.stack([logit_scale, logit_bias])

    slot = {0: texts}
    slot[1], slot[-1] = shift_z(texts, -1), shift_z(texts, 1)

    sensor_yh = swap_yh(sensor)
    match = matches.reshape(1, rows)
    match_yh = swap_yh(match)
    up, down, _, _ = lax.optimization_barrier((slot[1], slot[-1], sensor_yh, match_yh))
    slot[2], slot[-2] = shift_z(up, -1), shift_z(down, 1)
    sensor_later, _ = lax.optimization_barrier((sensor, sensor_yh))
    sensors = [sensor, swap_core(sensor_later), sensor_yh, swap_core(sensor_yh)]
    match_both = swap_core(jnp.concatenate([match, match_yh], 0))
    match = [match, match_both[:1], match_yh, match_both[1:]]
    shapes = [((4 * rows, width), BF16), ((4 * rows, 1), F32), ((4 * rows, 1), F32)]
    image_emb, image_inv, match_rows = call(
        project_kernel,
        [jax.ShapeDtypeStruct(*s) for s in shapes],
        {},
        proj_weight, *sensors, *match,
        far=(0,),
        packed=range(1, 5),
        cuts={0: CUT},
    )
    up, down, _ = lax.optimization_barrier((slot[2], slot[-2], image_emb))
    slot[3], slot[-3] = shift_z(up, -1), shift_z(down, 1)

    def starts_of(keys):
        step = (1 - 2 * core) * YH * CORE
        return [(loop_index + k * step + LOOP) % LOOP * rows for k in keys]

    def pairs(keys, dtypes, acc):
        operands = [numbers, jnp.stack(starts_of(keys)), image_emb, match_rows, *(slot[k] for k in keys)]
        out = [jax.ShapeDtypeStruct((4 * rows, width), F32)]
        out += [jax.ShapeDtypeStruct((rows, width), d) for d in dtypes]
        aliases = {}
        if acc is not None:
            aliases = {len(operands): 0}
            operands.append(acc)
        kernel = functools.partial(pairs_kernel, len(keys), acc is None)
        return call(kernel, out, aliases, *operands, packed=range(4, 4 + len(keys)), far_out=range(1, len(out)))

    acc, text_0, text_1, text_m1, text_2, text_m2 = pairs((0, 1, -1, 2, -2), (F32, BF16, BF16, BF16, BF16), None)
    last_text, _ = lax.optimization_barrier((slot[-3], acc))
    last_text = shift_z(last_text, 1)
    acc, text_3, text_m3 = pairs((3, -3), (BF16, BF16), acc)
    starts = jnp.stack(starts_of((4,)) + [core])
    shapes = [((4 * rows, width), F32), ((4 * rows, 1), F32), ((4 * rows, width // 8 * 7), BF16), ((4 * rows, rows), BF16)]
    acc, dot, packet, last_grad = call(
        last_kernel,
        [jax.ShapeDtypeStruct(*s) for s in shapes],
        {5: 0},
        numbers, starts, image_emb, match_rows, last_text, acc,
    )
    (text_4,) = call(
        last_text_kernel, [jax.ShapeDtypeStruct((rows, width), BF16)], {}, last_grad, image_emb, far_out=(0,)
    )

    shapes = [((DP, width // 16, feat), BF16), ((rows, width), BF16), ((rows, width), F32)]
    weight_part, row_send, row_keep = call(
        weight_kernel,
        [jax.ShapeDtypeStruct(*s) for s in shapes],
        {},
        starts, swap_core(packet), acc, dot, image_emb, image_inv, *sensors,
        packed=range(6, 10),
        far_out=range(3),
        sends=2 + DP,
    )
    weight_part = lax.all_to_all(weight_part, "dp", 0, 0, tiled=True)
    per_loop = feat // LOOP
    block = (per_loop // 2, width // 8)
    (weight_chunks,) = call(
        chunk_kernel, [jax.ShapeDtypeStruct((LOOP,) + block, BF16)], {}, weight_part, far_out=(0,)
    )
    weight_part = lax.all_to_all(weight_chunks, "loop", 0, 0, tiled=True)
    (shares,) = call(
        share_kernel, [jax.ShapeDtypeStruct((DP, per_loop, width // 8), F32)], {}, weight_part, far_out=(0,)
    )

    text_3, text_m3, text_4, text_1, text_m1, _ = lax.optimization_barrier(
        (text_3, text_m3, text_4, text_1, text_m1, row_keep)
    )
    row_got = swap_yh(row_send)
    from_below, from_above, far = shift_z(text_3, 1), shift_z(text_m3, -1), shift_z(text_4, 2)
    near_below, near_above = shift_z(text_1, 1), shift_z(text_m1, -1)
    from_below, from_above, far, near_below, near_above, row_got, _ = lax.optimization_barrier(
        (from_below, from_above, far, near_below, near_above, row_got, weight_chunks)
    )
    up = text_2.astype(F32) + from_below.astype(F32) + far.astype(F32)
    down = text_m2.astype(F32) + from_above.astype(F32)
    up, down = shift_z(up.astype(BF16), 2), shift_z(down.astype(BF16), -2)
    up, down, row_got, _ = lax.optimization_barrier((up, down, row_got, shares))
    shares = lax.all_to_all(shares, "dp", 0, 0, tiled=True)
    (weight_grad,) = call(
        layout_kernel, [jax.ShapeDtypeStruct((per_loop, width), F32)], {}, shares, far_out=(0,)
    )
    text_sum = text_0 + near_below.astype(F32) + near_above.astype(F32)
    text_sum = logit_scale * (text_sum + up.astype(F32) + down.astype(F32))
    text_wide = texts.astype(F32)
    text_inv = lax.rsqrt(jnp.sum(text_wide * text_wide, -1, keepdims=True) + 1e-06)
    text_unit = text_wide * text_inv
    text_grad = (text_sum - text_unit * jnp.sum(text_unit * text_sum, -1, keepdims=True)) * text_inv

    image_grad = row_keep + row_got.astype(F32)
    own_unit = image_emb[:rows].astype(F32)
    own_dot = jnp.sum(own_unit * image_grad, -1, keepdims=True)
    proj_grad = ((image_grad - own_unit * own_dot) * image_inv[:rows]).astype(BF16)
    sensor_grad = inner_rows(proj_grad, proj_weight).astype(BF16)
    return (sensor_grad[None], text_grad[None], weight_grad)


def solution(mesh):
    placed = (P("dp", "loop", None), P("dp", "loop", None), P(), P("dp", "loop"), P(), P())
    return jax.shard_map(
        on_device,
        mesh=mesh,
        in_specs=placed,
        out_specs=(P("dp", "loop", None), P("dp", "loop", None), P("loop", None)),
        check_vma=False,
    )
```

```python
import functools

import jax
import jax.numpy as jnp
from jax import lax
from jax.experimental import pallas as pl
from jax.experimental.pallas import tpu as pltpu
from jax.sharding import PartitionSpec as P

Z, YH, CORE = 8, 2, 2
LOOP = Z * YH * CORE
DP = 8
CUT = 640
BF16 = jnp.bfloat16
F32 = jnp.float32
VMEM = pl.BlockSpec(memory_space=pltpu.VMEM)
HBM = pl.BlockSpec(memory_space=pltpu.HBM)
SMEM = pl.BlockSpec(memory_space=pltpu.SMEM)


def route(move):
    pairs = []
    for z in range(Z):
        for y in range(YH):
            for c in range(CORE):
                to_z, to_y, to_c = move(z, y, c)
                source = (z * YH + y) * CORE + c
                pairs.append((source, ((to_z % Z) * YH + to_y) * CORE + to_c))
    return pairs


def shift_z(block, distance):
    return lax.ppermute(block, "loop", route(lambda z, y, c: (z + (1 - 2 * c) * distance, y, c)))


def swap_core(block):
    return lax.ppermute(block, "loop", route(lambda z, y, c: (z, y, 1 - c)))


def swap_yh(block):
    return lax.ppermute(block, "loop", route(lambda z, y, c: (z, 1 - y, c)))


def inner_rows(left, right):
    return lax.dot_general(left, right, (((1,), (1,)), ((), ())), preferred_element_type=F32)


def inner_cols(left, right):
    return lax.dot_general(left, right, (((0,), (0,)), ((), ())), preferred_element_type=F32)


class Moves:
    def __init__(self, base, sems, loads, held, outs, pack):
        self.base = base
        self.sems, self.loads, self.held, self.outs, self.pack, self.sent = sems, loads, held, outs, pack, []

    def need(self, n):
        self.loads[n].wait()

    def send(self, n, part=None):
        source, target = self.held[n], self.outs[n]
        if part is not None:
            source, target = source.at[part], target.at[part]
        copy = pltpu.make_async_copy(source, target, self.sems.at[self.base + len(self.sent)])
        copy.start()
        self.sent.append(copy)


def call(kernel, out, aliases, *operands, far=(), packed=(), far_out=(), sends=None, cuts=()):
    cuts = dict(cuts)
    far, packed, far_out, total = list(far), list(packed), list(far_out), len(operands)
    sends = len(far_out) if sends is None else sends

    def body(*refs):
        ins, outs, scratch = refs[:total], refs[total : total + len(out)], refs[total + len(out) :]
        held = dict(zip(far, scratch[: len(far)]))
        held_out = dict(zip(far_out, scratch[len(far) : len(far) + len(far_out)]))
        for m, n in enumerate(packed):
            height = operands[n].shape[0]
            held[n] = scratch[-2].at[pl.ds(m * height, height)]
        whole = [(m, n) for m, n in enumerate(in_hbm) if n not in cuts]
        loads = {n: pltpu.make_async_copy(ins[n], held[n], scratch[-1].at[m]) for m, n in whole}
        for n, cut in cuts.items():
            for m, part in enumerate((pl.ds(0, cut), pl.ds(cut, operands[n].shape[0] - cut))):
                sem = scratch[-1].at[len(in_hbm) + sends] if m else scratch[-1].at[far.index(n)]
                loads[n, m] = pltpu.make_async_copy(ins[n].at[part], held[n].at[part], sem)
        for load in loads.values():
            load.start()
        moves = Moves(len(in_hbm), scratch[-1], loads, held_out, outs, scratch[-2] if packed else None)
        kernel(moves, *(held.get(n, ref) for n, ref in enumerate(ins)), *(held_out.get(n, ref) for n, ref in enumerate(outs)))
        for copy in moves.sent:
            copy.wait()

    in_hbm = far + packed
    in_specs = [SMEM if o.ndim == 1 else HBM if n in in_hbm else VMEM for n, o in enumerate(operands)]
    scratch = [pltpu.VMEM(operands[n].shape, operands[n].dtype) for n in far]
    scratch += [pltpu.VMEM(out[n].shape, out[n].dtype) for n in far_out]
    if packed:
        height, width = operands[packed[0]].shape
        scratch.append(pltpu.VMEM((len(packed) * height, width), operands[packed[0]].dtype))
    scratch.append(pltpu.SemaphoreType.DMA((len(in_hbm) + sends + 1,)))
    operands = [pltpu.with_memory_space_constraint(o, pltpu.HBM) if n in in_hbm else o for n, o in enumerate(operands)]
    return pl.pallas_call(
        body,
        out_shape=[pltpu.HBM(o.shape, o.dtype) if n in far_out else o for n, o in enumerate(out)],
        in_specs=in_specs,
        out_specs=[HBM if n in far_out else VMEM for n in range(len(out))],
        scratch_shapes=scratch,
        input_output_aliases=aliases,
        cost_estimate=pl.CostEstimate(flops=1, bytes_accessed=1, transcendentals=0),
        compiler_params=pltpu.CompilerParams(vmem_limit_bytes=20 << 20),
    )(*operands)


def block_grads(numbers, columns, image_emb, match, text):
    wide = text.astype(F32)
    inv = lax.rsqrt(jnp.sum(wide * wide, -1, keepdims=True) + 1e-06)
    emb = (wide * inv).astype(BF16)
    logits = numbers[0] * inner_rows(image_emb, emb) + numbers[1]
    positive = (match == columns).astype(F32)
    return emb, (jax.nn.sigmoid(logits) - positive).astype(BF16)


def columns_of(place, key, rows):
    owner = place[0] + (key + Z) * (YH * CORE) - 2 * key * place[2] * (YH * CORE)
    start = owner % LOOP * rows
    return (lax.broadcasted_iota(jnp.int32, (1, rows), 1) + start).astype(F32)


def pairs_kernel(keys, first, moves, numbers, place, image_emb, match, *refs):
    count = len(keys)
    texts, refs = refs[:count], refs[count:]
    if not first:
        acc_in, refs = refs[0], refs[1:]
    acc_out, text_out = refs[0], refs[1:]
    image = image_emb[...]
    rows = texts[0].shape[0]
    columns = jnp.concatenate([columns_of(place, key, rows) for key in keys], 1)
    for n in range(count):
        moves.need(4 + n)
    emb, grad = block_grads(numbers, columns, image, match[...], moves.pack[...])
    text_part = inner_cols(grad, image)
    for n in range(count):
        text_out[n][...] = text_part[n * rows : (n + 1) * rows].astype(text_out[n].dtype)
        moves.send(1 + n)
    part = jnp.dot(grad, emb, preferred_element_type=F32)
    acc_out[...] = part if first else acc_in[...] + part


def project_kernel(moves, proj_weight, own, core, yh, both, *refs):
    matches, (emb, inv_out, match_out) = refs[:4], refs[4:]
    rows, cut = own.shape[0], CUT
    for n in range(4):
        moves.need(1 + n)
    sensor = moves.pack[...]
    moves.need((0, 0))
    projected = jnp.dot(sensor[:, :cut], proj_weight[:cut], preferred_element_type=F32)
    moves.need((0, 1))
    projected = projected + jnp.dot(sensor[:, cut:], proj_weight[cut:], preferred_element_type=F32)
    inv = lax.rsqrt(jnp.sum(projected * projected, -1, keepdims=True) + 1e-06)
    emb[...] = (projected * inv).astype(BF16)
    inv_out[...] = inv
    moves.send(1)
    moves.need(5)
    for n in range(4):
        match = jnp.broadcast_to(matches[n][...].astype(F32), (rows, rows))
        match_out[n * rows : (n + 1) * rows, :] = match.T[:, 0:1]


def last_kernel(moves, numbers, place, image_emb, match, text, acc_in, acc_out, dot_out, packet, grad_out):
    columns = columns_of(place, 4, text.shape[0])
    emb, grad = block_grads(numbers, columns, image_emb[...], match[...], text[...])
    grad_out[...] = grad
    acc = numbers[0] * (acc_in[...] + jnp.dot(grad, emb, preferred_element_type=F32))
    acc_out[...] = acc
    dot = jnp.sum(image_emb[...].astype(F32) * acc, -1, keepdims=True)
    dot_out[...] = dot
    rows, width = acc.shape
    half, quarter, block = width // 2, width // 4, rows // 4
    own = pl.multiple_of(place[2] * half, half)
    other = pl.multiple_of((1 - place[2]) * half, half)
    packet[:, :half] = acc_out[:, pl.ds(other, half)].astype(BF16)
    top = dot.astype(BF16).astype(F32)
    lane = lax.broadcasted_iota(jnp.int32, (rows, 128), 1)
    digits = jnp.where(lane == 0, top, jnp.where(lane == 1, dot - top, 0.0))
    packet[:, half : half + 128] = digits.astype(BF16)
    for side in range(2):
        lanes = pl.ds(pl.multiple_of(own + side * quarter, quarter), quarter)
        for n, slot in enumerate((1, 3)):
            at = (2 * side + n) * block
            packet[at : at + block, half + 128 :] = acc_out[slot * block : (slot + 1) * block, lanes].astype(BF16)


def last_text_kernel(moves, grad, image_emb, out):
    out[...] = inner_cols(grad[...], image_emb[...]).astype(out.dtype)
    moves.send(0)


def half_kernel(moves, place, got, acc, dot, kept, dot_out, packet, row_send, row_keep):
    rows, width = acc.shape
    half, quarter, block = width // 2, width // 4, rows // 4
    own_half = pl.multiple_of(place[2] * half, half)
    packet[rows:, :] = jnp.zeros((packet.shape[0] - rows, quarter), BF16)
    digit_rows = []
    for slot in range(4):
        mine = slice(slot * block, (slot + 1) * block)
        theirs = slice((slot ^ 1) * block, ((slot ^ 1) + 1) * block)
        digits = got[theirs, half : half + 128].astype(F32)
        whole_dot = dot[mine, :] + digits[:, 0:1] + digits[:, 1:2]
        dot_out[mine, :] = whole_dot
        flat = jnp.broadcast_to(whole_dot, (block, 128)).T[0:1, :]
        top = flat.astype(BF16).astype(F32)
        digit_rows.append(jnp.concatenate([top, flat - top], 1))
        for side in range(2):
            lanes = pl.ds(pl.multiple_of(own_half + side * quarter, quarter), quarter)
            total = acc[mine, lanes] + got[theirs, side * quarter : (side + 1) * quarter].astype(F32)

            @pl.when(place[1] == side)
            def _():
                kept[mine, :] = total

            @pl.when(place[1] != side)
            def _():
                packet[mine, :] = total.astype(BF16)

            if slot in (0, 2):
                target = (row_keep, row_send)[slot // 2]
                target[:, lanes] = total.astype(target.dtype)
                first = pl.multiple_of((1 - place[2]) * half + side * quarter, quarter)
                lanes = pl.ds(first, quarter)
                at = (2 * side + slot // 2) * block
                extra = got[at : at + block, half + 128 :].astype(F32)
                target[:, lanes] = (acc[mine, lanes] + extra).astype(target.dtype)
        if slot in (0, 2):
            moves.send(4 - slot // 2)
    fill = jnp.zeros((packet.shape[0] - rows - 4, quarter), F32)
    packet[rows:, :] = jnp.concatenate(digit_rows + [fill], 0).astype(BF16)


def weight_kernel(moves, place, got, kept, dot, image_emb, inv, own_rows, core_rows, yh_rows, both_rows, weight):
    rows, quarter = kept.shape
    block = rows // 4
    lanes = pl.ds(pl.multiple_of((place[2] * 2 + place[1]) * quarter, quarter), quarter)
    digits = got[rows:, :].astype(F32)
    moves.need(5)
    projs = []
    for slot in range(4):
        mine = slice(slot * block, (slot + 1) * block)
        theirs = slice((slot ^ 2) * block, ((slot ^ 2) + 1) * block)
        line = digits[slot ^ 2 : (slot ^ 2) + 1, :]
        other_dot = jnp.broadcast_to(line[:, :128] + line[:, 128:], (block, 128)).T[:, 0:1]
        whole = kept[mine, :] + got[theirs, :].astype(F32)
        unit = image_emb[mine, lanes].astype(F32)
        projs.append(((whole - unit * (dot[mine, :] + other_dot)) * inv[mine, :]).astype(BF16))
    proj = jnp.concatenate(projs, 0)
    for n in range(6, 10):
        moves.need(n)
    product = inner_cols(moves.pack[...], proj)
    count, height, wide = weight.shape
    tall = height // 2
    for n in range(count):
        piece = product[n * tall : (n + 1) * tall]
        weight[n] = jnp.concatenate([piece[:, :wide], piece[:, wide:]], 0).astype(BF16)
    moves.send(0)


def group_kernel(moves, parts, out):
    count, rows, _ = parts.shape
    quarters = count // Z
    for quarter in range(quarters):
        total = parts[quarter].astype(F32)
        for n in range(1, Z):
            total = total + parts[n * quarters + quarter].astype(F32)
        total = total.astype(BF16)
        for n in range(DP):
            out[n, quarter * rows : (quarter + 1) * rows] = total
    moves.send(0)


def layout_kernel(moves, parts, out):
    total = parts[0].astype(F32)
    for n in range(1, DP):
        total = total + parts[n].astype(F32)
    total = total * (1.0 / DP)
    tall, wide = out.shape[0], parts.shape[2]
    for y in range(YH):
        for core in range(CORE):
            for side in range(2):
                at = (y * CORE + core) * 2 + side
                to = ((core * YH + y) * 2 + side) * wide
                out[:, to : to + wide] = total[at * tall : (at + 1) * tall]
    moves.send(0)


def on_device(sensor_feats, text_embeds, proj_weight, matches, log_scale, logit_bias):
    sensor = sensor_feats[0]
    texts = text_embeds[0]
    rows = sensor.shape[0]
    feat, width = proj_weight.shape
    loop_index = lax.axis_index("loop")
    place = jnp.stack([loop_index, loop_index // CORE % YH, loop_index % CORE])
    logit_scale = jnp.exp(log_scale)
    numbers = jnp.stack([logit_scale, logit_bias])

    slot = {0: texts}
    slot[1], slot[-1] = shift_z(texts, -1), shift_z(texts, 1)

    sensor_yh = swap_yh(sensor)
    match = matches.reshape(1, rows)
    match_yh = swap_yh(match)
    up, down, _, _ = lax.optimization_barrier((slot[1], slot[-1], sensor_yh, match_yh))
    slot[2], slot[-2] = shift_z(up, -1), shift_z(down, 1)
    sensor_later, _ = lax.optimization_barrier((sensor, sensor_yh))
    sensors = [sensor, swap_core(sensor_later), sensor_yh, swap_core(sensor_yh)]
    match = [match, swap_core(match), match_yh, swap_core(match_yh)]
    shapes = [((4 * rows, width), BF16), ((4 * rows, 1), F32), ((4 * rows, 1), F32)]
    image_emb, image_inv, match_rows = call(
        project_kernel,
        [jax.ShapeDtypeStruct(*s) for s in shapes],
        {},
        proj_weight, *sensors, *match,
        far=(0, 5),
        packed=range(1, 5),
        far_out=(1,),
        cuts={0: CUT},
    )
    up, down, _ = lax.optimization_barrier((slot[2], slot[-2], image_emb))
    slot[3], slot[-3] = shift_z(up, -1), shift_z(down, 1)

    def pairs(keys, dtypes, acc):
        operands = [numbers, place, image_emb, match_rows, *(slot[k] for k in keys)]
        out = [jax.ShapeDtypeStruct((4 * rows, width), F32)]
        out += [jax.ShapeDtypeStruct((rows, width), d) for d in dtypes]
        aliases = {}
        if acc is not None:
            aliases = {len(operands): 0}
            operands.append(acc)
        kernel = functools.partial(pairs_kernel, keys, acc is None)
        return call(kernel, out, aliases, *operands, packed=range(4, 4 + len(keys)), far_out=range(1, len(out)))

    acc, text_0, text_1, text_m1, text_2, text_m2 = pairs((0, 1, -1, 2, -2), (F32, BF16, BF16, BF16, BF16), None)
    last_text, _ = lax.optimization_barrier((slot[-3], acc))
    last_text = shift_z(last_text, 1)
    acc, text_3, text_m3 = pairs((3, -3), (BF16, BF16), acc)
    shapes = [((4 * rows, width), F32), ((4 * rows, 1), F32), ((4 * rows, width // 8 * 7), BF16), ((4 * rows, rows), BF16)]
    acc, dot, packet, last_grad = call(
        last_kernel,
        [jax.ShapeDtypeStruct(*s) for s in shapes],
        {5: 0},
        numbers, place, image_emb, match_rows, last_text, acc,
    )
    (text_4,) = call(
        last_text_kernel, [jax.ShapeDtypeStruct((rows, width), BF16)], {}, last_grad, image_emb, far_out=(0,)
    )

    shapes = [((4 * rows, width // 4), F32), ((4 * rows, 1), F32), ((4 * rows + 16, width // 4), BF16)]
    shapes += [((rows, width), BF16), ((rows, width), F32)]
    kept, dot, packet, row_send, row_keep = call(
        half_kernel,
        [jax.ShapeDtypeStruct(*s) for s in shapes],
        {},
        place, swap_core(packet), acc, dot,
        far_out=(3, 4),
    )
    text_3, text_m3, text_4, _ = lax.optimization_barrier((text_3, text_m3, text_4, kept))
    from_below, from_above = shift_z(text_3, 1), shift_z(text_m3, -1)
    packet, text_4, from_below, from_above = lax.optimization_barrier((swap_yh(packet), text_4, from_below, from_above))
    per_loop = feat // LOOP
    block = (2 * per_loop, width // 8)
    (weight_part,) = call(
        weight_kernel,
        [jax.ShapeDtypeStruct((LOOP,) + block, BF16)],
        {},
        place, packet, kept, dot, image_emb, image_inv, *sensors,
        far=(5,),
        packed=range(6, 10),
        far_out=(0,),
    )
    group_part = lax.all_to_all(weight_part, "loop", 0, 0, tiled=True)
    (shares,) = call(
        group_kernel, [jax.ShapeDtypeStruct((DP, YH * CORE * block[0], block[1]), BF16)], {}, group_part, far_out=(0,)
    )

    text_4, text_1, text_m1, _ = lax.optimization_barrier((text_4, text_1, text_m1, packet))
    far = shift_z(text_4, 2)
    near_below, near_above = shift_z(text_1, 1), shift_z(text_m1, -1)
    from_below, from_above, far, near_below, near_above, row_send, _ = lax.optimization_barrier(
        (from_below, from_above, far, near_below, near_above, row_send, weight_part)
    )
    row_got = swap_yh(row_send)
    up = text_2.astype(F32) + from_below.astype(F32) + far.astype(F32)
    down = text_m2.astype(F32) + from_above.astype(F32)
    up, down = shift_z(up.astype(BF16), 2), shift_z(down.astype(BF16), -2)
    up, down, row_got, _ = lax.optimization_barrier((up, down, row_got, shares))
    shares = lax.all_to_all(shares, "dp", 0, 0, tiled=True)
    (weight_grad,) = call(
        layout_kernel, [jax.ShapeDtypeStruct((per_loop, width), F32)], {}, shares, far_out=(0,)
    )
    text_sum = text_0 + near_below.astype(F32) + near_above.astype(F32)
    text_sum = logit_scale * (text_sum + up.astype(F32) + down.astype(F32))
    text_wide = texts.astype(F32)
    text_inv = lax.rsqrt(jnp.sum(text_wide * text_wide, -1, keepdims=True) + 1e-06)
    text_unit = text_wide * text_inv
    text_grad = (text_sum - text_unit * jnp.sum(text_unit * text_sum, -1, keepdims=True)) * text_inv

    image_grad = row_keep + row_got.astype(F32)
    own_unit = image_emb[:rows].astype(F32)
    own_dot = jnp.sum(own_unit * image_grad, -1, keepdims=True)
    proj_grad = ((image_grad - own_unit * own_dot) * image_inv[:rows]).astype(BF16)
    sensor_grad = inner_rows(proj_grad, proj_weight).astype(BF16)
    return (sensor_grad[None], text_grad[None], weight_grad)


def solution(mesh):
    placed = (P("dp", "loop", None), P("dp", "loop", None), P(), P("dp", "loop"), P(), P())
    return jax.shard_map(
        on_device,
        mesh=mesh,
        in_specs=placed,
        out_specs=(P("dp", "loop", None), P("dp", "loop", None), P("loop", None)),
        check_vma=False,
    )
```

```python
import functools

import jax
import jax.numpy as jnp
from jax import lax
from jax.experimental import pallas as pl
from jax.experimental.pallas import tpu as pltpu
from jax.sharding import PartitionSpec as P

Z, YH, CORE = 8, 2, 2
LOOP = Z * YH * CORE
DP = 8
CUT = 640
BF16 = jnp.bfloat16
F32 = jnp.float32
VMEM = pl.BlockSpec(memory_space=pltpu.VMEM)
HBM = pl.BlockSpec(memory_space=pltpu.HBM)
SMEM = pl.BlockSpec(memory_space=pltpu.SMEM)


def route(move):
    pairs = []
    for z in range(Z):
        for y in range(YH):
            for c in range(CORE):
                to_z, to_y, to_c = move(z, y, c)
                source = (z * YH + y) * CORE + c
                pairs.append((source, ((to_z % Z) * YH + to_y) * CORE + to_c))
    return pairs


def shift_z(block, distance):
    return lax.ppermute(block, "loop", route(lambda z, y, c: (z + (1 - 2 * c) * distance, y, c)))


def swap_core(block):
    return lax.ppermute(block, "loop", route(lambda z, y, c: (z, y, 1 - c)))


def swap_yh(block):
    return lax.ppermute(block, "loop", route(lambda z, y, c: (z, 1 - y, c)))


def inner_rows(left, right):
    return lax.dot_general(left, right, (((1,), (1,)), ((), ())), preferred_element_type=F32)


def inner_cols(left, right):
    return lax.dot_general(left, right, (((0,), (0,)), ((), ())), preferred_element_type=F32)


class Moves:
    def __init__(self, base, sems, loads, held, outs, pack):
        self.base = base
        self.sems, self.loads, self.held, self.outs, self.pack, self.sent = sems, loads, held, outs, pack, []

    def need(self, n):
        self.loads[n].wait()

    def send(self, n, part=None):
        source, target = self.held[n], self.outs[n]
        if part is not None:
            source, target = source.at[part], target.at[part]
        copy = pltpu.make_async_copy(source, target, self.sems.at[self.base + len(self.sent)])
        copy.start()
        self.sent.append(copy)


def call(kernel, out, aliases, *operands, far=(), packed=(), far_out=(), sends=None, cuts=()):
    cuts = dict(cuts)
    far, packed, far_out, total = list(far), list(packed), list(far_out), len(operands)
    sends = len(far_out) if sends is None else sends

    def body(*refs):
        ins, outs, scratch = refs[:total], refs[total : total + len(out)], refs[total + len(out) :]
        held = dict(zip(far, scratch[: len(far)]))
        held_out = dict(zip(far_out, scratch[len(far) : len(far) + len(far_out)]))
        for m, n in enumerate(packed):
            height = operands[n].shape[0]
            held[n] = scratch[-2].at[pl.ds(m * height, height)]
        whole = [(m, n) for m, n in enumerate(in_hbm) if n not in cuts]
        loads = {n: pltpu.make_async_copy(ins[n], held[n], scratch[-1].at[m]) for m, n in whole}
        for n, cut in cuts.items():
            for m, part in enumerate((pl.ds(0, cut), pl.ds(cut, operands[n].shape[0] - cut))):
                sem = scratch[-1].at[len(in_hbm) + sends] if m else scratch[-1].at[far.index(n)]
                loads[n, m] = pltpu.make_async_copy(ins[n].at[part], held[n].at[part], sem)
        for load in loads.values():
            load.start()
        moves = Moves(len(in_hbm), scratch[-1], loads, held_out, outs, scratch[-2] if packed else None)
        kernel(moves, *(held.get(n, ref) for n, ref in enumerate(ins)), *(held_out.get(n, ref) for n, ref in enumerate(outs)))
        for copy in moves.sent:
            copy.wait()

    in_hbm = far + packed
    in_specs = [SMEM if o.ndim == 1 else HBM if n in in_hbm else VMEM for n, o in enumerate(operands)]
    scratch = [pltpu.VMEM(operands[n].shape, operands[n].dtype) for n in far]
    scratch += [pltpu.VMEM(out[n].shape, out[n].dtype) for n in far_out]
    if packed:
        height, width = operands[packed[0]].shape
        scratch.append(pltpu.VMEM((len(packed) * height, width), operands[packed[0]].dtype))
    scratch.append(pltpu.SemaphoreType.DMA((len(in_hbm) + sends + 1,)))
    operands = [pltpu.with_memory_space_constraint(o, pltpu.HBM) if n in in_hbm else o for n, o in enumerate(operands)]
    return pl.pallas_call(
        body,
        out_shape=[pltpu.HBM(o.shape, o.dtype) if n in far_out else o for n, o in enumerate(out)],
        in_specs=in_specs,
        out_specs=[HBM if n in far_out else VMEM for n in range(len(out))],
        scratch_shapes=scratch,
        input_output_aliases=aliases,
        cost_estimate=pl.CostEstimate(flops=1, bytes_accessed=1, transcendentals=0),
        compiler_params=pltpu.CompilerParams(vmem_limit_bytes=20 << 20),
    )(*operands)


def block_grads(numbers, columns, image_emb, match, text):
    wide = text.astype(F32)
    inv = lax.rsqrt(jnp.sum(wide * wide, -1, keepdims=True) + 1e-06)
    emb = (wide * inv).astype(BF16)
    logits = numbers[0] * inner_rows(image_emb, emb) + numbers[1]
    positive = (match == columns).astype(F32)
    return emb, (jax.nn.sigmoid(logits) - positive).astype(BF16)


def columns_of(place, key, rows):
    step = (1 - 2 * (place[0] & 1)) * (YH * CORE)
    start = (place[0] + key * step + LOOP) % LOOP * rows
    return (lax.broadcasted_iota(jnp.int32, (1, rows), 1) + start).astype(F32)


def pairs_kernel(keys, first, moves, numbers, place, image_emb, match, *refs):
    count = len(keys)
    texts, refs = refs[:count], refs[count:]
    if not first:
        acc_in, refs = refs[0], refs[1:]
    acc_out, text_out = refs[0], refs[1:]
    image = image_emb[...]
    rows = texts[0].shape[0]
    columns = jnp.concatenate([columns_of(place, key, rows) for key in keys], 1)
    for n in range(count):
        moves.need(4 + n)
    emb, grad = block_grads(numbers, columns, image, match[...], moves.pack[...])
    text_part = inner_cols(grad, image)
    for n in range(count):
        text_out[n][...] = text_part[n * rows : (n + 1) * rows].astype(text_out[n].dtype)
        moves.send(1 + n)
    part = jnp.dot(grad, emb, preferred_element_type=F32)
    acc_out[...] = part if first else acc_in[...] + part


def project_kernel(moves, proj_weight, own, core, yh, both, *refs):
    matches, (emb, inv_out, match_out) = refs[:4], refs[4:]
    rows, cut = own.shape[0], CUT
    for n in range(4):
        moves.need(1 + n)
    sensor = moves.pack[...]
    moves.need((0, 0))
    projected = jnp.dot(sensor[:, :cut], proj_weight[:cut], preferred_element_type=F32)
    moves.need((0, 1))
    projected = projected + jnp.dot(sensor[:, cut:], proj_weight[cut:], preferred_element_type=F32)
    inv = lax.rsqrt(jnp.sum(projected * projected, -1, keepdims=True) + 1e-06)
    emb[...] = (projected * inv).astype(BF16)
    inv_out[...] = inv
    moves.send(1)
    moves.need(5)
    for n in range(4):
        match = jnp.broadcast_to(matches[n][...].astype(F32), (rows, rows))
        match_out[n * rows : (n + 1) * rows, :] = match.T[:, 0:1]


def last_kernel(moves, numbers, place, image_emb, match, text, acc_in, acc_out, dot_out, packet, extra, grad_out):
    columns = columns_of(place, 4, text.shape[0])
    emb, grad = block_grads(numbers, columns, image_emb[...], match[...], text[...])
    grad_out[...] = grad
    acc = numbers[0] * (acc_in[...] + jnp.dot(grad, emb, preferred_element_type=F32))
    acc_out[...] = acc
    dot = jnp.sum(image_emb[...].astype(F32) * acc, -1, keepdims=True)
    dot_out[...] = dot
    rows, width = acc.shape
    half, block = width // 2, rows // 4
    core = place[0] & 1
    own = pl.ds(pl.multiple_of(core * half, half), half)
    other = pl.ds(pl.multiple_of((1 - core) * half, half), half)
    for n, slot in enumerate((1, 3)):
        extra[n * block : (n + 1) * block, :] = acc_out[slot * block : (slot + 1) * block, own].astype(BF16)
    moves.send(3)
    packet[:rows, :] = acc_out[:, other].astype(BF16)
    lines = []
    for slot in range(4):
        mine = slice(slot * block, (slot + 1) * block)
        flat = jnp.broadcast_to(dot[mine], (block, 128)).T[0:1, :]
        top = flat.astype(BF16).astype(F32)
        lines.append(jnp.concatenate([top, flat - top, jnp.zeros((1, half - 256), F32)], 1))
    lines.append(jnp.zeros((packet.shape[0] - rows - 4, half), F32))
    packet[rows:, :] = jnp.concatenate(lines, 0).astype(BF16)


def last_text_kernel(moves, grad, image_emb, out):
    out[...] = inner_cols(grad[...], image_emb[...]).astype(out.dtype)
    moves.send(0)


def weight_kernel(moves, place, got, acc, dot, image_emb, inv, own_rows, core_rows, yh_rows, both_rows, weight):
    rows, width = acc.shape
    half, quarter, block = width // 2, width // 4, rows // 4
    own = pl.ds(pl.multiple_of((place[0] & 1) * half, half), half)
    digits = got[rows:, :256].astype(F32)
    moves.need(5)
    projs = []
    for slot in range(4):
        mine = slice(slot * block, (slot + 1) * block)
        theirs = slice((slot ^ 1) * block, ((slot ^ 1) + 1) * block)
        kept = acc[mine, own] + got[theirs, :].astype(F32)
        line = digits[slot ^ 1 : (slot ^ 1) + 1, :]
        other_dot = jnp.broadcast_to(line[:, :128] + line[:, 128:], (block, 128)).T[:, 0:1]
        unit = image_emb[mine, own].astype(F32)
        projs.append(((kept - unit * (dot[mine, :] + other_dot)) * inv[mine, :]).astype(BF16))
    proj = jnp.concatenate(projs, 0)
    sensor = jnp.concatenate([own_rows[...], core_rows[...], yh_rows[...], both_rows[...]], 0)
    chunk = weight.shape[1]
    for side in range(2):
        product = inner_cols(proj[:, side * quarter : (side + 1) * quarter], sensor).astype(BF16)
        for m in range(quarter // chunk):
            at = side * (quarter // chunk) + m
            weight[at] = product[m * chunk : (m + 1) * chunk]
            moves.send(0, at)


def row_kernel(moves, place, got, extra, acc, row_send, row_keep):
    rows, width = acc.shape
    half, block = width // 2, rows // 4
    core = place[0] & 1
    own = pl.ds(pl.multiple_of(core * half, half), half)
    other = pl.ds(pl.multiple_of((1 - core) * half, half), half)
    moves.need(1)
    for n, target in enumerate((row_keep, row_send)):
        slot = 2 * n
        mine = slice(slot * block, (slot + 1) * block)
        theirs = slice((slot + 1) * block, (slot + 2) * block)
        target[:, own] = (acc[mine, own] + got[theirs, :].astype(F32)).astype(target.dtype)
        rest = extra[n * block : (n + 1) * block, :].astype(F32)
        target[:, other] = (acc[mine, other] + rest).astype(target.dtype)
        moves.send(1 - n)


def chunk_kernel(moves, parts, out):
    total = parts[0].astype(F32)
    for n in range(1, parts.shape[0]):
        total = total + parts[n].astype(F32)
    turned = total.T
    count, rows, lanes = out.shape
    for n in range(count):
        at = 2 * rows * n
        out[n] = jnp.concatenate([turned[at : at + rows], turned[at + rows : at + 2 * rows]], 1).astype(BF16)
    moves.send(0)


def share_kernel(moves, parts, out):
    rows = parts.shape[1]
    for core in range(CORE):
        total = parts[core].astype(F32)
        for n in range(1, Z * YH):
            total = total + parts[n * CORE + core].astype(F32)
        total = total * (1.0 / DP)
        for n in range(DP):
            out[n, core * rows : (core + 1) * rows] = total
    moves.send(0)


def layout_kernel(moves, shares, out):
    rows, lanes = shares.shape[1] // 2, shares.shape[2]
    cols = lanes // 2
    for core in range(CORE):
        here = slice(core * rows, (core + 1) * rows)
        for pair in range(DP // 2):
            left, right = shares[2 * pair, here], shares[2 * pair + 1, here]
            at = core * DP * cols + pair * lanes
            out[:rows, at : at + lanes] = jnp.concatenate([left[:, :cols], right[:, :cols]], 1)
            out[rows:, at : at + lanes] = jnp.concatenate([left[:, cols:], right[:, cols:]], 1)
    moves.send(0)


def on_device(sensor_feats, text_embeds, proj_weight, matches, log_scale, logit_bias):
    sensor = sensor_feats[0]
    texts = text_embeds[0]
    rows = sensor.shape[0]
    feat, width = proj_weight.shape
    loop_index = lax.axis_index("loop")
    place = loop_index.reshape(1)
    logit_scale = jnp.exp(log_scale)
    numbers = jnp.stack([logit_scale, logit_bias])

    slot = {0: texts}
    slot[1], slot[-1] = shift_z(texts, -1), shift_z(texts, 1)

    sensor_yh = swap_yh(sensor)
    match = matches.reshape(1, rows)
    match_yh = swap_yh(match)
    up, down, _, _ = lax.optimization_barrier((slot[1], slot[-1], sensor_yh, match_yh))
    slot[2], slot[-2] = shift_z(up, -1), shift_z(down, 1)
    sensor_later, _ = lax.optimization_barrier((sensor, sensor_yh))
    sensors = [sensor, swap_core(sensor_later), sensor_yh, swap_core(sensor_yh)]
    match = [match, swap_core(match), match_yh, swap_core(match_yh)]
    shapes = [((4 * rows, width), BF16), ((4 * rows, 1), F32), ((4 * rows, 1), F32)]
    image_emb, image_inv, match_rows = call(
        project_kernel,
        [jax.ShapeDtypeStruct(*s) for s in shapes],
        {},
        proj_weight, *sensors, *match,
        far=(0, 5),
        packed=range(1, 5),
        far_out=(1,),
        cuts={0: CUT},
    )
    up, down, _ = lax.optimization_barrier((slot[2], slot[-2], image_emb))
    slot[3], slot[-3] = shift_z(up, -1), shift_z(down, 1)

    def pairs(keys, dtypes, acc):
        operands = [numbers, place, image_emb, match_rows, *(slot[k] for k in keys)]
        out = [jax.ShapeDtypeStruct((4 * rows, width), F32)]
        out += [jax.ShapeDtypeStruct((rows, width), d) for d in dtypes]
        aliases = {}
        if acc is not None:
            aliases = {len(operands): 0}
            operands.append(acc)
        kernel = functools.partial(pairs_kernel, keys, acc is None)
        return call(kernel, out, aliases, *operands, packed=range(4, 4 + len(keys)), far_out=range(1, len(out)))

    acc, text_0, text_1, text_m1, text_2, text_m2 = pairs((0, 1, -1, 2, -2), (F32, BF16, BF16, BF16, BF16), None)
    last_text, _ = lax.optimization_barrier((slot[-3], acc))
    last_text = shift_z(last_text, 1)
    acc, text_3, text_m3 = pairs((3, -3), (BF16, BF16), acc)
    shapes = [((4 * rows, width), F32), ((4 * rows, 1), F32), ((4 * rows + 16, width // 2), BF16)]
    shapes += [((2 * rows, width // 2), BF16), ((4 * rows, rows), BF16)]
    acc, dot, packet, extra, last_grad = call(
        last_kernel,
        [jax.ShapeDtypeStruct(*s) for s in shapes],
        {5: 0},
        numbers, place, image_emb, match_rows, last_text, acc,
        far_out=(3,),
    )

    got = swap_core(packet)
    (weight_part,) = call(
        weight_kernel,
        [jax.ShapeDtypeStruct((DP, width // 16, feat), BF16)],
        {},
        place, got, acc, dot, image_emb, image_inv, *sensors,
        far=(5,),
        far_out=(0,),
        sends=DP,
    )
    last_grad, extra, text_1, text_m1, text_3, text_m3, _ = lax.optimization_barrier(
        (last_grad, extra, text_1, text_m1, text_3, text_m3, weight_part)
    )
    (text_4,) = call(
        last_text_kernel, [jax.ShapeDtypeStruct((rows, width), BF16)], {}, last_grad, image_emb, far_out=(0,)
    )
    shapes = [((rows, width), BF16), ((rows, width), F32)]
    row_send, row_keep = call(
        row_kernel,
        [jax.ShapeDtypeStruct(*s) for s in shapes],
        {},
        place, got, swap_core(extra), acc,
        far=(1,),
        far_out=(0, 1),
    )
    weight_part = lax.all_to_all(weight_part, "dp", 0, 0, tiled=True)

    per_loop = feat // LOOP
    block = (per_loop // 2, width // 8)
    (weight_chunks,) = call(
        chunk_kernel, [jax.ShapeDtypeStruct((LOOP,) + block, BF16)], {}, weight_part, far_out=(0,)
    )
    weight_part = lax.all_to_all(weight_chunks, "loop", 0, 0, tiled=True)
    (shares,) = call(
        share_kernel, [jax.ShapeDtypeStruct((DP, per_loop, width // 8), F32)], {}, weight_part, far_out=(0,)
    )

    from_below, from_above, far = shift_z(text_3, 1), shift_z(text_m3, -1), shift_z(text_4, 2)
    near_below, near_above = shift_z(text_1, 1), shift_z(text_m1, -1)
    from_below, from_above, far, near_below, near_above, row_send, _ = lax.optimization_barrier(
        (from_below, from_above, far, near_below, near_above, row_send, weight_chunks)
    )
    row_got = swap_yh(row_send)
    up = text_2.astype(F32) + from_below.astype(F32) + far.astype(F32)
    down = text_m2.astype(F32) + from_above.astype(F32)
    up, down = shift_z(up.astype(BF16), 2), shift_z(down.astype(BF16), -2)
    up, down, row_got, _ = lax.optimization_barrier((up, down, row_got, shares))
    shares = lax.all_to_all(shares, "dp", 0, 0, tiled=True)
    (weight_grad,) = call(
        layout_kernel, [jax.ShapeDtypeStruct((per_loop, width), F32)], {}, shares, far_out=(0,)
    )
    text_sum = text_0 + near_below.astype(F32) + near_above.astype(F32)
    text_sum = logit_scale * (text_sum + up.astype(F32) + down.astype(F32))
    text_wide = texts.astype(F32)
    text_inv = lax.rsqrt(jnp.sum(text_wide * text_wide, -1, keepdims=True) + 1e-06)
    text_unit = text_wide * text_inv
    text_grad = (text_sum - text_unit * jnp.sum(text_unit * text_sum, -1, keepdims=True)) * text_inv

    image_grad = row_keep + row_got.astype(F32)
    own_unit = image_emb[:rows].astype(F32)
    own_dot = jnp.sum(own_unit * image_grad, -1, keepdims=True)
    proj_grad = ((image_grad - own_unit * own_dot) * image_inv[:rows]).astype(BF16)
    sensor_grad = inner_rows(proj_grad, proj_weight).astype(BF16)
    return (sensor_grad[None], text_grad[None], weight_grad)


def solution(mesh):
    placed = (P("dp", "loop", None), P("dp", "loop", None), P(), P("dp", "loop"), P(), P())
    return jax.shard_map(
        on_device,
        mesh=mesh,
        in_specs=placed,
        out_specs=(P("dp", "loop", None), P("dp", "loop", None), P("loop", None)),
        check_vma=False,
    )
```

```python
import functools

import jax
import jax.numpy as jnp
from jax import lax
from jax.experimental import pallas as pl
from jax.experimental.pallas import tpu as pltpu
from jax.sharding import PartitionSpec as P

Z, YH, CORE = 8, 2, 2
LOOP = Z * YH * CORE
DP = 8
CUT = 640
BF16 = jnp.bfloat16
F32 = jnp.float32
VMEM = pl.BlockSpec(memory_space=pltpu.VMEM)
HBM = pl.BlockSpec(memory_space=pltpu.HBM)
SMEM = pl.BlockSpec(memory_space=pltpu.SMEM)


def route(move):
    pairs = []
    for z in range(Z):
        for y in range(YH):
            for c in range(CORE):
                to_z, to_y, to_c = move(z, y, c)
                source = (z * YH + y) * CORE + c
                pairs.append((source, ((to_z % Z) * YH + to_y) * CORE + to_c))
    return pairs


def shift_z(block, distance):
    return lax.ppermute(block, "loop", route(lambda z, y, c: (z + (1 - 2 * c) * distance, y, c)))


def swap_core(block):
    return lax.ppermute(block, "loop", route(lambda z, y, c: (z, y, 1 - c)))


def swap_yh(block):
    return lax.ppermute(block, "loop", route(lambda z, y, c: (z, 1 - y, c)))


def inner_rows(left, right):
    return lax.dot_general(left, right, (((1,), (1,)), ((), ())), preferred_element_type=F32)


def inner_cols(left, right):
    return lax.dot_general(left, right, (((0,), (0,)), ((), ())), preferred_element_type=F32)


class Moves:
    def __init__(self, base, sems, loads, held, outs, pack):
        self.base = base
        self.sems, self.loads, self.held, self.outs, self.pack, self.sent = sems, loads, held, outs, pack, []

    def need(self, n):
        self.loads[n].wait()

    def send(self, n, part=None):
        source, target = self.held[n], self.outs[n]
        if part is not None:
            source, target = source.at[part], target.at[part]
        copy = pltpu.make_async_copy(source, target, self.sems.at[self.base + len(self.sent)])
        copy.start()
        self.sent.append(copy)


def call(kernel, out, aliases, *operands, far=(), packed=(), far_out=(), sends=None, cuts=()):
    cuts = dict(cuts)
    far, packed, far_out, total = list(far), list(packed), list(far_out), len(operands)
    sends = len(far_out) if sends is None else sends

    def body(*refs):
        ins, outs, scratch = refs[:total], refs[total : total + len(out)], refs[total + len(out) :]
        held = dict(zip(far, scratch[: len(far)]))
        held_out = dict(zip(far_out, scratch[len(far) : len(far) + len(far_out)]))
        for m, n in enumerate(packed):
            height = operands[n].shape[0]
            held[n] = scratch[-2].at[pl.ds(m * height, height)]
        whole = [(m, n) for m, n in enumerate(in_hbm) if n not in cuts]
        loads = {n: pltpu.make_async_copy(ins[n], held[n], scratch[-1].at[m]) for m, n in whole}
        for n, cut in cuts.items():
            for m, part in enumerate((pl.ds(0, cut), pl.ds(cut, operands[n].shape[0] - cut))):
                sem = scratch[-1].at[len(in_hbm) + sends] if m else scratch[-1].at[far.index(n)]
                loads[n, m] = pltpu.make_async_copy(ins[n].at[part], held[n].at[part], sem)
        for load in loads.values():
            load.start()
        moves = Moves(len(in_hbm), scratch[-1], loads, held_out, outs, scratch[-2] if packed else None)
        kernel(moves, *(held.get(n, ref) for n, ref in enumerate(ins)), *(held_out.get(n, ref) for n, ref in enumerate(outs)))
        for copy in moves.sent:
            copy.wait()

    in_hbm = far + packed
    in_specs = [SMEM if o.ndim == 1 else HBM if n in in_hbm else VMEM for n, o in enumerate(operands)]
    scratch = [pltpu.VMEM(operands[n].shape, operands[n].dtype) for n in far]
    scratch += [pltpu.VMEM(out[n].shape, out[n].dtype) for n in far_out]
    if packed:
        height, width = operands[packed[0]].shape
        scratch.append(pltpu.VMEM((len(packed) * height, width), operands[packed[0]].dtype))
    scratch.append(pltpu.SemaphoreType.DMA((len(in_hbm) + sends + 1,)))
    operands = [pltpu.with_memory_space_constraint(o, pltpu.HBM) if n in in_hbm else o for n, o in enumerate(operands)]
    return pl.pallas_call(
        body,
        out_shape=[pltpu.HBM(o.shape, o.dtype) if n in far_out else o for n, o in enumerate(out)],
        in_specs=in_specs,
        out_specs=[HBM if n in far_out else VMEM for n in range(len(out))],
        scratch_shapes=scratch,
        input_output_aliases=aliases,
        cost_estimate=pl.CostEstimate(flops=1, bytes_accessed=1, transcendentals=0),
        compiler_params=pltpu.CompilerParams(vmem_limit_bytes=20 << 20),
    )(*operands)


def scale_of(numbers):
    return jnp.exp(jnp.full((1, 128), numbers[0], F32))[:, 0:1]


def block_grads(numbers, columns, image_emb, match, text):
    wide = text.astype(F32)
    inv = lax.rsqrt(jnp.sum(wide * wide, -1, keepdims=True) + 1e-06)
    emb = (wide * inv).astype(BF16)
    logits = scale_of(numbers) * inner_rows(image_emb, emb) + numbers[1]
    positive = (match == columns).astype(F32)
    return emb, (jax.nn.sigmoid(logits) - positive).astype(BF16)


def columns_of(place, key, rows):
    step = (1 - 2 * (place[0] & 1)) * (YH * CORE)
    start = (place[0] + key * step + LOOP) % LOOP * rows
    return (lax.broadcasted_iota(jnp.int32, (1, rows), 1) + start).astype(F32)


def pairs_kernel(keys, first, moves, numbers, place, image_emb, match, *refs):
    count = len(keys)
    texts, refs = refs[:count], refs[count:]
    if not first:
        acc_in, refs = refs[0], refs[1:]
    acc_out, text_out = refs[0], refs[1:]
    image = image_emb[...]
    rows = texts[0].shape[0]
    columns = jnp.concatenate([columns_of(place, key, rows) for key in keys], 1)
    for n in range(count):
        moves.need(4 + n)
    emb, grad = block_grads(numbers, columns, image, match[...], moves.pack[...])
    text_part = inner_cols(grad, image)
    for n in range(count):
        text_out[n][...] = text_part[n * rows : (n + 1) * rows].astype(text_out[n].dtype)
        moves.send(1 + n)
    part = jnp.dot(grad, emb, preferred_element_type=F32)
    acc_out[...] = part if first else acc_in[...] + part


def project_kernel(moves, proj_weight, own, core, yh, both, *refs):
    matches, (emb, inv_out, match_out) = refs[:4], refs[4:]
    rows, cut = own.shape[0], CUT
    for n in range(4):
        moves.need(1 + n)
    sensor = moves.pack[...]
    moves.need((0, 0))
    projected = jnp.dot(sensor[:, :cut], proj_weight[:cut], preferred_element_type=F32)
    moves.need((0, 1))
    projected = projected + jnp.dot(sensor[:, cut:], proj_weight[cut:], preferred_element_type=F32)
    inv = lax.rsqrt(jnp.sum(projected * projected, -1, keepdims=True) + 1e-06)
    emb[...] = (projected * inv).astype(BF16)
    inv_out[...] = inv
    moves.send(1)
    moves.need(5)
    for n in range(4):
        match = jnp.broadcast_to(matches[n][...].astype(F32), (rows, rows))
        match_out[n * rows : (n + 1) * rows, :] = match.T[:, 0:1]


def last_kernel(moves, numbers, place, image_emb, match, text, acc_in, acc_out, dot_out, packet, extra, grad_out):
    columns = columns_of(place, 4, text.shape[0])
    emb, grad = block_grads(numbers, columns, image_emb[...], match[...], text[...])
    grad_out[...] = grad
    acc = scale_of(numbers) * (acc_in[...] + jnp.dot(grad, emb, preferred_element_type=F32))
    acc_out[...] = acc
    dot = jnp.sum(image_emb[...].astype(F32) * acc, -1, keepdims=True)
    dot_out[...] = dot
    rows, width = acc.shape
    half, block = width // 2, rows // 4
    core = place[0] & 1
    own = pl.ds(pl.multiple_of(core * half, half), half)
    other = pl.ds(pl.multiple_of((1 - core) * half, half), half)
    for n, slot in enumerate((1, 3)):
        extra[n * block : (n + 1) * block, :] = acc_out[slot * block : (slot + 1) * block, own].astype(BF16)
    moves.send(3)
    packet[:rows, :] = acc_out[:, other].astype(BF16)
    lines = []
    for slot in range(4):
        mine = slice(slot * block, (slot + 1) * block)
        flat = jnp.broadcast_to(dot[mine], (block, 128)).T[0:1, :]
        top = flat.astype(BF16).astype(F32)
        lines.append(jnp.concatenate([top, flat - top, jnp.zeros((1, half - 256), F32)], 1))
    lines.append(jnp.zeros((packet.shape[0] - rows - 4, half), F32))
    packet[rows:, :] = jnp.concatenate(lines, 0).astype(BF16)


def last_text_kernel(moves, grad, image_emb, out):
    out[...] = inner_cols(grad[...], image_emb[...]).astype(out.dtype)
    moves.send(0)


def weight_kernel(moves, place, got, acc, dot, image_emb, inv, own_rows, core_rows, yh_rows, both_rows, weight, row_half):
    rows, width = acc.shape
    half, quarter, block = width // 2, width // 4, rows // 4
    own = pl.ds(pl.multiple_of((place[0] & 1) * half, half), half)
    digits = got[rows:, :256].astype(F32)
    moves.need(5)
    projs = []
    for slot in range(4):
        mine = slice(slot * block, (slot + 1) * block)
        theirs = slice((slot ^ 1) * block, ((slot ^ 1) + 1) * block)
        kept = acc[mine, own] + got[theirs, :].astype(F32)
        if slot in (0, 2):
            row_half[slot // 2 * block : (slot // 2 + 1) * block, :] = kept
            if slot == 2:
                moves.send(1)
        line = digits[slot ^ 1 : (slot ^ 1) + 1, :]
        other_dot = jnp.broadcast_to(line[:, :128] + line[:, 128:], (block, 128)).T[:, 0:1]
        unit = image_emb[mine, own].astype(F32)
        projs.append(((kept - unit * (dot[mine, :] + other_dot)) * inv[mine, :]).astype(BF16))
    proj = jnp.concatenate(projs, 0)
    sensor = jnp.concatenate([own_rows[...], core_rows[...], yh_rows[...], both_rows[...]], 0)
    chunk = weight.shape[1]
    for side in range(2):
        product = inner_cols(proj[:, side * quarter : (side + 1) * quarter], sensor).astype(BF16)
        for m in range(quarter // chunk):
            at = side * (quarter // chunk) + m
            weight[at] = product[m * chunk : (m + 1) * chunk]
            moves.send(0, at)


def row_kernel(moves, place, row_half, extra, acc, row_send, row_keep):
    rows, width = acc.shape
    half, block = width // 2, rows // 4
    core = place[0] & 1
    own = pl.ds(pl.multiple_of(core * half, half), half)
    other = pl.ds(pl.multiple_of((1 - core) * half, half), half)
    moves.need(1)
    for n, target in enumerate((row_keep, row_send)):
        here = slice(n * block, (n + 1) * block)
        target[:, own] = row_half[here, :].astype(target.dtype)
        rest = extra[here, :].astype(F32)
        target[:, other] = (acc[2 * n * block : (2 * n + 1) * block, other] + rest).astype(target.dtype)
        moves.send(1 - n)


def chunk_kernel(moves, parts, out):
    total = parts[0].astype(F32)
    for n in range(1, parts.shape[0]):
        total = total + parts[n].astype(F32)
    turned = total.T
    count, rows, lanes = out.shape
    for n in range(count):
        at = 2 * rows * n
        out[n] = jnp.concatenate([turned[at : at + rows], turned[at + rows : at + 2 * rows]], 1).astype(BF16)
    moves.send(0)


def share_kernel(moves, parts, out):
    rows = parts.shape[1]
    for core in range(CORE):
        total = parts[core].astype(F32)
        for n in range(1, Z * YH):
            total = total + parts[n * CORE + core].astype(F32)
        total = total * (1.0 / DP)
        for n in range(DP):
            out[n, core * rows : (core + 1) * rows] = total
    moves.send(0)


def layout_kernel(moves, shares, out):
    rows, lanes = shares.shape[1] // 2, shares.shape[2]
    cols = lanes // 2
    for core in range(CORE):
        here = slice(core * rows, (core + 1) * rows)
        for pair in range(DP // 2):
            left, right = shares[2 * pair, here], shares[2 * pair + 1, here]
            at = core * DP * cols + pair * lanes
            out[:rows, at : at + lanes] = jnp.concatenate([left[:, :cols], right[:, :cols]], 1)
            out[rows:, at : at + lanes] = jnp.concatenate([left[:, cols:], right[:, cols:]], 1)
    moves.send(0)


def on_device(sensor_feats, text_embeds, proj_weight, matches, log_scale, logit_bias):
    sensor = sensor_feats[0]
    texts = text_embeds[0]
    rows = sensor.shape[0]
    feat, width = proj_weight.shape
    loop_index = lax.axis_index("loop")
    place = loop_index.reshape(1)
    logit_scale = jnp.exp(log_scale)
    numbers = jnp.stack([log_scale, logit_bias])

    slot = {0: texts}
    slot[1], slot[-1] = shift_z(texts, -1), shift_z(texts, 1)

    sensor_yh = swap_yh(sensor)
    match = matches.reshape(1, rows)
    match_yh = swap_yh(match)
    up, down, _, _ = lax.optimization_barrier((slot[1], slot[-1], sensor_yh, match_yh))
    slot[2], slot[-2] = shift_z(up, -1), shift_z(down, 1)
    sensor_later, _ = lax.optimization_barrier((sensor, sensor_yh))
    sensors = [sensor, swap_core(sensor_later), sensor_yh, swap_core(sensor_yh)]
    match_both = swap_core(jnp.concatenate([match, match_yh], 0))
    match = [match, match_both[:1], match_yh, match_both[1:]]
    shapes = [((4 * rows, width), BF16), ((4 * rows, 1), F32), ((4 * rows, 1), F32)]
    image_emb, image_inv, match_rows = call(
        project_kernel,
        [jax.ShapeDtypeStruct(*s) for s in shapes],
        {},
        proj_weight, *sensors, *match,
        far=(0, 5),
        packed=range(1, 5),
        far_out=(1,),
        cuts={0: CUT},
    )
    up, down, _ = lax.optimization_barrier((slot[2], slot[-2], image_emb))
    slot[3], slot[-3], slot[4] = shift_z(up, -1), shift_z(down, 1), shift_z(down, 2)

    def pairs(keys, dtypes, acc):
        operands = [numbers, place, image_emb, match_rows, *(slot[k] for k in keys)]
        out = [jax.ShapeDtypeStruct((4 * rows, width), F32)]
        out += [jax.ShapeDtypeStruct((rows, width), d) for d in dtypes]
        aliases = {}
        if acc is not None:
            aliases = {len(operands): 0}
            operands.append(acc)
        kernel = functools.partial(pairs_kernel, keys, acc is None)
        return call(kernel, out, aliases, *operands, packed=range(4, 4 + len(keys)), far_out=range(1, len(out)))

    acc, text_0, text_1, text_m1, text_2, text_m2 = pairs((0, 1, -1, 2, -2), (F32, BF16, BF16, BF16, BF16), None)
    acc, text_3, text_m3 = pairs((3, -3), (BF16, BF16), acc)
    shapes = [((4 * rows, width), F32), ((4 * rows, 1), F32), ((4 * rows + 16, width // 2), BF16)]
    shapes += [((2 * rows, width // 2), BF16), ((4 * rows, rows), BF16)]
    acc, dot, packet, extra, last_grad = call(
        last_kernel,
        [jax.ShapeDtypeStruct(*s) for s in shapes],
        {5: 0},
        numbers, place, image_emb, match_rows, slot[4], acc,
        far_out=(3,),
    )

    got = swap_core(packet)
    weight_part, row_half = call(
        weight_kernel,
        [jax.ShapeDtypeStruct((DP, width // 16, feat), BF16), jax.ShapeDtypeStruct((2 * rows, width // 2), F32)],
        {},
        place, got, acc, dot, image_emb, image_inv, *sensors,
        far=(5,),
        far_out=(0, 1),
        sends=DP + 1,
    )
    last_grad, extra, text_1, text_m1, text_3, text_m3, _ = lax.optimization_barrier(
        (last_grad, extra, text_1, text_m1, text_3, text_m3, weight_part)
    )
    (text_4,) = call(
        last_text_kernel, [jax.ShapeDtypeStruct((rows, width), BF16)], {}, last_grad, image_emb, far_out=(0,)
    )
    shapes = [((rows, width), BF16), ((rows, width), F32)]
    row_send, row_keep = call(
        row_kernel,
        [jax.ShapeDtypeStruct(*s) for s in shapes],
        {},
        place, row_half, swap_core(extra), acc,
        far=(1,),
        far_out=(0, 1),
    )
    weight_part = lax.all_to_all(weight_part, "dp", 0, 0, tiled=True)

    per_loop = feat // LOOP
    block = (per_loop // 2, width // 8)
    (weight_chunks,) = call(
        chunk_kernel, [jax.ShapeDtypeStruct((LOOP,) + block, BF16)], {}, weight_part, far_out=(0,)
    )
    weight_part = lax.all_to_all(weight_chunks, "loop", 0, 0, tiled=True)
    (shares,) = call(
        share_kernel, [jax.ShapeDtypeStruct((DP, per_loop, width // 8), F32)], {}, weight_part, far_out=(0,)
    )

    from_below, from_above, far = shift_z(text_3, 1), shift_z(text_m3, -1), shift_z(text_4, 2)
    near_below, near_above = shift_z(text_1, 1), shift_z(text_m1, -1)
    from_below, from_above, far, near_below, near_above, row_send, _ = lax.optimization_barrier(
        (from_below, from_above, far, near_below, near_above, row_send, weight_chunks)
    )
    row_got = swap_yh(row_send)
    up = text_2.astype(F32) + from_below.astype(F32) + far.astype(F32)
    down = text_m2.astype(F32) + from_above.astype(F32)
    up, down = shift_z(up.astype(BF16), 2), shift_z(down.astype(BF16), -2)
    up, down, row_got, _ = lax.optimization_barrier((up, down, row_got, shares))
    shares = lax.all_to_all(shares, "dp", 0, 0, tiled=True)
    (weight_grad,) = call(
        layout_kernel, [jax.ShapeDtypeStruct((per_loop, width), F32)], {}, shares, far_out=(0,)
    )
    text_sum = text_0 + near_below.astype(F32) + near_above.astype(F32)
    text_sum = logit_scale * (text_sum + up.astype(F32) + down.astype(F32))
    text_wide = texts.astype(F32)
    text_inv = lax.rsqrt(jnp.sum(text_wide * text_wide, -1, keepdims=True) + 1e-06)
    text_unit = text_wide * text_inv
    text_grad = (text_sum - text_unit * jnp.sum(text_unit * text_sum, -1, keepdims=True)) * text_inv

    image_grad = row_keep + row_got.astype(F32)
    own_unit = image_emb[:rows].astype(F32)
    own_dot = jnp.sum(own_unit * image_grad, -1, keepdims=True)
    proj_grad = ((image_grad - own_unit * own_dot) * image_inv[:rows]).astype(BF16)
    sensor_grad = inner_rows(proj_grad, proj_weight).astype(BF16)
    return (sensor_grad[None], text_grad[None], weight_grad)


def solution(mesh):
    placed = (P("dp", "loop", None), P("dp", "loop", None), P(), P("dp", "loop"), P(), P())
    return jax.shard_map(
        on_device,
        mesh=mesh,
        in_specs=placed,
        out_specs=(P("dp", "loop", None), P("dp", "loop", None), P("loop", None)),
        check_vma=False,
    )
```

```python
import functools

import jax
import jax.numpy as jnp
from jax import lax
from jax.experimental import pallas as pl
from jax.experimental.pallas import tpu as pltpu
from jax.sharding import PartitionSpec as P

Z, YH, CORE = 8, 2, 2
LOOP = Z * YH * CORE
DP = 8
CUT = 640
BF16 = jnp.bfloat16
F32 = jnp.float32
VMEM = pl.BlockSpec(memory_space=pltpu.VMEM)
HBM = pl.BlockSpec(memory_space=pltpu.HBM)
SMEM = pl.BlockSpec(memory_space=pltpu.SMEM)


def route(move):
    pairs = []
    for z in range(Z):
        for y in range(YH):
            for c in range(CORE):
                to_z, to_y, to_c = move(z, y, c)
                source = (z * YH + y) * CORE + c
                pairs.append((source, ((to_z % Z) * YH + to_y) * CORE + to_c))
    return pairs


def shift_z(block, distance):
    return lax.ppermute(block, "loop", route(lambda z, y, c: (z + (1 - 2 * c) * distance, y, c)))


def swap_core(block):
    return lax.ppermute(block, "loop", route(lambda z, y, c: (z, y, 1 - c)))


def swap_yh(block):
    return lax.ppermute(block, "loop", route(lambda z, y, c: (z, 1 - y, c)))


def inner_rows(left, right):
    return lax.dot_general(left, right, (((1,), (1,)), ((), ())), preferred_element_type=F32)


def inner_cols(left, right):
    return lax.dot_general(left, right, (((0,), (0,)), ((), ())), preferred_element_type=F32)


class Moves:
    def __init__(self, base, sems, loads, held, outs, pack):
        self.base = base
        self.sems, self.loads, self.held, self.outs, self.pack, self.sent = sems, loads, held, outs, pack, []

    def need(self, n):
        self.loads[n].wait()

    def send(self, n, part=None):
        source, target = self.held[n], self.outs[n]
        if part is not None:
            source, target = source.at[part], target.at[part]
        copy = pltpu.make_async_copy(source, target, self.sems.at[self.base + len(self.sent)])
        copy.start()
        self.sent.append(copy)


def call(kernel, out, aliases, *operands, far=(), packed=(), far_out=(), sends=None, cuts=()):
    cuts = dict(cuts)
    far, packed, far_out, total = list(far), list(packed), list(far_out), len(operands)
    sends = len(far_out) if sends is None else sends

    def body(*refs):
        ins, outs, scratch = refs[:total], refs[total : total + len(out)], refs[total + len(out) :]
        held = dict(zip(far, scratch[: len(far)]))
        held_out = dict(zip(far_out, scratch[len(far) : len(far) + len(far_out)]))
        for m, n in enumerate(packed):
            height = operands[n].shape[0]
            held[n] = scratch[-2].at[pl.ds(m * height, height)]
        whole = [(m, n) for m, n in enumerate(in_hbm) if n not in cuts]
        loads = {n: pltpu.make_async_copy(ins[n], held[n], scratch[-1].at[m]) for m, n in whole}
        for n, cut in cuts.items():
            for m, part in enumerate((pl.ds(0, cut), pl.ds(cut, operands[n].shape[0] - cut))):
                sem = scratch[-1].at[len(in_hbm) + sends] if m else scratch[-1].at[far.index(n)]
                loads[n, m] = pltpu.make_async_copy(ins[n].at[part], held[n].at[part], sem)
        for load in loads.values():
            load.start()
        moves = Moves(len(in_hbm), scratch[-1], loads, held_out, outs, scratch[-2] if packed else None)
        kernel(moves, *(held.get(n, ref) for n, ref in enumerate(ins)), *(held_out.get(n, ref) for n, ref in enumerate(outs)))
        for copy in moves.sent:
            copy.wait()

    in_hbm = far + packed
    in_specs = [SMEM if o.ndim == 1 else HBM if n in in_hbm else VMEM for n, o in enumerate(operands)]
    scratch = [pltpu.VMEM(operands[n].shape, operands[n].dtype) for n in far]
    scratch += [pltpu.VMEM(out[n].shape, out[n].dtype) for n in far_out]
    if packed:
        height, width = operands[packed[0]].shape
        scratch.append(pltpu.VMEM((len(packed) * height, width), operands[packed[0]].dtype))
    scratch.append(pltpu.SemaphoreType.DMA((len(in_hbm) + sends + 1,)))
    operands = [pltpu.with_memory_space_constraint(o, pltpu.HBM) if n in in_hbm else o for n, o in enumerate(operands)]
    return pl.pallas_call(
        body,
        out_shape=[pltpu.HBM(o.shape, o.dtype) if n in far_out else o for n, o in enumerate(out)],
        in_specs=in_specs,
        out_specs=[HBM if n in far_out else VMEM for n in range(len(out))],
        scratch_shapes=scratch,
        input_output_aliases=aliases,
        cost_estimate=pl.CostEstimate(flops=1, bytes_accessed=1, transcendentals=0),
        compiler_params=pltpu.CompilerParams(vmem_limit_bytes=20 << 20),
    )(*operands)


def scale_of(numbers):
    return jnp.exp(jnp.full((1, 128), numbers[0], F32))[:, 0:1]


def block_grads(numbers, columns, image_emb, match, text):
    wide = text.astype(F32)
    inv = lax.rsqrt(jnp.sum(wide * wide, -1, keepdims=True) + 1e-06)
    emb = (wide * inv).astype(BF16)
    logits = scale_of(numbers) * inner_rows(image_emb, emb) + numbers[1]
    positive = (match == columns).astype(F32)
    return emb, (jax.nn.sigmoid(logits) - positive).astype(BF16)


def columns_of(place, key, rows):
    step = (1 - 2 * (place[0] & 1)) * (YH * CORE)
    start = (place[0] + key * step + LOOP) % LOOP * rows
    return (lax.broadcasted_iota(jnp.int32, (1, rows), 1) + start).astype(F32)


def pairs_kernel(keys, first, moves, numbers, place, image_emb, match, *refs):
    count = len(keys)
    texts, refs = refs[:count], refs[count:]
    if not first:
        acc_in, refs = refs[0], refs[1:]
    acc_out, text_out = refs[0], refs[1:]
    image = image_emb[...]
    rows = texts[0].shape[0]
    columns = jnp.concatenate([columns_of(place, key, rows) for key in keys], 1)
    for n in range(count):
        moves.need(4 + n)
    emb, grad = block_grads(numbers, columns, image, match[...], moves.pack[...])
    text_part = scale_of(numbers) * inner_cols(grad, image)
    for n in range(count):
        text_out[n][...] = text_part[n * rows : (n + 1) * rows].astype(text_out[n].dtype)
        moves.send(1 + n)
    part = jnp.dot(grad, emb, preferred_element_type=F32)
    acc_out[...] = part if first else acc_in[...] + part


def project_kernel(moves, proj_weight, own, core, yh, both, *refs):
    matches, (emb, inv_out, match_out) = refs[:4], refs[4:]
    rows, cut = own.shape[0], CUT
    for n in range(4):
        moves.need(1 + n)
    sensor = moves.pack[...]
    moves.need((0, 0))
    projected = jnp.dot(sensor[:, :cut], proj_weight[:cut], preferred_element_type=F32)
    moves.need((0, 1))
    projected = projected + jnp.dot(sensor[:, cut:], proj_weight[cut:], preferred_element_type=F32)
    inv = lax.rsqrt(jnp.sum(projected * projected, -1, keepdims=True) + 1e-06)
    emb[...] = (projected * inv).astype(BF16)
    inv_out[...] = inv
    moves.send(1)
    moves.need(5)
    for n in range(4):
        match = jnp.broadcast_to(matches[n][...].astype(F32), (rows, rows))
        match_out[n * rows : (n + 1) * rows, :] = match.T[:, 0:1]


def last_kernel(moves, numbers, place, image_emb, match, text, acc_in, acc_out, dot_out, packet, grad_out):
    columns = columns_of(place, 4, text.shape[0])
    emb, grad = block_grads(numbers, columns, image_emb[...], match[...], text[...])
    grad_out[...] = grad
    acc = scale_of(numbers) * (acc_in[...] + jnp.dot(grad, emb, preferred_element_type=F32))
    acc_out[...] = acc
    dot = jnp.sum(image_emb[...].astype(F32) * acc, -1, keepdims=True)
    dot_out[...] = dot
    rows, width = acc.shape
    half, block = width // 2, rows // 4
    core = place[0] & 1
    other = pl.ds(pl.multiple_of((1 - core) * half, half), half)
    packet[:rows, :] = acc_out[:, other].astype(BF16)
    lines = []
    for slot in range(4):
        mine = slice(slot * block, (slot + 1) * block)
        flat = jnp.broadcast_to(dot[mine], (block, 128)).T[0:1, :]
        top = flat.astype(BF16).astype(F32)
        lines.append(jnp.concatenate([top, flat - top, jnp.zeros((1, half - 256), F32)], 1))
    lines.append(jnp.zeros((packet.shape[0] - rows - 4, half), F32))
    packet[rows:, :] = jnp.concatenate(lines, 0).astype(BF16)


def last_text_kernel(moves, numbers, grad, image_emb, out):
    out[...] = (scale_of(numbers) * inner_cols(grad[...], image_emb[...])).astype(out.dtype)
    moves.send(0)


def weight_kernel(moves, place, got, acc, dot, image_emb, inv, own_rows, core_rows, yh_rows, both_rows, weight, row_half):
    rows, width = acc.shape
    half, quarter, block = width // 2, width // 4, rows // 4
    own = pl.ds(pl.multiple_of((place[0] & 1) * half, half), half)
    digits = got[rows:, :256].astype(F32)
    moves.need(5)
    projs = []
    for slot in range(4):
        mine = slice(slot * block, (slot + 1) * block)
        theirs = slice((slot ^ 1) * block, ((slot ^ 1) + 1) * block)
        kept = acc[mine, own] + got[theirs, :].astype(F32)
        if slot in (0, 2):
            row_half[slot // 2 * block : (slot // 2 + 1) * block, :] = kept
            if slot == 2:
                moves.send(1)
        line = digits[slot ^ 1 : (slot ^ 1) + 1, :]
        other_dot = jnp.broadcast_to(line[:, :128] + line[:, 128:], (block, 128)).T[:, 0:1]
        unit = image_emb[mine, own].astype(F32)
        projs.append(((kept - unit * (dot[mine, :] + other_dot)) * inv[mine, :]).astype(BF16))
    proj = jnp.concatenate(projs, 0)
    sensor = jnp.concatenate([own_rows[...], core_rows[...], yh_rows[...], both_rows[...]], 0)
    chunk = weight.shape[1]
    for side in range(2):
        product = inner_cols(proj[:, side * quarter : (side + 1) * quarter], sensor).astype(BF16)
        for m in range(quarter // chunk):
            at = side * (quarter // chunk) + m
            weight[at] = product[m * chunk : (m + 1) * chunk]
            moves.send(0, at)


def extra_kernel(moves, place, acc, extra):
    rows, width = acc.shape
    half, block = width // 2, rows // 4
    own = pl.ds(pl.multiple_of((place[0] & 1) * half, half), half)
    for n, slot in enumerate((1, 3)):
        extra[n * block : (n + 1) * block, :] = acc[slot * block : (slot + 1) * block, own].astype(BF16)


def row_kernel(moves, place, row_half, extra, acc, row_send, row_keep):
    rows, width = acc.shape
    half, block = width // 2, rows // 4
    core = place[0] & 1
    own = pl.ds(pl.multiple_of(core * half, half), half)
    other = pl.ds(pl.multiple_of((1 - core) * half, half), half)
    moves.need(1)
    for n, target in enumerate((row_keep, row_send)):
        here = slice(n * block, (n + 1) * block)
        target[:, own] = row_half[here, :].astype(target.dtype)
        rest = extra[here, :].astype(F32)
        target[:, other] = (acc[2 * n * block : (2 * n + 1) * block, other] + rest).astype(target.dtype)
        moves.send(1 - n)


def sums_kernel(moves, text_2, below, far, text_m2, above, up, down):
    for n in range(3):
        moves.need(n)
    up[...] = (text_2[...].astype(F32) + below[...].astype(F32) + far[...].astype(F32)).astype(BF16)
    moves.send(0)
    moves.need(3)
    moves.need(4)
    down[...] = (text_m2[...].astype(F32) + above[...].astype(F32)).astype(BF16)
    moves.send(1)


def text_kernel(moves, text, own, near_below, near_above, up, down, out):
    for n in range(6):
        moves.need(n)
    total = own[...] + near_below[...].astype(F32) + near_above[...].astype(F32)
    total = total + up[...].astype(F32) + down[...].astype(F32)
    wide = text[...].astype(F32)
    inv = lax.rsqrt(jnp.sum(wide * wide, -1, keepdims=True) + 1e-06)
    unit = wide * inv
    out[...] = (total - unit * jnp.sum(unit * total, -1, keepdims=True)) * inv
    moves.send(0)


def sensor_kernel(moves, row_keep, row_got, inv, proj_weight, image_emb, out):
    rows = row_keep.shape[0]
    for n in range(3):
        moves.need(n)
    image_grad = row_keep[...] + row_got[...].astype(F32)
    unit = image_emb[:rows, :].astype(F32)
    dot = jnp.sum(unit * image_grad, -1, keepdims=True)
    proj_grad = ((image_grad - unit * dot) * inv[:rows, :]).astype(BF16)
    moves.need(3)
    out[...] = inner_rows(proj_grad, proj_weight[...]).astype(BF16)
    moves.send(0)


def chunk_kernel(moves, parts, out):
    total = parts[0].astype(F32)
    for n in range(1, parts.shape[0]):
        total = total + parts[n].astype(F32)
    turned = total.T
    count, rows, lanes = out.shape
    for n in range(count):
        at = 2 * rows * n
        out[n] = jnp.concatenate([turned[at : at + rows], turned[at + rows : at + 2 * rows]], 1).astype(BF16)
    moves.send(0)


def share_kernel(moves, parts, out):
    rows = parts.shape[1]
    for core in range(CORE):
        total = parts[core].astype(F32)
        for n in range(1, Z * YH):
            total = total + parts[n * CORE + core].astype(F32)
        total = total * (1.0 / DP)
        for n in range(DP):
            out[n, core * rows : (core + 1) * rows] = total
    moves.send(0)


def layout_kernel(moves, shares, out):
    rows, lanes = shares.shape[1] // 2, shares.shape[2]
    cols = lanes // 2
    for core in range(CORE):
        here = slice(core * rows, (core + 1) * rows)
        for pair in range(DP // 2):
            left, right = shares[2 * pair, here], shares[2 * pair + 1, here]
            at = core * DP * cols + pair * lanes
            out[:rows, at : at + lanes] = jnp.concatenate([left[:, :cols], right[:, :cols]], 1)
            out[rows:, at : at + lanes] = jnp.concatenate([left[:, cols:], right[:, cols:]], 1)
    moves.send(0)


def on_device(sensor_feats, text_embeds, proj_weight, matches, log_scale, logit_bias):
    sensor = sensor_feats[0]
    texts = text_embeds[0]
    rows = sensor.shape[0]
    feat, width = proj_weight.shape
    loop_index = lax.axis_index("loop")
    place = loop_index.reshape(1)
    numbers = jnp.stack([log_scale, logit_bias])

    slot = {0: texts}
    slot[1], slot[-1] = shift_z(texts, -1), shift_z(texts, 1)

    sensor_yh = swap_yh(sensor)
    match = matches.reshape(1, rows)
    match_yh = swap_yh(match)
    up, down, _, _ = lax.optimization_barrier((slot[1], slot[-1], sensor_yh, match_yh))
    slot[2], slot[-2] = shift_z(up, -1), shift_z(down, 1)
    sensor_later, _ = lax.optimization_barrier((sensor, sensor_yh))
    sensors = [sensor, swap_core(sensor_later), sensor_yh, swap_core(sensor_yh)]
    match_both = swap_core(jnp.concatenate([match, match_yh], 0))
    match = [match, match_both[:1], match_yh, match_both[1:]]
    shapes = [((4 * rows, width), BF16), ((4 * rows, 1), F32), ((4 * rows, 1), F32)]
    image_emb, image_inv, match_rows = call(
        project_kernel,
        [jax.ShapeDtypeStruct(*s) for s in shapes],
        {},
        proj_weight, *sensors, *match,
        far=(0, 5),
        packed=range(1, 5),
        far_out=(1,),
        cuts={0: CUT},
    )
    up, down, _ = lax.optimization_barrier((slot[2], slot[-2], image_emb))
    slot[3], slot[-3], slot[4] = shift_z(up, -1), shift_z(down, 1), shift_z(down, 2)

    def pairs(keys, dtypes, acc):
        operands = [numbers, place, image_emb, match_rows, *(slot[k] for k in keys)]
        out = [jax.ShapeDtypeStruct((4 * rows, width), F32)]
        out += [jax.ShapeDtypeStruct((rows, width), d) for d in dtypes]
        aliases = {}
        if acc is not None:
            aliases = {len(operands): 0}
            operands.append(acc)
        kernel = functools.partial(pairs_kernel, keys, acc is None)
        return call(kernel, out, aliases, *operands, packed=range(4, 4 + len(keys)), far_out=range(1, len(out)))

    acc, text_0, text_1, text_m1, text_2, text_m2 = pairs((0, 1, -1, 2, -2), (F32, BF16, BF16, BF16, BF16), None)
    acc, text_3, text_m3 = pairs((3, -3), (BF16, BF16), acc)
    shapes = [((4 * rows, width), F32), ((4 * rows, 1), F32), ((4 * rows + 16, width // 2), BF16)]
    shapes.append(((4 * rows, rows), BF16))
    acc, dot, packet, last_grad = call(
        last_kernel,
        [jax.ShapeDtypeStruct(*s) for s in shapes],
        {5: 0},
        numbers, place, image_emb, match_rows, slot[4], acc,
    )

    got = swap_core(packet)
    weight_part, row_half = call(
        weight_kernel,
        [jax.ShapeDtypeStruct((DP, width // 16, feat), BF16), jax.ShapeDtypeStruct((2 * rows, width // 2), F32)],
        {},
        place, got, acc, dot, image_emb, image_inv, *sensors,
        far=(5,),
        far_out=(0, 1),
        sends=DP + 1,
    )
    last_grad, acc, text_1, text_m1, text_3, text_m3, _ = lax.optimization_barrier(
        (last_grad, acc, text_1, text_m1, text_3, text_m3, weight_part)
    )
    (extra,) = call(extra_kernel, [jax.ShapeDtypeStruct((2 * rows, width // 2), BF16)], {}, place, acc)
    (text_4,) = call(
        last_text_kernel, [jax.ShapeDtypeStruct((rows, width), BF16)], {}, numbers, last_grad, image_emb, far_out=(0,)
    )
    shapes = [((rows, width), BF16), ((rows, width), F32)]
    row_send, row_keep = call(
        row_kernel,
        [jax.ShapeDtypeStruct(*s) for s in shapes],
        {},
        place, row_half, swap_core(extra), acc,
        far=(1,),
        far_out=(0, 1),
    )
    weight_part = lax.all_to_all(weight_part, "dp", 0, 0, tiled=True)

    per_loop = feat // LOOP
    block = (per_loop // 2, width // 8)
    (weight_chunks,) = call(
        chunk_kernel, [jax.ShapeDtypeStruct((LOOP,) + block, BF16)], {}, weight_part, far_out=(0,)
    )
    weight_part = lax.all_to_all(weight_chunks, "loop", 0, 0, tiled=True)
    (shares,) = call(
        share_kernel, [jax.ShapeDtypeStruct((DP, per_loop, width // 8), F32)], {}, weight_part, far_out=(0,)
    )

    from_below, from_above, far = shift_z(text_3, 1), shift_z(text_m3, -1), shift_z(text_4, 2)
    near_below, near_above = shift_z(text_1, 1), shift_z(text_m1, -1)
    row_got = swap_yh(row_send)
    from_below, from_above, far, near_below, near_above, row_got, _ = lax.optimization_barrier(
        (from_below, from_above, far, near_below, near_above, row_got, weight_chunks)
    )
    up, down = call(
        sums_kernel,
        [jax.ShapeDtypeStruct((rows, width), BF16)] * 2,
        {},
        text_2, from_below, far, text_m2, from_above,
        far=range(5),
        far_out=range(2),
    )
    up, down = shift_z(up, 2), shift_z(down, -2)

    (sensor_grad,) = call(
        sensor_kernel,
        [jax.ShapeDtypeStruct((rows, feat), BF16)],
        {},
        row_keep, row_got, image_inv, proj_weight, image_emb,
        far=range(4),
        far_out=(0,),
    )
    shares, _ = lax.optimization_barrier((shares, sensor_grad))
    up, down, _ = lax.optimization_barrier((up, down, shares))
    shares = lax.all_to_all(shares, "dp", 0, 0, tiled=True)
    (weight_grad,) = call(
        layout_kernel, [jax.ShapeDtypeStruct((per_loop, width), F32)], {}, shares, far_out=(0,)
    )
    (text_grad,) = call(
        text_kernel,
        [jax.ShapeDtypeStruct((rows, width), F32)],
        {},
        texts, text_0, near_below, near_above, up, down,
        far=range(6),
        far_out=(0,),
    )
    return (sensor_grad[None], text_grad[None], weight_grad)


def solution(mesh):
    placed = (P("dp", "loop", None), P("dp", "loop", None), P(), P("dp", "loop"), P(), P())
    return jax.shard_map(
        on_device,
        mesh=mesh,
        in_specs=placed,
        out_specs=(P("dp", "loop", None), P("dp", "loop", None), P("loop", None)),
        check_vma=False,
    )
```

```python
import functools

import jax
import jax.numpy as jnp
from jax import lax
from jax.experimental import pallas as pl
from jax.experimental.pallas import tpu as pltpu
from jax.sharding import PartitionSpec as P

Z, YH, CORE = 8, 2, 2
LOOP = Z * YH * CORE
DP = 8
CUT = 640
BF16 = jnp.bfloat16
F32 = jnp.float32
VMEM = pl.BlockSpec(memory_space=pltpu.VMEM)
HBM = pl.BlockSpec(memory_space=pltpu.HBM)
SMEM = pl.BlockSpec(memory_space=pltpu.SMEM)


def route(move):
    pairs = []
    for z in range(Z):
        for y in range(YH):
            for c in range(CORE):
                to_z, to_y, to_c = move(z, y, c)
                source = (z * YH + y) * CORE + c
                pairs.append((source, ((to_z % Z) * YH + to_y) * CORE + to_c))
    return pairs


def shift_z(block, distance):
    return lax.ppermute(block, "loop", route(lambda z, y, c: (z + (1 - 2 * c) * distance, y, c)))


def swap_core(block):
    return lax.ppermute(block, "loop", route(lambda z, y, c: (z, y, 1 - c)))


def swap_yh(block):
    return lax.ppermute(block, "loop", route(lambda z, y, c: (z, 1 - y, c)))


def inner_rows(left, right):
    return lax.dot_general(left, right, (((1,), (1,)), ((), ())), preferred_element_type=F32)


def inner_cols(left, right):
    return lax.dot_general(left, right, (((0,), (0,)), ((), ())), preferred_element_type=F32)


class Moves:
    def __init__(self, base, sems, loads, held, outs, pack):
        self.base = base
        self.sems, self.loads, self.held, self.outs, self.pack, self.sent = sems, loads, held, outs, pack, []

    def need(self, n):
        self.loads[n].wait()

    def push(self, source, n, part):
        copy = pltpu.make_async_copy(source, self.outs[n].at[part], self.sems.at[self.base + len(self.sent)])
        copy.start()
        self.sent.append(copy)

    def send(self, n, part=None):
        source, target = self.held[n], self.outs[n]
        if part is not None:
            source, target = source.at[part], target.at[part]
        copy = pltpu.make_async_copy(source, target, self.sems.at[self.base + len(self.sent)])
        copy.start()
        self.sent.append(copy)


def call(kernel, out, aliases, *operands, far=(), packed=(), far_out=(), pushed=(), sends=None, cuts=()):
    cuts = dict(cuts)
    far, packed, far_out, total = list(far), list(packed), list(far_out), len(operands)
    sends = len(far_out) if sends is None else sends

    def body(*refs):
        ins, outs, scratch = refs[:total], refs[total : total + len(out)], refs[total + len(out) :]
        held = dict(zip(far, scratch[: len(far)]))
        held_out = dict(zip(far_out, scratch[len(far) : len(far) + len(far_out)]))
        for m, n in enumerate(packed):
            height = operands[n].shape[0]
            held[n] = scratch[-2].at[pl.ds(m * height, height)]
        whole = [(m, n) for m, n in enumerate(in_hbm) if n not in cuts]
        loads = {n: pltpu.make_async_copy(ins[n], held[n], scratch[-1].at[m]) for m, n in whole}
        for n, cut in cuts.items():
            for m, part in enumerate((pl.ds(0, cut), pl.ds(cut, operands[n].shape[0] - cut))):
                sem = scratch[-1].at[len(in_hbm) + sends] if m else scratch[-1].at[far.index(n)]
                loads[n, m] = pltpu.make_async_copy(ins[n].at[part], held[n].at[part], sem)
        for load in loads.values():
            load.start()
        moves = Moves(len(in_hbm), scratch[-1], loads, held_out, outs, scratch[-2] if packed else None)
        kernel(moves, *(held.get(n, ref) for n, ref in enumerate(ins)), *(held_out.get(n, ref) for n, ref in enumerate(outs)))
        for copy in moves.sent:
            copy.wait()

    in_hbm, out_hbm = far + packed, far_out + list(pushed)
    in_specs = [SMEM if o.ndim == 1 else HBM if n in in_hbm else VMEM for n, o in enumerate(operands)]
    scratch = [pltpu.VMEM(operands[n].shape, operands[n].dtype) for n in far]
    scratch += [pltpu.VMEM(out[n].shape, out[n].dtype) for n in far_out]
    if packed:
        height, width = operands[packed[0]].shape
        scratch.append(pltpu.VMEM((len(packed) * height, width), operands[packed[0]].dtype))
    scratch.append(pltpu.SemaphoreType.DMA((len(in_hbm) + sends + 1,)))
    operands = [pltpu.with_memory_space_constraint(o, pltpu.HBM) if n in in_hbm else o for n, o in enumerate(operands)]
    return pl.pallas_call(
        body,
        out_shape=[pltpu.HBM(o.shape, o.dtype) if n in out_hbm else o for n, o in enumerate(out)],
        in_specs=in_specs,
        out_specs=[HBM if n in out_hbm else VMEM for n in range(len(out))],
        scratch_shapes=scratch,
        input_output_aliases=aliases,
        cost_estimate=pl.CostEstimate(flops=1, bytes_accessed=1, transcendentals=0),
        compiler_params=pltpu.CompilerParams(vmem_limit_bytes=20 << 20),
    )(*operands)


def scale_of(numbers):
    return jnp.exp(jnp.full((1, 128), numbers[0], F32))[:, 0:1]


def block_grads(numbers, columns, image_emb, match, text):
    wide = text.astype(F32)
    inv = lax.rsqrt(jnp.sum(wide * wide, -1, keepdims=True) + 1e-06)
    emb = (wide * inv).astype(BF16)
    logits = scale_of(numbers) * inner_rows(image_emb, emb) + numbers[1]
    positive = (match == columns).astype(F32)
    return emb, (jax.nn.sigmoid(logits) - positive).astype(BF16)


def columns_of(place, key, rows):
    step = (1 - 2 * (place[0] & 1)) * (YH * CORE)
    start = (place[0] + key * step + LOOP) % LOOP * rows
    return (lax.broadcasted_iota(jnp.int32, (1, rows), 1) + start).astype(F32)


def pairs_body(keys, moves, first, numbers, place, image_emb, match, texts, acc_in, acc_out, text_out):
    count = len(keys)
    image = image_emb[...]
    rows = texts[0].shape[0]
    columns = jnp.concatenate([columns_of(place, key, rows) for key in keys], 1)
    for n in range(count):
        moves.need(first + n)
    emb, grad = block_grads(numbers, columns, image, match[...], moves.pack[...])
    text_part = scale_of(numbers) * inner_cols(grad, image)
    shift = 2 if acc_in is None else 1
    for n in range(count):
        text_out[n][...] = text_part[n * rows : (n + 1) * rows].astype(text_out[n].dtype)
        moves.send(shift + n)
    part = jnp.dot(grad, emb, preferred_element_type=F32)
    acc_out[...] = part if acc_in is None else acc_in[...] + part


def pairs_kernel(keys, moves, numbers, place, image_emb, match, *refs):
    count = len(keys)
    pairs_body(keys, moves, 4, numbers, place, image_emb, match, refs[:count], refs[count], refs[count + 1], refs[count + 2 :])


def project_kernel(moves, proj_weight, own, core, yh, both, emb, inv_out):
    for n in range(4):
        moves.need(1 + n)
    sensor = moves.pack[...]
    moves.need((0, 0))
    projected = jnp.dot(sensor[:, :CUT], proj_weight[:CUT], preferred_element_type=F32)
    moves.need((0, 1))
    projected = projected + jnp.dot(sensor[:, CUT:], proj_weight[CUT:], preferred_element_type=F32)
    inv = lax.rsqrt(jnp.sum(projected * projected, -1, keepdims=True) + 1e-06)
    inv_out[...] = inv
    moves.send(1)
    emb[...] = (projected * inv).astype(BF16)


def first_pairs_kernel(keys, moves, numbers, place, image_emb, own, core, yh, both, *refs):
    texts, match, outs = refs[: len(keys)], refs[len(keys)], refs[len(keys) + 1 :]
    block = own.shape[1]
    for n, line in enumerate((own, core, yh, both)):
        turned = jnp.broadcast_to(line[...].astype(F32), (128, block)).T
        match[n * block : (n + 1) * block, :] = turned[:, 0:1]
    pairs_body(keys, moves, 7, numbers, place, image_emb, match, texts, None, outs[0], outs[1:])


def last_kernel(moves, numbers, place, image_emb, match, text, acc_in, acc_out, dot_out, packet, grad_out):
    columns = columns_of(place, 4, text.shape[0])
    emb, grad = block_grads(numbers, columns, image_emb[...], match[...], text[...])
    grad_out[...] = grad
    acc = scale_of(numbers) * (acc_in[...] + jnp.dot(grad, emb, preferred_element_type=F32))
    acc_out[...] = acc
    dot = jnp.sum(image_emb[...].astype(F32) * acc, -1, keepdims=True)
    dot_out[...] = dot
    rows, width = acc.shape
    half, block = width // 2, rows // 4
    core = place[0] & 1
    other = pl.ds(pl.multiple_of((1 - core) * half, half), half)
    packet[:rows, :] = acc_out[:, other].astype(BF16)
    lines = []
    for slot in range(4):
        mine = slice(slot * block, (slot + 1) * block)
        flat = jnp.broadcast_to(dot[mine], (block, 128)).T[0:1, :]
        top = flat.astype(BF16).astype(F32)
        lines.append(jnp.concatenate([top, flat - top, jnp.zeros((1, half - 256), F32)], 1))
    lines.append(jnp.zeros((packet.shape[0] - rows - 4, half), F32))
    packet[rows:, :] = jnp.concatenate(lines, 0).astype(BF16)


def last_text_kernel(moves, numbers, grad, image_emb, out):
    out[...] = (scale_of(numbers) * inner_cols(grad[...], image_emb[...])).astype(out.dtype)
    moves.send(0)


def weight_kernel(moves, place, got, acc, dot, image_emb, inv, own_rows, core_rows, yh_rows, both_rows, weight, row_half, row_other, extra):
    rows, width = acc.shape
    half, quarter, block = width // 2, width // 4, rows // 4
    core = place[0] & 1
    own = pl.ds(pl.multiple_of(core * half, half), half)
    other = pl.ds(pl.multiple_of((1 - core) * half, half), half)
    for n in range(2):
        here = pl.ds(n * block, block)
        moves.push(acc.at[pl.ds((2 * n + 1) * block, block), own], 3, here)
        moves.push(acc.at[pl.ds(2 * n * block, block), other], 2, here)
    digits = got[rows:, :256].astype(F32)
    moves.need(5)
    projs = []
    for slot in range(4):
        mine = slice(slot * block, (slot + 1) * block)
        theirs = slice((slot ^ 1) * block, ((slot ^ 1) + 1) * block)
        kept = acc[mine, own] + got[theirs, :].astype(F32)
        if slot in (0, 2):
            row_half[slot // 2 * block : (slot // 2 + 1) * block, :] = kept
            if slot == 2:
                moves.send(1)
        line = digits[slot ^ 1 : (slot ^ 1) + 1, :]
        other_dot = jnp.broadcast_to(line[:, :128] + line[:, 128:], (block, 128)).T[:, 0:1]
        unit = image_emb[mine, own].astype(F32)
        projs.append(((kept - unit * (dot[mine, :] + other_dot)) * inv[mine, :]).astype(BF16))
    proj = jnp.concatenate(projs, 0)
    sensor = jnp.concatenate([own_rows[...], core_rows[...], yh_rows[...], both_rows[...]], 0)
    chunk = weight.shape[1]
    for side in range(2):
        product = inner_cols(proj[:, side * quarter : (side + 1) * quarter], sensor).astype(BF16)
        for m in range(quarter // chunk):
            at = side * (quarter // chunk) + m
            weight[at] = product[m * chunk : (m + 1) * chunk]
            moves.send(0, at)


def row_kernel(moves, place, row_half, row_other, extra, row_send, row_keep):
    block, half = row_half.shape[0] // 2, row_half.shape[1]
    core = place[0] & 1
    own = pl.ds(pl.multiple_of(core * half, half), half)
    other = pl.ds(pl.multiple_of((1 - core) * half, half), half)
    for n in range(3):
        moves.need(1 + n)
    for n, target in ((1, row_send), (0, row_keep)):
        here = slice(n * block, (n + 1) * block)
        target[:, own] = row_half[here, :].astype(target.dtype)
        target[:, other] = (row_other[here, :] + extra[here, :]).astype(target.dtype)
        moves.send(1 - n)


def sums_kernel(moves, text_2, below, far, text_m2, above, up, down):
    for n in range(3):
        moves.need(n)
    up[...] = (text_2[...].astype(F32) + below[...].astype(F32) + far[...].astype(F32)).astype(BF16)
    moves.send(0)
    moves.need(3)
    moves.need(4)
    down[...] = (text_m2[...].astype(F32) + above[...].astype(F32)).astype(BF16)
    moves.send(1)


def text_kernel(moves, text, own, near_below, near_above, up, down, out):
    for n in range(6):
        moves.need(n)
    total = own[...] + near_below[...].astype(F32) + near_above[...].astype(F32)
    total = total + up[...].astype(F32) + down[...].astype(F32)
    wide = text[...].astype(F32)
    inv = lax.rsqrt(jnp.sum(wide * wide, -1, keepdims=True) + 1e-06)
    unit = wide * inv
    out[...] = (total - unit * jnp.sum(unit * total, -1, keepdims=True)) * inv
    moves.send(0)


def sensor_kernel(moves, row_keep, row_got, inv, proj_weight, image_emb, out):
    rows = row_keep.shape[0]
    for n in range(3):
        moves.need(n)
    image_grad = row_keep[...] + row_got[...].astype(F32)
    unit = image_emb[:rows, :].astype(F32)
    dot = jnp.sum(unit * image_grad, -1, keepdims=True)
    proj_grad = ((image_grad - unit * dot) * inv[:rows, :]).astype(BF16)
    moves.need(3)
    out[...] = inner_rows(proj_grad, proj_weight[...]).astype(BF16)
    moves.send(0)


def chunk_kernel(moves, parts, out):
    total = parts[0].astype(F32)
    for n in range(1, parts.shape[0]):
        total = total + parts[n].astype(F32)
    turned = total.T
    count, rows, lanes = out.shape
    for n in range(count):
        at = 2 * rows * n
        out[n] = jnp.concatenate([turned[at : at + rows], turned[at + rows : at + 2 * rows]], 1).astype(BF16)
    moves.send(0)


def share_kernel(moves, parts, out):
    rows = parts.shape[1]
    for core in range(CORE):
        total = parts[core].astype(F32)
        for n in range(1, Z * YH):
            total = total + parts[n * CORE + core].astype(F32)
        total = total * (1.0 / DP)
        for n in range(DP):
            out[n, core * rows : (core + 1) * rows] = total
    moves.send(0)


def layout_kernel(moves, shares, out):
    rows, lanes = shares.shape[1] // 2, shares.shape[2]
    cols = lanes // 2
    for core in range(CORE):
        here = slice(core * rows, (core + 1) * rows)
        for pair in range(DP // 2):
            left, right = shares[2 * pair, here], shares[2 * pair + 1, here]
            at = core * DP * cols + pair * lanes
            out[:rows, at : at + lanes] = jnp.concatenate([left[:, :cols], right[:, :cols]], 1)
            out[rows:, at : at + lanes] = jnp.concatenate([left[:, cols:], right[:, cols:]], 1)
    moves.send(0)


def on_device(sensor_feats, text_embeds, proj_weight, matches, log_scale, logit_bias):
    sensor = sensor_feats[0]
    texts = text_embeds[0]
    rows = sensor.shape[0]
    feat, width = proj_weight.shape
    loop_index = lax.axis_index("loop")
    place = loop_index.reshape(1)
    numbers = jnp.stack([log_scale, logit_bias])

    slot = {0: texts}
    slot[1], slot[-1] = shift_z(texts, -1), shift_z(texts, 1)

    sensor_yh = swap_yh(sensor)
    match = matches.reshape(1, rows)
    match_yh = swap_yh(match)
    up, down, _, _ = lax.optimization_barrier((slot[1], slot[-1], sensor_yh, match_yh))
    slot[2], slot[-2] = shift_z(up, -1), shift_z(down, 1)
    sensor_later, _ = lax.optimization_barrier((sensor, sensor_yh))
    sensors = [sensor, swap_core(sensor_later), sensor_yh, swap_core(sensor_yh)]
    match_both = swap_core(jnp.concatenate([match, match_yh], 0))
    match = [match, match_both[:1], match_yh, match_both[1:]]
    image_emb, image_inv = call(
        project_kernel,
        [jax.ShapeDtypeStruct((4 * rows, width), BF16), jax.ShapeDtypeStruct((4 * rows, 1), F32)],
        {},
        proj_weight, *sensors,
        far=(0,),
        packed=range(1, 5),
        far_out=(1,),
        cuts={0: CUT},
    )
    up, down, _ = lax.optimization_barrier((slot[2], slot[-2], image_emb))
    slot[3], slot[-3], slot[4] = shift_z(up, -1), shift_z(down, 1), shift_z(down, 2)

    text_shape = jax.ShapeDtypeStruct((rows, width), BF16)
    acc_shape = jax.ShapeDtypeStruct((4 * rows, width), F32)
    keys = (0, 1, -1, 2, -2)
    match_rows, acc, text_0, text_1, text_m1, text_2, text_m2 = call(
        functools.partial(first_pairs_kernel, keys),
        [jax.ShapeDtypeStruct((4 * rows, 1), F32), acc_shape, jax.ShapeDtypeStruct((rows, width), F32)] + [text_shape] * 4,
        {},
        numbers, place, image_emb, *match, *(slot[k] for k in keys),
        packed=range(7, 12),
        far_out=range(2, 7),
    )
    keys = (3, -3)
    acc, text_3, text_m3 = call(
        functools.partial(pairs_kernel, keys),
        [acc_shape] + [text_shape] * 2,
        {6: 0},
        numbers, place, image_emb, match_rows, *(slot[k] for k in keys), acc,
        packed=range(4, 6),
        far_out=range(1, 3),
    )
    shapes = [((4 * rows, width), F32), ((4 * rows, 1), F32), ((4 * rows + 16, width // 2), BF16)]
    shapes.append(((4 * rows, rows), BF16))
    acc, dot, packet, last_grad = call(
        last_kernel,
        [jax.ShapeDtypeStruct(*s) for s in shapes],
        {5: 0},
        numbers, place, image_emb, match_rows, slot[4], acc,
    )

    got = swap_core(packet)
    weight_part, row_half, row_other, extra = call(
        weight_kernel,
        [jax.ShapeDtypeStruct((DP, width // 16, feat), BF16)] + [jax.ShapeDtypeStruct((2 * rows, width // 2), F32)] * 3,
        {},
        place, got, acc, dot, image_emb, image_inv, *sensors,
        far=(5,),
        far_out=(0, 1),
        pushed=(2, 3),
        sends=DP + 5,
    )
    last_grad, text_1, text_m1, text_3, text_m3, _ = lax.optimization_barrier(
        (last_grad, text_1, text_m1, text_3, text_m3, weight_part)
    )
    (text_4,) = call(
        last_text_kernel, [jax.ShapeDtypeStruct((rows, width), BF16)], {}, numbers, last_grad, image_emb, far_out=(0,)
    )
    shapes = [((rows, width), BF16), ((rows, width), F32)]
    row_send, row_keep = call(
        row_kernel,
        [jax.ShapeDtypeStruct(*s) for s in shapes],
        {},
        place, row_half, row_other, swap_core(extra),
        far=range(1, 4),
        far_out=(0, 1),
    )
    weight_part = lax.all_to_all(weight_part, "dp", 0, 0, tiled=True)

    per_loop = feat // LOOP
    block = (per_loop // 2, width // 8)
    (weight_chunks,) = call(
        chunk_kernel, [jax.ShapeDtypeStruct((LOOP,) + block, BF16)], {}, weight_part, far_out=(0,)
    )
    weight_part = lax.all_to_all(weight_chunks, "loop", 0, 0, tiled=True)
    (shares,) = call(
        share_kernel, [jax.ShapeDtypeStruct((DP, per_loop, width // 8), F32)], {}, weight_part, far_out=(0,)
    )

    from_below, from_above, far = shift_z(text_3, 1), shift_z(text_m3, -1), shift_z(text_4, 2)
    near_below, near_above = shift_z(text_1, 1), shift_z(text_m1, -1)
    row_got = swap_yh(row_send)
    from_below, from_above, far, near_below, near_above, row_got, _ = lax.optimization_barrier(
        (from_below, from_above, far, near_below, near_above, row_got, weight_chunks)
    )
    up, down = call(
        sums_kernel,
        [jax.ShapeDtypeStruct((rows, width), BF16)] * 2,
        {},
        text_2, from_below, far, text_m2, from_above,
        far=range(5),
        far_out=range(2),
    )
    up, down = shift_z(up, 2), shift_z(down, -2)

    (sensor_grad,) = call(
        sensor_kernel,
        [jax.ShapeDtypeStruct((rows, feat), BF16)],
        {},
        row_keep, row_got, image_inv, proj_weight, image_emb,
        far=range(4),
        far_out=(0,),
    )
    shares, _ = lax.optimization_barrier((shares, sensor_grad))
    up, down, _ = lax.optimization_barrier((up, down, shares))
    shares = lax.all_to_all(shares, "dp", 0, 0, tiled=True)
    (weight_grad,) = call(
        layout_kernel, [jax.ShapeDtypeStruct((per_loop, width), F32)], {}, shares, far_out=(0,)
    )
    (text_grad,) = call(
        text_kernel,
        [jax.ShapeDtypeStruct((rows, width), F32)],
        {},
        texts, text_0, near_below, near_above, up, down,
        far=range(6),
        far_out=(0,),
    )
    return (sensor_grad[None], text_grad[None], weight_grad)


def solution(mesh):
    placed = (P("dp", "loop", None), P("dp", "loop", None), P(), P("dp", "loop"), P(), P())
    return jax.shard_map(
        on_device,
        mesh=mesh,
        in_specs=placed,
        out_specs=(P("dp", "loop", None), P("dp", "loop", None), P("loop", None)),
        check_vma=False,
    )
```

```python
import functools

import jax
import jax.numpy as jnp
from jax import lax
from jax.experimental import pallas as pl
from jax.experimental.pallas import tpu as pltpu
from jax.sharding import PartitionSpec as P

Z, YH, CORE = 8, 2, 2
LOOP = Z * YH * CORE
DP = 8
CUT = 640
BF16 = jnp.bfloat16
F32 = jnp.float32
VMEM = pl.BlockSpec(memory_space=pltpu.VMEM)
HBM = pl.BlockSpec(memory_space=pltpu.HBM)
ANY = pl.BlockSpec(memory_space=pl.ANY)
SMEM = pl.BlockSpec(memory_space=pltpu.SMEM)


def route(move):
    pairs = []
    for z in range(Z):
        for y in range(YH):
            for c in range(CORE):
                to_z, to_y, to_c = move(z, y, c)
                source = (z * YH + y) * CORE + c
                pairs.append((source, ((to_z % Z) * YH + to_y) * CORE + to_c))
    return pairs


def shift_z(block, distance):
    return lax.ppermute(block, "loop", route(lambda z, y, c: (z + (1 - 2 * c) * distance, y, c)))


def swap_core(block):
    return lax.ppermute(block, "loop", route(lambda z, y, c: (z, y, 1 - c)))


def swap_yh(block):
    return lax.ppermute(block, "loop", route(lambda z, y, c: (z, 1 - y, c)))


def inner_rows(left, right):
    return lax.dot_general(left, right, (((1,), (1,)), ((), ())), preferred_element_type=F32)


def inner_cols(left, right):
    return lax.dot_general(left, right, (((0,), (0,)), ((), ())), preferred_element_type=F32)


class Moves:
    def __init__(self, base, sems, loads, held, outs, pack):
        self.base = base
        self.sems, self.loads, self.held, self.outs, self.pack, self.sent = sems, loads, held, outs, pack, []

    def need(self, n):
        self.loads[n].wait()

    def push(self, source, n, part):
        copy = pltpu.make_async_copy(source, self.outs[n].at[part], self.sems.at[self.base + len(self.sent)])
        copy.start()
        self.sent.append(copy)

    def send(self, n, part=None):
        source, target = self.held[n], self.outs[n]
        if part is not None:
            source, target = source.at[part], target.at[part]
        copy = pltpu.make_async_copy(source, target, self.sems.at[self.base + len(self.sent)])
        copy.start()
        self.sent.append(copy)


def call(kernel, out, aliases, *operands, far=(), packed=(), far_out=(), pushed=(), sends=None, cuts=(), loose=()):
    cuts = dict(cuts)
    far, packed, far_out, total = list(far), list(packed), list(far_out), len(operands)
    sends = len(far_out) if sends is None else sends

    def body(*refs):
        ins, outs, scratch = refs[:total], refs[total : total + len(out)], refs[total + len(out) :]
        held = dict(zip(far, scratch[: len(far)]))
        held_out = dict(zip(far_out, scratch[len(far) : len(far) + len(far_out)]))
        for m, n in enumerate(packed):
            height = operands[n].shape[0]
            held[n] = scratch[-2].at[pl.ds(m * height, height)]
        whole = [(m, n) for m, n in enumerate(in_hbm) if n not in cuts]
        loads = {n: pltpu.make_async_copy(ins[n], held[n], scratch[-1].at[m]) for m, n in whole}
        for n, cut in cuts.items():
            for m, part in enumerate((pl.ds(0, cut), pl.ds(cut, operands[n].shape[0] - cut))):
                sem = scratch[-1].at[len(in_hbm) + sends] if m else scratch[-1].at[far.index(n)]
                loads[n, m] = pltpu.make_async_copy(ins[n].at[part], held[n].at[part], sem)
        for load in loads.values():
            load.start()
        moves = Moves(len(in_hbm), scratch[-1], loads, held_out, outs, scratch[-2] if packed else None)
        kernel(moves, *(held.get(n, ref) for n, ref in enumerate(ins)), *(held_out.get(n, ref) for n, ref in enumerate(outs)))
        for copy in moves.sent:
            copy.wait()

    in_hbm, out_hbm = far + packed, far_out + list(pushed)
    in_specs = [SMEM if o.ndim == 1 else HBM if n in in_hbm else VMEM for n, o in enumerate(operands)]
    in_specs = [ANY if n in loose else spec for n, spec in enumerate(in_specs)]
    scratch = [pltpu.VMEM(operands[n].shape, operands[n].dtype) for n in far]
    scratch += [pltpu.VMEM(out[n].shape, out[n].dtype) for n in far_out]
    if packed:
        height, width = operands[packed[0]].shape
        scratch.append(pltpu.VMEM((len(packed) * height, width), operands[packed[0]].dtype))
    scratch.append(pltpu.SemaphoreType.DMA((len(in_hbm) + sends + 1,)))
    operands = [o if n in loose or n not in in_hbm else pltpu.with_memory_space_constraint(o, pltpu.HBM) for n, o in enumerate(operands)]
    return pl.pallas_call(
        body,
        out_shape=[pltpu.HBM(o.shape, o.dtype) if n in out_hbm else o for n, o in enumerate(out)],
        in_specs=in_specs,
        out_specs=[HBM if n in out_hbm else VMEM for n in range(len(out))],
        scratch_shapes=scratch,
        input_output_aliases=aliases,
        cost_estimate=pl.CostEstimate(flops=1, bytes_accessed=1, transcendentals=0),
        compiler_params=pltpu.CompilerParams(vmem_limit_bytes=20 << 20),
    )(*operands)


def scale_of(numbers):
    return jnp.exp(jnp.full((1, 128), numbers[0], F32))[:, 0:1]


def block_grads(numbers, columns, image_emb, match, text):
    wide = text.astype(F32)
    inv = lax.rsqrt(jnp.sum(wide * wide, -1, keepdims=True) + 1e-06)
    emb = (wide * inv).astype(BF16)
    logits = scale_of(numbers) * inner_rows(image_emb, emb) + numbers[1]
    positive = (match == columns).astype(F32)
    return emb, (jax.nn.sigmoid(logits) - positive).astype(BF16)


def columns_of(place, key, rows):
    step = (1 - 2 * (place[0] & 1)) * (YH * CORE)
    start = (place[0] + key * step + LOOP) % LOOP * rows
    return (lax.broadcasted_iota(jnp.int32, (1, rows), 1) + start).astype(F32)


def pairs_body(keys, moves, first, numbers, place, image_emb, match, texts, acc_in, acc_out, text_out):
    count = len(keys)
    image = image_emb[...]
    rows = texts[0].shape[0]
    columns = jnp.concatenate([columns_of(place, key, rows) for key in keys], 1)
    for n in range(count):
        moves.need(first + n)
    emb, grad = block_grads(numbers, columns, image, match[...], moves.pack[...])
    text_part = scale_of(numbers) * inner_cols(grad, image)
    shift = 2 if acc_in is None else 1
    for n in range(count):
        text_out[n][...] = text_part[n * rows : (n + 1) * rows].astype(text_out[n].dtype)
        moves.send(shift + n)
    part = jnp.dot(grad, emb, preferred_element_type=F32)
    acc_out[...] = part if acc_in is None else acc_in[...] + part


def pairs_kernel(keys, moves, numbers, place, image_emb, match, *refs):
    count = len(keys)
    pairs_body(keys, moves, 4, numbers, place, image_emb, match, refs[:count], refs[count], refs[count + 1], refs[count + 2 :])


def project_kernel(moves, proj_weight, own, core, yh, both, emb, inv_out):
    for n in range(4):
        moves.need(1 + n)
    sensor = moves.pack[...]
    moves.need((0, 0))
    projected = jnp.dot(sensor[:, :CUT], proj_weight[:CUT], preferred_element_type=F32)
    moves.need((0, 1))
    projected = projected + jnp.dot(sensor[:, CUT:], proj_weight[CUT:], preferred_element_type=F32)
    inv = lax.rsqrt(jnp.sum(projected * projected, -1, keepdims=True) + 1e-06)
    inv_out[...] = inv
    moves.send(1)
    emb[...] = (projected * inv).astype(BF16)


def first_pairs_kernel(keys, moves, numbers, place, image_emb, own, core, yh, both, *refs):
    texts, match, outs = refs[: len(keys)], refs[len(keys)], refs[len(keys) + 1 :]
    block = own.shape[1]
    for n, line in enumerate((own, core, yh, both)):
        turned = jnp.broadcast_to(line[...].astype(F32), (128, block)).T
        match[n * block : (n + 1) * block, :] = turned[:, 0:1]
    pairs_body(keys, moves, 7, numbers, place, image_emb, match, texts, None, outs[0], outs[1:])


def last_kernel(moves, numbers, place, image_emb, match, text, acc_in, acc_out, dot_out, packet, grad_out):
    columns = columns_of(place, 4, text.shape[0])
    emb, grad = block_grads(numbers, columns, image_emb[...], match[...], text[...])
    grad_out[...] = grad
    acc = scale_of(numbers) * (acc_in[...] + jnp.dot(grad, emb, preferred_element_type=F32))
    acc_out[...] = acc
    dot = jnp.sum(image_emb[...].astype(F32) * acc, -1, keepdims=True)
    dot_out[...] = dot
    rows, width = acc.shape
    half, block = width // 2, rows // 4
    core = place[0] & 1
    other = pl.ds(pl.multiple_of((1 - core) * half, half), half)
    packet[:rows, :] = acc_out[:, other].astype(BF16)
    lines = []
    for slot in range(4):
        mine = slice(slot * block, (slot + 1) * block)
        flat = jnp.broadcast_to(dot[mine], (block, 128)).T[0:1, :]
        top = flat.astype(BF16).astype(F32)
        lines.append(jnp.concatenate([top, flat - top, jnp.zeros((1, half - 256), F32)], 1))
    lines.append(jnp.zeros((packet.shape[0] - rows - 4, half), F32))
    packet[rows:, :] = jnp.concatenate(lines, 0).astype(BF16)


def last_text_kernel(moves, numbers, grad, image_emb, out):
    out[...] = (scale_of(numbers) * inner_cols(grad[...], image_emb[...])).astype(out.dtype)
    moves.send(0)


def weight_kernel(moves, place, got, acc, dot, image_emb, inv, own_rows, core_rows, yh_rows, both_rows, weight, row_half, row_other, extra):
    rows, width = acc.shape
    half, quarter, block = width // 2, width // 4, rows // 4
    core = place[0] & 1
    own = pl.ds(pl.multiple_of(core * half, half), half)
    other = pl.ds(pl.multiple_of((1 - core) * half, half), half)
    for n in range(2):
        here = pl.ds(n * block, block)
        moves.push(acc.at[pl.ds((2 * n + 1) * block, block), own], 3, here)
        moves.push(acc.at[pl.ds(2 * n * block, block), other], 2, here)
    digits = got[rows:, :256].astype(F32)
    moves.need(5)
    projs = []
    for slot in range(4):
        mine = slice(slot * block, (slot + 1) * block)
        theirs = slice((slot ^ 1) * block, ((slot ^ 1) + 1) * block)
        kept = acc[mine, own] + got[theirs, :].astype(F32)
        if slot in (0, 2):
            row_half[slot // 2 * block : (slot // 2 + 1) * block, :] = kept
            if slot == 2:
                moves.send(1)
        line = digits[slot ^ 1 : (slot ^ 1) + 1, :]
        other_dot = jnp.broadcast_to(line[:, :128] + line[:, 128:], (block, 128)).T[:, 0:1]
        unit = image_emb[mine, own].astype(F32)
        projs.append(((kept - unit * (dot[mine, :] + other_dot)) * inv[mine, :]).astype(BF16))
    proj = jnp.concatenate(projs, 0)
    sensor = jnp.concatenate([own_rows[...], core_rows[...], yh_rows[...], both_rows[...]], 0)
    chunk = weight.shape[1]
    for side in range(2):
        product = inner_cols(proj[:, side * quarter : (side + 1) * quarter], sensor).astype(BF16)
        for m in range(quarter // chunk):
            at = side * (quarter // chunk) + m
            weight[at] = product[m * chunk : (m + 1) * chunk]
            moves.send(0, at)


def row_kernel(moves, place, row_half, row_other, extra, row_send, row_keep):
    block, half = row_half.shape[0] // 2, row_half.shape[1]
    core = place[0] & 1
    own = pl.ds(pl.multiple_of(core * half, half), half)
    other = pl.ds(pl.multiple_of((1 - core) * half, half), half)
    for n in range(3):
        moves.need(1 + n)
    for n, target in ((1, row_send), (0, row_keep)):
        here = slice(n * block, (n + 1) * block)
        target[:, own] = row_half[here, :].astype(target.dtype)
        target[:, other] = (row_other[here, :] + extra[here, :]).astype(target.dtype)
        moves.send(1 - n)


def sums_kernel(moves, text_2, below, far, text_m2, above, up, down):
    for n in range(3):
        moves.need(n)
    up[...] = (text_2[...].astype(F32) + below[...].astype(F32) + far[...].astype(F32)).astype(BF16)
    moves.send(0)
    moves.need(3)
    moves.need(4)
    down[...] = (text_m2[...].astype(F32) + above[...].astype(F32)).astype(BF16)
    moves.send(1)


def text_kernel(moves, text, own, near_below, near_above, up, down, out):
    for n in range(6):
        moves.need(n)
    total = own[...] + near_below[...].astype(F32) + near_above[...].astype(F32)
    total = total + up[...].astype(F32) + down[...].astype(F32)
    wide = text[...].astype(F32)
    inv = lax.rsqrt(jnp.sum(wide * wide, -1, keepdims=True) + 1e-06)
    unit = wide * inv
    out[...] = (total - unit * jnp.sum(unit * total, -1, keepdims=True)) * inv
    moves.send(0)


def sensor_kernel(moves, row_keep, row_got, inv, proj_weight, image_emb, out):
    rows = row_keep.shape[0]
    for n in range(3):
        moves.need(n)
    image_grad = row_keep[...] + row_got[...].astype(F32)
    unit = image_emb[:rows, :].astype(F32)
    dot = jnp.sum(unit * image_grad, -1, keepdims=True)
    proj_grad = ((image_grad - unit * dot) * inv[:rows, :]).astype(BF16)
    moves.need(3)
    out[...] = inner_rows(proj_grad, proj_weight[...]).astype(BF16)
    moves.send(0)


def chunk_kernel(moves, parts, out):
    total = parts[0].astype(F32)
    for n in range(1, parts.shape[0]):
        total = total + parts[n].astype(F32)
    turned = total.T
    count, rows, lanes = out.shape
    for n in range(count):
        at = 2 * rows * n
        out[n] = jnp.concatenate([turned[at : at + rows], turned[at + rows : at + 2 * rows]], 1).astype(BF16)
    moves.send(0)


def share_kernel(moves, parts, out):
    rows = parts.shape[1]
    for core in range(CORE):
        total = parts[core].astype(F32)
        for n in range(1, Z * YH):
            total = total + parts[n * CORE + core].astype(F32)
        total = total * (1.0 / DP)
        for n in range(DP):
            out[n, core * rows : (core + 1) * rows] = total
    moves.send(0)


def layout_kernel(moves, shares, out):
    rows, lanes = shares.shape[1] // 2, shares.shape[2]
    cols = lanes // 2
    for core in range(CORE):
        here = slice(core * rows, (core + 1) * rows)
        for pair in range(DP // 2):
            left, right = shares[2 * pair, here], shares[2 * pair + 1, here]
            at = core * DP * cols + pair * lanes
            out[:rows, at : at + lanes] = jnp.concatenate([left[:, :cols], right[:, :cols]], 1)
            out[rows:, at : at + lanes] = jnp.concatenate([left[:, cols:], right[:, cols:]], 1)
    moves.send(0)


def on_device(sensor_feats, text_embeds, proj_weight, matches, log_scale, logit_bias):
    sensor = sensor_feats[0]
    texts = text_embeds[0]
    rows = sensor.shape[0]
    feat, width = proj_weight.shape
    loop_index = lax.axis_index("loop")
    place = loop_index.reshape(1)
    numbers = jnp.stack([log_scale, logit_bias])

    slot = {0: texts}
    slot[1], slot[-1] = shift_z(texts, -1), shift_z(texts, 1)

    sensor_yh = swap_yh(sensor)
    match = matches.reshape(1, rows)
    match_yh = swap_yh(match)
    up, down, _, _ = lax.optimization_barrier((slot[1], slot[-1], sensor_yh, match_yh))
    slot[2], slot[-2] = shift_z(up, -1), shift_z(down, 1)
    sensor_later, sensor_yh_later, _, _, _ = lax.optimization_barrier((sensor, sensor_yh, match_yh, slot[1], slot[-1]))
    sensors = [sensor, swap_core(sensor_later), sensor_yh, swap_core(sensor_yh_later)]
    match_both = swap_core(jnp.concatenate([match, match_yh], 0))
    match = [match, match_both[:1], match_yh, match_both[1:]]
    image_emb, image_inv = call(
        project_kernel,
        [jax.ShapeDtypeStruct((4 * rows, width), BF16), jax.ShapeDtypeStruct((4 * rows, 1), F32)],
        {},
        proj_weight, *sensors,
        far=(0,),
        packed=range(1, 5),
        far_out=(1,),
        cuts={0: CUT},
    )
    up, down, _ = lax.optimization_barrier((slot[2], slot[-2], image_emb))
    slot[3], slot[-3], slot[4] = shift_z(up, -1), shift_z(down, 1), shift_z(down, 2)

    text_shape = jax.ShapeDtypeStruct((rows, width), BF16)
    acc_shape = jax.ShapeDtypeStruct((4 * rows, width), F32)
    keys = (0, 1, -1, 2, -2)
    match_rows, acc, text_0, text_1, text_m1, text_2, text_m2 = call(
        functools.partial(first_pairs_kernel, keys),
        [jax.ShapeDtypeStruct((4 * rows, 1), F32), acc_shape, jax.ShapeDtypeStruct((rows, width), F32)] + [text_shape] * 4,
        {},
        numbers, place, image_emb, *match, *(slot[k] for k in keys),
        packed=range(7, 12),
        far_out=range(2, 7),
    )
    keys = (3, -3)
    acc, text_3, text_m3 = call(
        functools.partial(pairs_kernel, keys),
        [acc_shape] + [text_shape] * 2,
        {6: 0},
        numbers, place, image_emb, match_rows, *(slot[k] for k in keys), acc,
        packed=range(4, 6),
        far_out=range(1, 3),
        loose=range(4, 6),
    )
    shapes = [((4 * rows, width), F32), ((4 * rows, 1), F32), ((4 * rows + 16, width // 2), BF16)]
    shapes.append(((4 * rows, rows), BF16))
    acc, dot, packet, last_grad = call(
        last_kernel,
        [jax.ShapeDtypeStruct(*s) for s in shapes],
        {5: 0},
        numbers, place, image_emb, match_rows, slot[4], acc,
    )

    got = swap_core(packet)
    weight_part, row_half, row_other, extra = call(
        weight_kernel,
        [jax.ShapeDtypeStruct((DP, width // 16, feat), BF16)] + [jax.ShapeDtypeStruct((2 * rows, width // 2), F32)] * 3,
        {},
        place, got, acc, dot, image_emb, image_inv, *sensors,
        far=(5,),
        far_out=(0, 1),
        pushed=(2, 3),
        sends=DP + 5,
    )
    last_grad, text_1, text_m1, text_3, text_m3, _ = lax.optimization_barrier(
        (last_grad, text_1, text_m1, text_3, text_m3, weight_part)
    )
    (text_4,) = call(
        last_text_kernel, [jax.ShapeDtypeStruct((rows, width), BF16)], {}, numbers, last_grad, image_emb, far_out=(0,)
    )
    shapes = [((rows, width), BF16), ((rows, width), F32)]
    row_send, row_keep = call(
        row_kernel,
        [jax.ShapeDtypeStruct(*s) for s in shapes],
        {},
        place, row_half, row_other, swap_core(extra),
        far=range(1, 4),
        far_out=(0, 1),
    )
    weight_part = lax.all_to_all(weight_part, "dp", 0, 0, tiled=True)

    per_loop = feat // LOOP
    block = (per_loop // 2, width // 8)
    (weight_chunks,) = call(
        chunk_kernel, [jax.ShapeDtypeStruct((LOOP,) + block, BF16)], {}, weight_part, far_out=(0,)
    )
    weight_part = lax.all_to_all(weight_chunks, "loop", 0, 0, tiled=True)
    (shares,) = call(
        share_kernel, [jax.ShapeDtypeStruct((DP, per_loop, width // 8), F32)], {}, weight_part, far_out=(0,)
    )

    from_below, from_above, far = shift_z(text_3, 1), shift_z(text_m3, -1), shift_z(text_4, 2)
    near_below, near_above = shift_z(text_1, 1), shift_z(text_m1, -1)
    row_got = swap_yh(row_send)
    from_below, from_above, far, near_below, near_above, row_got, _ = lax.optimization_barrier(
        (from_below, from_above, far, near_below, near_above, row_got, weight_chunks)
    )
    up, down = call(
        sums_kernel,
        [jax.ShapeDtypeStruct((rows, width), BF16)] * 2,
        {},
        text_2, from_below, far, text_m2, from_above,
        far=range(5),
        far_out=range(2),
        loose=(1, 2, 4),
    )
    up, down = shift_z(up, 2), shift_z(down, -2)

    (sensor_grad,) = call(
        sensor_kernel,
        [jax.ShapeDtypeStruct((rows, feat), BF16)],
        {},
        row_keep, row_got, image_inv, proj_weight, image_emb,
        far=range(4),
        far_out=(0,),
    )
    shares, _ = lax.optimization_barrier((shares, sensor_grad))
    up, down, _ = lax.optimization_barrier((up, down, shares))
    shares = lax.all_to_all(shares, "dp", 0, 0, tiled=True)
    (weight_grad,) = call(
        layout_kernel, [jax.ShapeDtypeStruct((per_loop, width), F32)], {}, shares, far_out=(0,)
    )
    (text_grad,) = call(
        text_kernel,
        [jax.ShapeDtypeStruct((rows, width), F32)],
        {},
        texts, text_0, near_below, near_above, up, down,
        far=range(6),
        far_out=(0,),
        loose=(4, 5),
    )
    return (sensor_grad[None], text_grad[None], weight_grad)


def solution(mesh):
    placed = (P("dp", "loop", None), P("dp", "loop", None), P(), P("dp", "loop"), P(), P())
    return jax.shard_map(
        on_device,
        mesh=mesh,
        in_specs=placed,
        out_specs=(P("dp", "loop", None), P("dp", "loop", None), P("loop", None)),
        check_vma=False,
    )
```

```python
import functools

import jax
import jax.numpy as jnp
from jax import lax
from jax.experimental import pallas as pl
from jax.experimental.pallas import tpu as pltpu
from jax.sharding import PartitionSpec as P

Z, YH, CORE = 8, 2, 2
LOOP = Z * YH * CORE
DP = 8
CUT = 640
BF16 = jnp.bfloat16
F32 = jnp.float32
VMEM = pl.BlockSpec(memory_space=pltpu.VMEM)
HBM = pl.BlockSpec(memory_space=pltpu.HBM)
ANY = pl.BlockSpec(memory_space=pl.ANY)
SMEM = pl.BlockSpec(memory_space=pltpu.SMEM)


def route(move):
    pairs = []
    for z in range(Z):
        for y in range(YH):
            for c in range(CORE):
                to_z, to_y, to_c = move(z, y, c)
                source = (z * YH + y) * CORE + c
                pairs.append((source, ((to_z % Z) * YH + to_y) * CORE + to_c))
    return pairs


def shift_z(block, distance):
    return lax.ppermute(block, "loop", route(lambda z, y, c: (z + (1 - 2 * c) * distance, y, c)))


def swap_core(block):
    return lax.ppermute(block, "loop", route(lambda z, y, c: (z, y, 1 - c)))


def swap_yh(block):
    return lax.ppermute(block, "loop", route(lambda z, y, c: (z, 1 - y, c)))


def inner_rows(left, right):
    return lax.dot_general(left, right, (((1,), (1,)), ((), ())), preferred_element_type=F32)


def inner_cols(left, right):
    return lax.dot_general(left, right, (((0,), (0,)), ((), ())), preferred_element_type=F32)


class Moves:
    def __init__(self, base, sems, loads, held, outs, pack):
        self.base = base
        self.sems, self.loads, self.held, self.outs, self.pack, self.sent = sems, loads, held, outs, pack, []

    def need(self, n):
        self.loads[n].wait()

    def push(self, source, n, part):
        copy = pltpu.make_async_copy(source, self.outs[n].at[part], self.sems.at[self.base + len(self.sent)])
        copy.start()
        self.sent.append(copy)

    def send(self, n, part=None):
        source, target = self.held[n], self.outs[n]
        if part is not None:
            source, target = source.at[part], target.at[part]
        copy = pltpu.make_async_copy(source, target, self.sems.at[self.base + len(self.sent)])
        copy.start()
        self.sent.append(copy)


def call(kernel, out, aliases, *operands, far=(), packed=(), far_out=(), pushed=(), sends=None, cuts=(), loose=()):
    cuts = dict(cuts)
    far, packed, far_out, total = list(far), list(packed), list(far_out), len(operands)
    sends = len(far_out) if sends is None else sends

    def body(*refs):
        ins, outs, scratch = refs[:total], refs[total : total + len(out)], refs[total + len(out) :]
        held = dict(zip(far, scratch[: len(far)]))
        held_out = dict(zip(far_out, scratch[len(far) : len(far) + len(far_out)]))
        for m, n in enumerate(packed):
            height = operands[n].shape[0]
            held[n] = scratch[-2].at[pl.ds(m * height, height)]
        whole = [(m, n) for m, n in enumerate(in_hbm) if n not in cuts]
        loads = {n: pltpu.make_async_copy(ins[n], held[n], scratch[-1].at[m]) for m, n in whole}
        for n, cut in cuts.items():
            for m, part in enumerate((pl.ds(0, cut), pl.ds(cut, operands[n].shape[0] - cut))):
                sem = scratch[-1].at[len(in_hbm) + sends] if m else scratch[-1].at[far.index(n)]
                loads[n, m] = pltpu.make_async_copy(ins[n].at[part], held[n].at[part], sem)
        for load in loads.values():
            load.start()
        moves = Moves(len(in_hbm), scratch[-1], loads, held_out, outs, scratch[-2] if packed else None)
        kernel(moves, *(held.get(n, ref) for n, ref in enumerate(ins)), *(held_out.get(n, ref) for n, ref in enumerate(outs)))
        for copy in moves.sent:
            copy.wait()

    in_hbm, out_hbm = far + packed, far_out + list(pushed)
    in_specs = [SMEM if o.ndim == 1 else HBM if n in in_hbm else VMEM for n, o in enumerate(operands)]
    in_specs = [ANY if n in loose else spec for n, spec in enumerate(in_specs)]
    scratch = [pltpu.VMEM(operands[n].shape, operands[n].dtype) for n in far]
    scratch += [pltpu.VMEM(out[n].shape, out[n].dtype) for n in far_out]
    if packed:
        height, width = operands[packed[0]].shape
        scratch.append(pltpu.VMEM((len(packed) * height, width), operands[packed[0]].dtype))
    scratch.append(pltpu.SemaphoreType.DMA((len(in_hbm) + sends + 1,)))
    operands = [o if n in loose or n not in in_hbm else pltpu.with_memory_space_constraint(o, pltpu.HBM) for n, o in enumerate(operands)]
    return pl.pallas_call(
        body,
        out_shape=[pltpu.HBM(o.shape, o.dtype) if n in out_hbm else o for n, o in enumerate(out)],
        in_specs=in_specs,
        out_specs=[HBM if n in out_hbm else VMEM for n in range(len(out))],
        scratch_shapes=scratch,
        input_output_aliases=aliases,
        cost_estimate=pl.CostEstimate(flops=1, bytes_accessed=1, transcendentals=0),
        compiler_params=pltpu.CompilerParams(vmem_limit_bytes=20 << 20),
    )(*operands)


def scale_of(numbers):
    return jnp.exp(jnp.full((1, 128), numbers[0], F32))[:, 0:1]


def block_grads(numbers, columns, image_emb, match, text):
    wide = text.astype(F32)
    inv = lax.rsqrt(jnp.sum(wide * wide, -1, keepdims=True) + 1e-06)
    emb = (wide * inv).astype(BF16)
    logits = scale_of(numbers) * inner_rows(image_emb, emb) + numbers[1]
    positive = (match == columns).astype(F32)
    return emb, (jax.nn.sigmoid(logits) - positive).astype(BF16)


def columns_of(place, key, rows):
    step = (1 - 2 * (place[0] & 1)) * (YH * CORE)
    start = (place[0] + key * step + LOOP) % LOOP * rows
    return (lax.broadcasted_iota(jnp.int32, (1, rows), 1) + start).astype(F32)


def pairs_body(keys, moves, first, numbers, place, image_emb, match, texts, acc_in, acc_out, text_out):
    count = len(keys)
    image = image_emb[...]
    rows = texts[0].shape[0]
    columns = jnp.concatenate([columns_of(place, key, rows) for key in keys], 1)
    for n in range(count):
        moves.need(first + n)
    emb, grad = block_grads(numbers, columns, image, match[...], moves.pack[...])
    text_part = scale_of(numbers) * inner_cols(grad, image)
    shift = 2 if acc_in is None else 1
    for n in range(count):
        text_out[n][...] = text_part[n * rows : (n + 1) * rows].astype(text_out[n].dtype)
        moves.send(shift + n)
    part = jnp.dot(grad, emb, preferred_element_type=F32)
    acc_out[...] = part if acc_in is None else acc_in[...] + part


def pairs_kernel(keys, moves, numbers, place, image_emb, match, *refs):
    count = len(keys)
    pairs_body(keys, moves, 4, numbers, place, image_emb, match, refs[:count], refs[count], refs[count + 1], refs[count + 2 :])


def project_kernel(moves, proj_weight, own, core, yh, both, emb, inv_out):
    for n in range(4):
        moves.need(1 + n)
    sensor = moves.pack[...]
    moves.need((0, 0))
    projected = jnp.dot(sensor[:, :CUT], proj_weight[:CUT], preferred_element_type=F32)
    moves.need((0, 1))
    projected = projected + jnp.dot(sensor[:, CUT:], proj_weight[CUT:], preferred_element_type=F32)
    inv = lax.rsqrt(jnp.sum(projected * projected, -1, keepdims=True) + 1e-06)
    inv_out[...] = inv
    moves.send(1)
    emb[...] = (projected * inv).astype(BF16)


def first_pairs_kernel(keys, moves, numbers, place, image_emb, own, core, yh, both, *refs):
    texts, match, outs = refs[: len(keys)], refs[len(keys)], refs[len(keys) + 1 :]
    block = own.shape[1]
    for n, line in enumerate((own, core, yh, both)):
        turned = jnp.broadcast_to(line[...].astype(F32), (128, block)).T
        match[n * block : (n + 1) * block, :] = turned[:, 0:1]
    pairs_body(keys, moves, 7, numbers, place, image_emb, match, texts, None, outs[0], outs[1:])


def last_kernel(moves, numbers, place, image_emb, match, text, acc_in, acc_out, dot_out, packet, grad_out):
    columns = columns_of(place, 4, text.shape[0])
    emb, grad = block_grads(numbers, columns, image_emb[...], match[...], text[...])
    grad_out[...] = grad
    acc = scale_of(numbers) * (acc_in[...] + jnp.dot(grad, emb, preferred_element_type=F32))
    acc_out[...] = acc
    dot = jnp.sum(image_emb[...].astype(F32) * acc, -1, keepdims=True)
    dot_out[...] = dot
    rows, width = acc.shape
    half, block = width // 2, rows // 4
    core = place[0] & 1
    other = pl.ds(pl.multiple_of((1 - core) * half, half), half)
    packet[:rows, :] = acc_out[:, other].astype(BF16)
    lines = []
    for slot in range(4):
        mine = slice(slot * block, (slot + 1) * block)
        flat = jnp.broadcast_to(dot[mine], (block, 128)).T[0:1, :]
        top = flat.astype(BF16).astype(F32)
        lines.append(jnp.concatenate([top, flat - top, jnp.zeros((1, half - 256), F32)], 1))
    lines.append(jnp.zeros((packet.shape[0] - rows - 4, half), F32))
    packet[rows:, :] = jnp.concatenate(lines, 0).astype(BF16)


def last_text_kernel(moves, numbers, grad, image_emb, out):
    out[...] = (scale_of(numbers) * inner_cols(grad[...], image_emb[...])).astype(out.dtype)
    moves.send(0)


def weight_kernel(moves, place, got, acc, dot, image_emb, inv, own_rows, core_rows, yh_rows, both_rows, weight, row_half, row_other, extra):
    rows, width = acc.shape
    half, quarter, block = width // 2, width // 4, rows // 4
    core = place[0] & 1
    own = pl.ds(pl.multiple_of(core * half, half), half)
    other = pl.ds(pl.multiple_of((1 - core) * half, half), half)
    for n in range(2):
        here = pl.ds(n * block, block)
        moves.push(acc.at[pl.ds((2 * n + 1) * block, block), own], 3, here)
        moves.push(acc.at[pl.ds(2 * n * block, block), other], 2, here)
    digits = got[rows:, :256].astype(F32)
    moves.need(5)
    projs = []
    for slot in range(4):
        mine = slice(slot * block, (slot + 1) * block)
        theirs = slice((slot ^ 1) * block, ((slot ^ 1) + 1) * block)
        kept = acc[mine, own] + got[theirs, :].astype(F32)
        if slot in (0, 2):
            row_half[slot // 2 * block : (slot // 2 + 1) * block, :] = kept
            if slot == 2:
                moves.send(1)
        line = digits[slot ^ 1 : (slot ^ 1) + 1, :]
        other_dot = jnp.broadcast_to(line[:, :128] + line[:, 128:], (block, 128)).T[:, 0:1]
        unit = image_emb[mine, own].astype(F32)
        projs.append(((kept - unit * (dot[mine, :] + other_dot)) * inv[mine, :]).astype(BF16))
    proj = jnp.concatenate(projs, 0)
    sensor = jnp.concatenate([own_rows[...], core_rows[...], yh_rows[...], both_rows[...]], 0)
    chunk = weight.shape[1]
    for side in range(2):
        product = inner_cols(proj[:, side * quarter : (side + 1) * quarter], sensor).astype(BF16)
        for m in range(quarter // chunk):
            at = side * (quarter // chunk) + m
            weight[at] = product[m * chunk : (m + 1) * chunk]
            moves.send(0, at)


def row_kernel(moves, place, row_half, row_other, extra, row_send, row_keep):
    block, half = row_half.shape[0] // 2, row_half.shape[1]
    core = place[0] & 1
    own = pl.ds(pl.multiple_of(core * half, half), half)
    other = pl.ds(pl.multiple_of((1 - core) * half, half), half)
    for n in range(3):
        moves.need(1 + n)
    for n, target in ((1, row_send), (0, row_keep)):
        here = slice(n * block, (n + 1) * block)
        target[:, own] = row_half[here, :].astype(target.dtype)
        target[:, other] = (row_other[here, :] + extra[here, :]).astype(target.dtype)
        moves.send(1 - n)


def sums_kernel(moves, text_2, below, far, text_m2, above, up, down):
    for n in range(3):
        moves.need(n)
    up[...] = (text_2[...].astype(F32) + below[...].astype(F32) + far[...].astype(F32)).astype(BF16)
    moves.send(0)
    moves.need(3)
    moves.need(4)
    down[...] = (text_m2[...].astype(F32) + above[...].astype(F32)).astype(BF16)
    moves.send(1)


def text_kernel(moves, text, own, near_below, near_above, up, down, out):
    for n in range(6):
        moves.need(n)
    total = own[...] + near_below[...].astype(F32) + near_above[...].astype(F32)
    total = total + up[...].astype(F32) + down[...].astype(F32)
    wide = text[...].astype(F32)
    inv = lax.rsqrt(jnp.sum(wide * wide, -1, keepdims=True) + 1e-06)
    unit = wide * inv
    out[...] = (total - unit * jnp.sum(unit * total, -1, keepdims=True)) * inv
    moves.send(0)


def sensor_kernel(moves, row_keep, row_got, inv, proj_weight, image_emb, out):
    rows = row_keep.shape[0]
    for n in range(3):
        moves.need(n)
    image_grad = row_keep[...] + row_got[...].astype(F32)
    unit = image_emb[:rows, :].astype(F32)
    dot = jnp.sum(unit * image_grad, -1, keepdims=True)
    proj_grad = ((image_grad - unit * dot) * inv[:rows, :]).astype(BF16)
    moves.need(3)
    out[...] = inner_rows(proj_grad, proj_weight[...]).astype(BF16)
    moves.send(0)


def chunk_kernel(moves, parts, out):
    total = parts[0].astype(F32)
    for n in range(1, parts.shape[0]):
        total = total + parts[n].astype(F32)
    turned = total.T
    count, rows, lanes = out.shape
    for n in range(count):
        at = 2 * rows * n
        out[n] = jnp.concatenate([turned[at : at + rows], turned[at + rows : at + 2 * rows]], 1).astype(BF16)
    moves.send(0)


def share_kernel(moves, parts, out):
    rows = parts.shape[1]
    for core in range(CORE):
        total = parts[core].astype(F32)
        for n in range(1, Z * YH):
            total = total + parts[n * CORE + core].astype(F32)
        total = total * (1.0 / DP)
        for n in range(DP):
            out[n, core * rows : (core + 1) * rows] = total
    moves.send(0)


def layout_kernel(moves, shares, out):
    rows, lanes = shares.shape[1] // 2, shares.shape[2]
    cols = lanes // 2
    for core in range(CORE):
        here = slice(core * rows, (core + 1) * rows)
        for pair in range(DP // 2):
            left, right = shares[2 * pair, here], shares[2 * pair + 1, here]
            at = core * DP * cols + pair * lanes
            out[:rows, at : at + lanes] = jnp.concatenate([left[:, :cols], right[:, :cols]], 1)
            out[rows:, at : at + lanes] = jnp.concatenate([left[:, cols:], right[:, cols:]], 1)
    moves.send(0)


def on_device(sensor_feats, text_embeds, proj_weight, matches, log_scale, logit_bias):
    sensor = sensor_feats[0]
    texts = text_embeds[0]
    rows = sensor.shape[0]
    feat, width = proj_weight.shape
    loop_index = lax.axis_index("loop")
    place = loop_index.reshape(1)
    numbers = jnp.stack([log_scale, logit_bias])

    slot = {0: texts}
    slot[1], slot[-1] = shift_z(texts, -1), shift_z(texts, 1)

    sensor_yh = swap_yh(sensor)
    match = matches.reshape(1, rows)
    match_yh = swap_yh(match)
    up, down, _, _ = lax.optimization_barrier((slot[1], slot[-1], sensor_yh, match_yh))
    slot[2], slot[-2] = shift_z(up, -1), shift_z(down, 1)
    sensor_later, sensor_yh_later, _, _, _ = lax.optimization_barrier((sensor, sensor_yh, match_yh, slot[1], slot[-1]))
    sensors = [sensor, swap_core(sensor_later), sensor_yh, swap_core(sensor_yh_later)]
    match_both = swap_core(jnp.concatenate([match, match_yh], 0))
    match = [match, match_both[:1], match_yh, match_both[1:]]
    image_emb, image_inv = call(
        project_kernel,
        [jax.ShapeDtypeStruct((4 * rows, width), BF16), jax.ShapeDtypeStruct((4 * rows, 1), F32)],
        {},
        proj_weight, *sensors,
        far=(0,),
        packed=range(1, 5),
        far_out=(1,),
        cuts={0: CUT},
        loose=range(2, 5),
    )
    up, down, _ = lax.optimization_barrier((slot[2], slot[-2], image_emb))
    slot[3], slot[-3] = shift_z(up, -1), shift_z(down, 1)
    far, _ = lax.optimization_barrier((down, match_both))
    slot[4] = shift_z(far, 2)

    text_shape = jax.ShapeDtypeStruct((rows, width), BF16)
    acc_shape = jax.ShapeDtypeStruct((4 * rows, width), F32)
    keys = (0, 1, -1, 2, -2)
    match_rows, acc, text_0, text_1, text_m1, text_2, text_m2 = call(
        functools.partial(first_pairs_kernel, keys),
        [jax.ShapeDtypeStruct((4 * rows, 1), F32), acc_shape, jax.ShapeDtypeStruct((rows, width), F32)] + [text_shape] * 4,
        {},
        numbers, place, image_emb, *match, *(slot[k] for k in keys),
        packed=range(7, 12),
        far_out=range(2, 7),
    )
    text_far = {}
    for key in (-3, 3):
        acc, text_far[key] = call(
            functools.partial(pairs_kernel, (key,)),
            [acc_shape, text_shape],
            {5: 0},
            numbers, place, image_emb, match_rows, slot[key], acc,
            packed=(4,),
            far_out=(1,),
            loose=(4,),
        )
    text_3, text_m3 = text_far[3], text_far[-3]
    shapes = [((4 * rows, width), F32), ((4 * rows, 1), F32), ((4 * rows + 16, width // 2), BF16)]
    shapes.append(((4 * rows, rows), BF16))
    acc, dot, packet, last_grad = call(
        last_kernel,
        [jax.ShapeDtypeStruct(*s) for s in shapes],
        {5: 0},
        numbers, place, image_emb, match_rows, slot[4], acc,
    )

    got = swap_core(packet)
    weight_part, row_half, row_other, extra = call(
        weight_kernel,
        [jax.ShapeDtypeStruct((DP, width // 16, feat), BF16)] + [jax.ShapeDtypeStruct((2 * rows, width // 2), F32)] * 3,
        {},
        place, got, acc, dot, image_emb, image_inv, *sensors,
        far=(5,),
        far_out=(0, 1),
        pushed=(2, 3),
        sends=DP + 5,
    )
    last_grad, text_1, text_m1, text_3, text_m3, _ = lax.optimization_barrier(
        (last_grad, text_1, text_m1, text_3, text_m3, weight_part)
    )
    (text_4,) = call(
        last_text_kernel, [jax.ShapeDtypeStruct((rows, width), BF16)], {}, numbers, last_grad, image_emb, far_out=(0,)
    )
    shapes = [((rows, width), BF16), ((rows, width), F32)]
    row_send, row_keep = call(
        row_kernel,
        [jax.ShapeDtypeStruct(*s) for s in shapes],
        {},
        place, row_half, row_other, swap_core(extra),
        far=range(1, 4),
        far_out=(0, 1),
    )
    weight_part = lax.all_to_all(weight_part, "dp", 0, 0, tiled=True)

    per_loop = feat // LOOP
    block = (per_loop // 2, width // 8)
    (weight_chunks,) = call(
        chunk_kernel, [jax.ShapeDtypeStruct((LOOP,) + block, BF16)], {}, weight_part, far_out=(0,)
    )
    weight_part = lax.all_to_all(weight_chunks, "loop", 0, 0, tiled=True)
    (shares,) = call(
        share_kernel, [jax.ShapeDtypeStruct((DP, per_loop, width // 8), F32)], {}, weight_part, far_out=(0,)
    )

    from_below, from_above, far = shift_z(text_3, 1), shift_z(text_m3, -1), shift_z(text_4, 2)
    near_below, near_above = shift_z(text_1, 1), shift_z(text_m1, -1)
    row_got = swap_yh(row_send)
    from_below, from_above, far, near_below, near_above, row_got, _ = lax.optimization_barrier(
        (from_below, from_above, far, near_below, near_above, row_got, weight_chunks)
    )
    up, down = call(
        sums_kernel,
        [jax.ShapeDtypeStruct((rows, width), BF16)] * 2,
        {},
        text_2, from_below, far, text_m2, from_above,
        far=range(5),
        far_out=range(2),
        loose=(1, 2, 4),
    )
    up, down = shift_z(up, 2), shift_z(down, -2)

    (sensor_grad,) = call(
        sensor_kernel,
        [jax.ShapeDtypeStruct((rows, feat), BF16)],
        {},
        row_keep, row_got, image_inv, proj_weight, image_emb,
        far=range(4),
        far_out=(0,),
    )
    shares, _ = lax.optimization_barrier((shares, sensor_grad))
    up, down, _ = lax.optimization_barrier((up, down, shares))
    shares = lax.all_to_all(shares, "dp", 0, 0, tiled=True)
    (weight_grad,) = call(
        layout_kernel, [jax.ShapeDtypeStruct((per_loop, width), F32)], {}, shares, far_out=(0,)
    )
    (text_grad,) = call(
        text_kernel,
        [jax.ShapeDtypeStruct((rows, width), F32)],
        {},
        texts, text_0, near_below, near_above, up, down,
        far=range(6),
        far_out=(0,),
        loose=(4, 5),
    )
    return (sensor_grad[None], text_grad[None], weight_grad)


def solution(mesh):
    placed = (P("dp", "loop", None), P("dp", "loop", None), P(), P("dp", "loop"), P(), P())
    return jax.shard_map(
        on_device,
        mesh=mesh,
        in_specs=placed,
        out_specs=(P("dp", "loop", None), P("dp", "loop", None), P("loop", None)),
        check_vma=False,
    )
```

```python
import functools

import jax
import jax.numpy as jnp
from jax import lax
from jax.experimental import pallas as pl
from jax.experimental.pallas import tpu as pltpu
from jax.sharding import PartitionSpec as P

Z, YH, CORE = 8, 2, 2
LOOP = Z * YH * CORE
DP = 8
CUT = 640
BF16 = jnp.bfloat16
F32 = jnp.float32
VMEM = pl.BlockSpec(memory_space=pltpu.VMEM)
HBM = pl.BlockSpec(memory_space=pltpu.HBM)
ANY = pl.BlockSpec(memory_space=pl.ANY)
SMEM = pl.BlockSpec(memory_space=pltpu.SMEM)


def route(move):
    pairs = []
    for z in range(Z):
        for y in range(YH):
            for c in range(CORE):
                to_z, to_y, to_c = move(z, y, c)
                source = (z * YH + y) * CORE + c
                pairs.append((source, ((to_z % Z) * YH + to_y) * CORE + to_c))
    return pairs


def shift_z(block, distance):
    return lax.ppermute(block, "loop", route(lambda z, y, c: (z + (1 - 2 * c) * distance, y, c)))


def swap_core(block):
    return lax.ppermute(block, "loop", route(lambda z, y, c: (z, y, 1 - c)))


def swap_yh(block):
    return lax.ppermute(block, "loop", route(lambda z, y, c: (z, 1 - y, c)))


def inner_rows(left, right):
    return lax.dot_general(left, right, (((1,), (1,)), ((), ())), preferred_element_type=F32)


def inner_cols(left, right):
    return lax.dot_general(left, right, (((0,), (0,)), ((), ())), preferred_element_type=F32)


class Moves:
    def __init__(self, base, sems, loads, held, outs, pack):
        self.base = base
        self.sems, self.loads, self.held, self.outs, self.pack, self.sent = sems, loads, held, outs, pack, []

    def need(self, n):
        self.loads[n].wait()

    def push(self, source, n, part):
        copy = pltpu.make_async_copy(source, self.outs[n].at[part], self.sems.at[self.base + len(self.sent)])
        copy.start()
        self.sent.append(copy)

    def send(self, n, part=None):
        source, target = self.held[n], self.outs[n]
        if part is not None:
            source, target = source.at[part], target.at[part]
        copy = pltpu.make_async_copy(source, target, self.sems.at[self.base + len(self.sent)])
        copy.start()
        self.sent.append(copy)


def call(kernel, out, aliases, *operands, far=(), packed=(), far_out=(), pushed=(), sends=None, cuts=(), loose=()):
    cuts = dict(cuts)
    far, packed, far_out, total = list(far), list(packed), list(far_out), len(operands)
    sends = len(far_out) if sends is None else sends

    def body(*refs):
        ins, outs, scratch = refs[:total], refs[total : total + len(out)], refs[total + len(out) :]
        held = dict(zip(far, scratch[: len(far)]))
        held_out = dict(zip(far_out, scratch[len(far) : len(far) + len(far_out)]))
        for m, n in enumerate(packed):
            height = operands[n].shape[0]
            held[n] = scratch[-2].at[pl.ds(m * height, height)]
        whole = [(m, n) for m, n in enumerate(in_hbm) if n not in cuts]
        loads = {n: pltpu.make_async_copy(ins[n], held[n], scratch[-1].at[m]) for m, n in whole}
        for n, cut in cuts.items():
            for m, part in enumerate((pl.ds(0, cut), pl.ds(cut, operands[n].shape[0] - cut))):
                sem = scratch[-1].at[len(in_hbm) + sends] if m else scratch[-1].at[far.index(n)]
                loads[n, m] = pltpu.make_async_copy(ins[n].at[part], held[n].at[part], sem)
        for load in loads.values():
            load.start()
        moves = Moves(len(in_hbm), scratch[-1], loads, held_out, outs, scratch[-2] if packed else None)
        kernel(moves, *(held.get(n, ref) for n, ref in enumerate(ins)), *(held_out.get(n, ref) for n, ref in enumerate(outs)))
        for copy in moves.sent:
            copy.wait()

    in_hbm, out_hbm = far + packed, far_out + list(pushed)
    in_specs = [SMEM if o.ndim == 1 else HBM if n in in_hbm else VMEM for n, o in enumerate(operands)]
    in_specs = [ANY if n in loose else spec for n, spec in enumerate(in_specs)]
    scratch = [pltpu.VMEM(operands[n].shape, operands[n].dtype) for n in far]
    scratch += [pltpu.VMEM(out[n].shape, out[n].dtype) for n in far_out]
    if packed:
        height, width = operands[packed[0]].shape
        scratch.append(pltpu.VMEM((len(packed) * height, width), operands[packed[0]].dtype))
    scratch.append(pltpu.SemaphoreType.DMA((len(in_hbm) + sends + 1,)))
    operands = [o if n in loose or n not in in_hbm else pltpu.with_memory_space_constraint(o, pltpu.HBM) for n, o in enumerate(operands)]
    return pl.pallas_call(
        body,
        out_shape=[pltpu.HBM(o.shape, o.dtype) if n in out_hbm else o for n, o in enumerate(out)],
        in_specs=in_specs,
        out_specs=[HBM if n in out_hbm else VMEM for n in range(len(out))],
        scratch_shapes=scratch,
        input_output_aliases=aliases,
        cost_estimate=pl.CostEstimate(flops=1, bytes_accessed=1, transcendentals=0),
        compiler_params=pltpu.CompilerParams(vmem_limit_bytes=20 << 20),
    )(*operands)


def scale_of(numbers):
    return numbers[0:1, 0:1]


def block_grads(numbers, columns, image_emb, match, text):
    wide = text.astype(F32)
    inv = lax.rsqrt(jnp.sum(wide * wide, -1, keepdims=True) + 1e-06)
    emb = (wide * inv).astype(BF16)
    logits = scale_of(numbers) * inner_rows(image_emb, emb) + numbers[1:2, 0:1]
    positive = (match == columns).astype(F32)
    return emb, (jax.nn.sigmoid(logits) - positive).astype(BF16)


def columns_of(place, key, rows):
    step = (1 - 2 * (place[0] & 1)) * (YH * CORE)
    start = (place[0] + key * step + LOOP) % LOOP * rows
    return (lax.broadcasted_iota(jnp.int32, (1, rows), 1) + start).astype(F32)


def pairs_body(keys, moves, first, numbers, place, image_emb, match, texts, acc_in, acc_out, text_out):
    count = len(keys)
    image = image_emb[...]
    rows = texts[0].shape[0]
    columns = jnp.concatenate([columns_of(place, key, rows) for key in keys], 1)
    for n in range(count):
        moves.need(first + n)
    emb, grad = block_grads(numbers, columns, image, match[...], moves.pack[...])
    text_part = scale_of(numbers) * inner_cols(grad, image)
    shift = 2 if acc_in is None else 1
    for n in range(count):
        text_out[n][...] = text_part[n * rows : (n + 1) * rows].astype(text_out[n].dtype)
        moves.send(shift + n)
    part = jnp.dot(grad, emb, preferred_element_type=F32)
    acc_out[...] = part if acc_in is None else acc_in[...] + part


def pairs_kernel(keys, moves, numbers, place, image_emb, match, *refs):
    count = len(keys)
    pairs_body(keys, moves, 4, numbers, place, image_emb, match, refs[:count], refs[count], refs[count + 1], refs[count + 2 :])


def project_kernel(moves, proj_weight, own, core, yh, both, log_scale, bias, emb, inv_out, numbers):
    for n in range(4):
        moves.need(1 + n)
    sensor = moves.pack[...]
    moves.need((0, 0))
    projected = jnp.dot(sensor[:, :CUT], proj_weight[:CUT], preferred_element_type=F32)
    moves.need((0, 1))
    projected = projected + jnp.dot(sensor[:, CUT:], proj_weight[CUT:], preferred_element_type=F32)
    inv = lax.rsqrt(jnp.sum(projected * projected, -1, keepdims=True) + 1e-06)
    inv_out[...] = inv
    moves.send(1)
    emb[...] = (projected * inv).astype(BF16)
    row = lax.broadcasted_iota(jnp.int32, numbers.shape, 0)
    scale = jnp.exp(jnp.full(numbers.shape, log_scale[0], F32))
    numbers[...] = jnp.where(row == 0, scale, bias[0])


def first_pairs_kernel(keys, moves, numbers, place, image_emb, own, core, yh, both, *refs):
    texts, match, outs = refs[: len(keys)], refs[len(keys)], refs[len(keys) + 1 :]
    block = own.shape[1]
    for n, line in enumerate((own, core, yh, both)):
        turned = jnp.broadcast_to(line[...].astype(F32), (128, block)).T
        match[n * block : (n + 1) * block, :] = turned[:, 0:1]
    pairs_body(keys, moves, 7, numbers, place, image_emb, match, texts, None, outs[0], outs[1:])


def last_kernel(moves, numbers, place, image_emb, match, text, acc_in, acc_out, dot_out, packet, grad_out):
    columns = columns_of(place, 4, text.shape[0])
    emb, grad = block_grads(numbers, columns, image_emb[...], match[...], text[...])
    grad_out[...] = grad
    acc = scale_of(numbers) * (acc_in[...] + jnp.dot(grad, emb, preferred_element_type=F32))
    acc_out[...] = acc
    dot = jnp.sum(image_emb[...].astype(F32) * acc, -1, keepdims=True)
    dot_out[...] = dot
    rows, width = acc.shape
    half, block = width // 2, rows // 4
    core = place[0] & 1
    other = pl.ds(pl.multiple_of((1 - core) * half, half), half)
    packet[:rows, :] = acc_out[:, other].astype(BF16)
    lines = []
    for slot in range(4):
        mine = slice(slot * block, (slot + 1) * block)
        flat = jnp.broadcast_to(dot[mine], (block, 128)).T[0:1, :]
        top = flat.astype(BF16).astype(F32)
        lines.append(jnp.concatenate([top, flat - top, jnp.zeros((1, half - 256), F32)], 1))
    lines.append(jnp.zeros((packet.shape[0] - rows - 4, half), F32))
    packet[rows:, :] = jnp.concatenate(lines, 0).astype(BF16)


def last_text_kernel(moves, numbers, grad, image_emb, out):
    out[...] = (scale_of(numbers) * inner_cols(grad[...], image_emb[...])).astype(out.dtype)
    moves.send(0)


def weight_kernel(moves, place, got, acc, dot, image_emb, inv, own_rows, core_rows, yh_rows, both_rows, weight, row_half, row_other, extra):
    rows, width = acc.shape
    half, quarter, block = width // 2, width // 4, rows // 4
    core = place[0] & 1
    own = pl.ds(pl.multiple_of(core * half, half), half)
    other = pl.ds(pl.multiple_of((1 - core) * half, half), half)
    for n in range(2):
        here = pl.ds(n * block, block)
        moves.push(acc.at[pl.ds((2 * n + 1) * block, block), own], 3, here)
        moves.push(acc.at[pl.ds(2 * n * block, block), other], 2, here)
    digits = got[rows:, :256].astype(F32)
    moves.need(5)
    projs = []
    for slot in range(4):
        mine = slice(slot * block, (slot + 1) * block)
        theirs = slice((slot ^ 1) * block, ((slot ^ 1) + 1) * block)
        kept = acc[mine, own] + got[theirs, :].astype(F32)
        if slot in (0, 2):
            row_half[slot // 2 * block : (slot // 2 + 1) * block, :] = kept
            if slot == 2:
                moves.send(1)
        line = digits[slot ^ 1 : (slot ^ 1) + 1, :]
        other_dot = jnp.broadcast_to(line[:, :128] + line[:, 128:], (block, 128)).T[:, 0:1]
        unit = image_emb[mine, own].astype(F32)
        projs.append(((kept - unit * (dot[mine, :] + other_dot)) * inv[mine, :]).astype(BF16))
    proj = jnp.concatenate(projs, 0)
    sensor = jnp.concatenate([own_rows[...], core_rows[...], yh_rows[...], both_rows[...]], 0)
    chunk = weight.shape[1]
    for side in range(2):
        product = inner_cols(proj[:, side * quarter : (side + 1) * quarter], sensor).astype(BF16)
        for m in range(quarter // chunk):
            at = side * (quarter // chunk) + m
            weight[at] = product[m * chunk : (m + 1) * chunk]
            moves.send(0, at)


def row_kernel(moves, place, row_half, row_other, extra, row_send, row_keep):
    block, half = row_half.shape[0] // 2, row_half.shape[1]
    core = place[0] & 1
    own = pl.ds(pl.multiple_of(core * half, half), half)
    other = pl.ds(pl.multiple_of((1 - core) * half, half), half)
    for n in range(3):
        moves.need(1 + n)
    for n, target in ((1, row_send), (0, row_keep)):
        here = slice(n * block, (n + 1) * block)
        target[:, own] = row_half[here, :].astype(target.dtype)
        target[:, other] = (row_other[here, :] + extra[here, :]).astype(target.dtype)
        moves.send(1 - n)


def sums_kernel(moves, text_2, below, far, text_m2, above, up, down):
    for n in range(3):
        moves.need(n)
    up[...] = (text_2[...].astype(F32) + below[...].astype(F32) + far[...].astype(F32)).astype(BF16)
    moves.send(0)
    moves.need(3)
    moves.need(4)
    down[...] = (text_m2[...].astype(F32) + above[...].astype(F32)).astype(BF16)
    moves.send(1)


def text_kernel(moves, text, own, near_below, near_above, up, down, out):
    for n in range(6):
        moves.need(n)
    total = own[...] + near_below[...].astype(F32) + near_above[...].astype(F32)
    total = total + up[...].astype(F32) + down[...].astype(F32)
    wide = text[...].astype(F32)
    inv = lax.rsqrt(jnp.sum(wide * wide, -1, keepdims=True) + 1e-06)
    unit = wide * inv
    out[...] = (total - unit * jnp.sum(unit * total, -1, keepdims=True)) * inv
    moves.send(0)


def sensor_kernel(moves, row_keep, row_got, inv, proj_weight, image_emb, out):
    rows = row_keep.shape[0]
    for n in range(3):
        moves.need(n)
    image_grad = row_keep[...] + row_got[...].astype(F32)
    unit = image_emb[:rows, :].astype(F32)
    dot = jnp.sum(unit * image_grad, -1, keepdims=True)
    proj_grad = ((image_grad - unit * dot) * inv[:rows, :]).astype(BF16)
    moves.need(3)
    out[...] = inner_rows(proj_grad, proj_weight[...]).astype(BF16)
    moves.send(0)


def chunk_kernel(moves, parts, out):
    total = parts[0].astype(F32)
    for n in range(1, parts.shape[0]):
        total = total + parts[n].astype(F32)
    turned = total.T
    count, rows, lanes = out.shape
    for n in range(count):
        at = 2 * rows * n
        out[n] = jnp.concatenate([turned[at : at + rows], turned[at + rows : at + 2 * rows]], 1).astype(BF16)
    moves.send(0)


def share_kernel(moves, parts, out):
    rows = parts.shape[1]
    for core in range(CORE):
        total = parts[core].astype(F32)
        for n in range(1, Z * YH):
            total = total + parts[n * CORE + core].astype(F32)
        total = total * (1.0 / DP)
        for n in range(DP):
            out[n, core * rows : (core + 1) * rows] = total
    moves.send(0)


def layout_kernel(moves, shares, out):
    rows, lanes = shares.shape[1] // 2, shares.shape[2]
    cols = lanes // 2
    for core in range(CORE):
        here = slice(core * rows, (core + 1) * rows)
        for pair in range(DP // 2):
            left, right = shares[2 * pair, here], shares[2 * pair + 1, here]
            at = core * DP * cols + pair * lanes
            out[:rows, at : at + lanes] = jnp.concatenate([left[:, :cols], right[:, :cols]], 1)
            out[rows:, at : at + lanes] = jnp.concatenate([left[:, cols:], right[:, cols:]], 1)
    moves.send(0)


def on_device(sensor_feats, text_embeds, proj_weight, matches, log_scale, logit_bias):
    sensor = sensor_feats[0]
    texts = text_embeds[0]
    rows = sensor.shape[0]
    feat, width = proj_weight.shape
    loop_index = lax.axis_index("loop")
    place = loop_index.reshape(1)

    slot = {0: texts}
    slot[1], slot[-1] = shift_z(texts, -1), shift_z(texts, 1)

    sensor_yh = swap_yh(sensor)
    match = matches.reshape(1, rows)
    match_yh = swap_yh(match)
    up, down, _, _ = lax.optimization_barrier((slot[1], slot[-1], sensor_yh, match_yh))
    slot[2], slot[-2] = shift_z(up, -1), shift_z(down, 1)
    sensor_later, sensor_yh_later, _, _, _ = lax.optimization_barrier((sensor, sensor_yh, match_yh, slot[1], slot[-1]))
    sensors = [sensor, swap_core(sensor_later), sensor_yh, swap_core(sensor_yh_later)]
    match_both = swap_core(jnp.concatenate([match, match_yh], 0))
    match = [match, match_both[:1], match_yh, match_both[1:]]
    image_emb, image_inv, numbers = call(
        project_kernel,
        [jax.ShapeDtypeStruct(*s) for s in (((4 * rows, width), BF16), ((4 * rows, 1), F32), ((8, 128), F32))],
        {},
        proj_weight, *sensors, log_scale.reshape(1), logit_bias.reshape(1),
        far=(0,),
        packed=range(1, 5),
        far_out=(1,),
        cuts={0: CUT},
        loose=range(2, 5),
    )
    up, down, _ = lax.optimization_barrier((slot[2], slot[-2], image_emb))
    slot[3], slot[-3] = shift_z(up, -1), shift_z(down, 1)
    far, _ = lax.optimization_barrier((down, match_both))
    slot[4] = shift_z(far, 2)

    text_shape = jax.ShapeDtypeStruct((rows, width), BF16)
    acc_shape = jax.ShapeDtypeStruct((4 * rows, width), F32)
    keys = (0, 1, -1, 2, -2)
    match_rows, acc, text_0, text_1, text_m1, text_2, text_m2 = call(
        functools.partial(first_pairs_kernel, keys),
        [jax.ShapeDtypeStruct((4 * rows, 1), F32), acc_shape, jax.ShapeDtypeStruct((rows, width), F32)] + [text_shape] * 4,
        {},
        numbers, place, image_emb, *match, *(slot[k] for k in keys),
        packed=range(7, 12),
        far_out=range(2, 7),
    )
    text_far = {}
    for key in (-3, 3):
        acc, text_far[key] = call(
            functools.partial(pairs_kernel, (key,)),
            [acc_shape, text_shape],
            {5: 0},
            numbers, place, image_emb, match_rows, slot[key], acc,
            packed=(4,),
            far_out=(1,),
            loose=(4,),
        )
    text_3, text_m3 = text_far[3], text_far[-3]
    shapes = [((4 * rows, width), F32), ((4 * rows, 1), F32), ((4 * rows + 16, width // 2), BF16)]
    shapes.append(((4 * rows, rows), BF16))
    acc, dot, packet, last_grad = call(
        last_kernel,
        [jax.ShapeDtypeStruct(*s) for s in shapes],
        {5: 0},
        numbers, place, image_emb, match_rows, slot[4], acc,
    )

    got = swap_core(packet)
    weight_part, row_half, row_other, extra = call(
        weight_kernel,
        [jax.ShapeDtypeStruct((DP, width // 16, feat), BF16)] + [jax.ShapeDtypeStruct((2 * rows, width // 2), F32)] * 3,
        {},
        place, got, acc, dot, image_emb, image_inv, *sensors,
        far=(5,),
        far_out=(0, 1),
        pushed=(2, 3),
        sends=DP + 5,
    )
    last_grad, text_1, text_m1, text_3, text_m3, _ = lax.optimization_barrier(
        (last_grad, text_1, text_m1, text_3, text_m3, weight_part)
    )
    (text_4,) = call(
        last_text_kernel, [jax.ShapeDtypeStruct((rows, width), BF16)], {}, numbers, last_grad, image_emb, far_out=(0,)
    )
    shapes = [((rows, width), BF16), ((rows, width), F32)]
    row_send, row_keep = call(
        row_kernel,
        [jax.ShapeDtypeStruct(*s) for s in shapes],
        {},
        place, row_half, row_other, swap_core(extra),
        far=range(1, 4),
        far_out=(0, 1),
    )
    weight_part = lax.all_to_all(weight_part, "dp", 0, 0, tiled=True)

    per_loop = feat // LOOP
    block = (per_loop // 2, width // 8)
    (weight_chunks,) = call(
        chunk_kernel, [jax.ShapeDtypeStruct((LOOP,) + block, BF16)], {}, weight_part, far_out=(0,)
    )
    weight_part = lax.all_to_all(weight_chunks, "loop", 0, 0, tiled=True)
    (shares,) = call(
        share_kernel, [jax.ShapeDtypeStruct((DP, per_loop, width // 8), F32)], {}, weight_part, far_out=(0,)
    )

    from_below, from_above, far = shift_z(text_3, 1), shift_z(text_m3, -1), shift_z(text_4, 2)
    near_below, near_above = shift_z(text_1, 1), shift_z(text_m1, -1)
    row_got = swap_yh(row_send)
    from_below, from_above, far, near_below, near_above, row_got, _ = lax.optimization_barrier(
        (from_below, from_above, far, near_below, near_above, row_got, weight_chunks)
    )
    up, down = call(
        sums_kernel,
        [jax.ShapeDtypeStruct((rows, width), BF16)] * 2,
        {},
        text_2, from_below, far, text_m2, from_above,
        far=range(5),
        far_out=range(2),
        loose=(1, 2, 4),
    )
    up, down = shift_z(up, 2), shift_z(down, -2)

    (sensor_grad,) = call(
        sensor_kernel,
        [jax.ShapeDtypeStruct((rows, feat), BF16)],
        {},
        row_keep, row_got, image_inv, proj_weight, image_emb,
        far=range(4),
        far_out=(0,),
    )
    shares, _ = lax.optimization_barrier((shares, sensor_grad))
    up, down, _ = lax.optimization_barrier((up, down, shares))
    shares = lax.all_to_all(shares, "dp", 0, 0, tiled=True)
    (weight_grad,) = call(
        layout_kernel, [jax.ShapeDtypeStruct((per_loop, width), F32)], {}, shares, far_out=(0,)
    )
    (text_grad,) = call(
        text_kernel,
        [jax.ShapeDtypeStruct((rows, width), F32)],
        {},
        texts, text_0, near_below, near_above, up, down,
        far=range(6),
        far_out=(0,),
        loose=(4, 5),
    )
    return (sensor_grad[None], text_grad[None], weight_grad)


def solution(mesh):
    placed = (P("dp", "loop", None), P("dp", "loop", None), P(), P("dp", "loop"), P(), P())
    return jax.shard_map(
        on_device,
        mesh=mesh,
        in_specs=placed,
        out_specs=(P("dp", "loop", None), P("dp", "loop", None), P("loop", None)),
        check_vma=False,
    )
```

```python
import functools

import jax
import jax.numpy as jnp
from jax import lax
from jax.experimental import pallas as pl
from jax.experimental.pallas import tpu as pltpu
from jax.sharding import PartitionSpec as P

Z, YH, CORE = 8, 2, 2
LOOP = Z * YH * CORE
DP = 8
CUT = 640
BF16 = jnp.bfloat16
F32 = jnp.float32
VMEM = pl.BlockSpec(memory_space=pltpu.VMEM)
HBM = pl.BlockSpec(memory_space=pltpu.HBM)
ANY = pl.BlockSpec(memory_space=pl.ANY)
SMEM = pl.BlockSpec(memory_space=pltpu.SMEM)


def route(move):
    pairs = []
    for z in range(Z):
        for y in range(YH):
            for c in range(CORE):
                to_z, to_y, to_c = move(z, y, c)
                source = (z * YH + y) * CORE + c
                pairs.append((source, ((to_z % Z) * YH + to_y) * CORE + to_c))
    return pairs


def shift_z(block, distance):
    return lax.ppermute(block, "loop", route(lambda z, y, c: (z + (1 - 2 * c) * distance, y, c)))


def swap_core(block):
    return lax.ppermute(block, "loop", route(lambda z, y, c: (z, y, 1 - c)))


def swap_yh(block):
    return lax.ppermute(block, "loop", route(lambda z, y, c: (z, 1 - y, c)))


def inner_rows(left, right):
    return lax.dot_general(left, right, (((1,), (1,)), ((), ())), preferred_element_type=F32)


def inner_cols(left, right):
    return lax.dot_general(left, right, (((0,), (0,)), ((), ())), preferred_element_type=F32)


class Moves:
    def __init__(self, base, sems, loads, held, outs, pack):
        self.base = base
        self.sems, self.loads, self.held, self.outs, self.pack, self.sent = sems, loads, held, outs, pack, []

    def need(self, n):
        self.loads[n].wait()

    def push(self, source, n, part):
        copy = pltpu.make_async_copy(source, self.outs[n].at[part], self.sems.at[self.base + len(self.sent)])
        copy.start()
        self.sent.append(copy)

    def send(self, n, part=None):
        source, target = self.held[n], self.outs[n]
        if part is not None:
            source, target = source.at[part], target.at[part]
        copy = pltpu.make_async_copy(source, target, self.sems.at[self.base + len(self.sent)])
        copy.start()
        self.sent.append(copy)


def call(kernel, out, aliases, *operands, far=(), packed=(), far_out=(), pushed=(), sends=None, cuts=(), loose=()):
    cuts = dict(cuts)
    far, packed, far_out, total = list(far), list(packed), list(far_out), len(operands)
    sends = len(far_out) if sends is None else sends

    def body(*refs):
        ins, outs, scratch = refs[:total], refs[total : total + len(out)], refs[total + len(out) :]
        held = dict(zip(far, scratch[: len(far)]))
        held_out = dict(zip(far_out, scratch[len(far) : len(far) + len(far_out)]))
        for m, n in enumerate(packed):
            height = operands[n].shape[0]
            held[n] = scratch[-2].at[pl.ds(m * height, height)]
        whole = [(m, n) for m, n in enumerate(in_hbm) if n not in cuts]
        loads = {n: pltpu.make_async_copy(ins[n], held[n], scratch[-1].at[m]) for m, n in whole}
        for n, cut in cuts.items():
            for m, part in enumerate((pl.ds(0, cut), pl.ds(cut, operands[n].shape[0] - cut))):
                sem = scratch[-1].at[len(in_hbm) + sends] if m else scratch[-1].at[far.index(n)]
                loads[n, m] = pltpu.make_async_copy(ins[n].at[part], held[n].at[part], sem)
        for load in loads.values():
            load.start()
        moves = Moves(len(in_hbm), scratch[-1], loads, held_out, outs, scratch[-2] if packed else None)
        kernel(moves, *(held.get(n, ref) for n, ref in enumerate(ins)), *(held_out.get(n, ref) for n, ref in enumerate(outs)))
        for copy in moves.sent:
            copy.wait()

    in_hbm, out_hbm = far + packed, far_out + list(pushed)
    in_specs = [SMEM if o.ndim == 1 else HBM if n in in_hbm else VMEM for n, o in enumerate(operands)]
    in_specs = [ANY if n in loose else spec for n, spec in enumerate(in_specs)]
    scratch = [pltpu.VMEM(operands[n].shape, operands[n].dtype) for n in far]
    scratch += [pltpu.VMEM(out[n].shape, out[n].dtype) for n in far_out]
    if packed:
        height, width = operands[packed[0]].shape
        scratch.append(pltpu.VMEM((len(packed) * height, width), operands[packed[0]].dtype))
    scratch.append(pltpu.SemaphoreType.DMA((len(in_hbm) + sends + 1,)))
    operands = [o if n in loose or n not in in_hbm else pltpu.with_memory_space_constraint(o, pltpu.HBM) for n, o in enumerate(operands)]
    return pl.pallas_call(
        body,
        out_shape=[pltpu.HBM(o.shape, o.dtype) if n in out_hbm else o for n, o in enumerate(out)],
        in_specs=in_specs,
        out_specs=[HBM if n in out_hbm else VMEM for n in range(len(out))],
        scratch_shapes=scratch,
        input_output_aliases=aliases,
        cost_estimate=pl.CostEstimate(flops=1, bytes_accessed=1, transcendentals=0),
        compiler_params=pltpu.CompilerParams(vmem_limit_bytes=20 << 20),
    )(*operands)


def scale_of(numbers):
    return numbers[0:1, 0:1]


def block_grads(numbers, columns, image_emb, match, text):
    wide = text.astype(F32)
    inv = lax.rsqrt(jnp.sum(wide * wide, -1, keepdims=True) + 1e-06)
    emb = (wide * inv).astype(BF16)
    logits = scale_of(numbers) * inner_rows(image_emb, emb) + numbers[1:2, 0:1]
    positive = (match == columns).astype(F32)
    return emb, (jax.nn.sigmoid(logits) - positive).astype(BF16)


def columns_of(place, key, rows):
    step = (1 - 2 * (place[0] & 1)) * (YH * CORE)
    start = (place[0] + key * step + LOOP) % LOOP * rows
    return (lax.broadcasted_iota(jnp.int32, (1, rows), 1) + start).astype(F32)


def pairs_body(keys, moves, first, numbers, place, image_emb, match, texts, acc_in, acc_out, text_out):
    count = len(keys)
    image = image_emb[...]
    rows = texts[0].shape[0]
    columns = jnp.concatenate([columns_of(place, key, rows) for key in keys], 1)
    for n in range(count):
        moves.need(first + n)
    emb, grad = block_grads(numbers, columns, image, match[...], moves.pack[...])
    text_part = scale_of(numbers) * inner_cols(grad, image)
    shift = 2 if acc_in is None else 1
    for n in range(count):
        text_out[n][...] = text_part[n * rows : (n + 1) * rows].astype(text_out[n].dtype)
        moves.send(shift + n)
    part = jnp.dot(grad, emb, preferred_element_type=F32)
    acc_out[...] = part if acc_in is None else acc_in[...] + part


def pairs_kernel(keys, moves, numbers, place, image_emb, match, *refs):
    count = len(keys)
    pairs_body(keys, moves, 4, numbers, place, image_emb, match, refs[:count], refs[count], refs[count + 1], refs[count + 2 :])


def project_kernel(moves, proj_weight, own, core, yh, both, log_scale, bias, emb, inv_out, numbers):
    for n in range(4):
        moves.need(1 + n)
    sensor = moves.pack[...]
    moves.need((0, 0))
    projected = jnp.dot(sensor[:, :CUT], proj_weight[:CUT], preferred_element_type=F32)
    moves.need((0, 1))
    projected = projected + jnp.dot(sensor[:, CUT:], proj_weight[CUT:], preferred_element_type=F32)
    inv = lax.rsqrt(jnp.sum(projected * projected, -1, keepdims=True) + 1e-06)
    inv_out[...] = inv
    moves.send(1)
    emb[...] = (projected * inv).astype(BF16)
    row = lax.broadcasted_iota(jnp.int32, numbers.shape, 0)
    scale = jnp.exp(jnp.full(numbers.shape, log_scale[0], F32))
    numbers[...] = jnp.where(row == 0, scale, bias[0])


def first_pairs_kernel(keys, moves, numbers, place, image_emb, own, core, yh, both, *refs):
    texts, match, outs = refs[: len(keys)], refs[len(keys)], refs[len(keys) + 1 :]
    block = own.shape[1]
    for n, line in enumerate((own, core, yh, both)):
        turned = jnp.broadcast_to(line[...].astype(F32), (128, block)).T
        match[n * block : (n + 1) * block, :] = turned[:, 0:1]
    pairs_body(keys, moves, 7, numbers, place, image_emb, match, texts, None, outs[0], outs[1:])


def last_kernel(moves, numbers, place, image_emb, match, text, acc_in, acc_out, dot_out, packet, grad_out):
    columns = columns_of(place, 4, text.shape[0])
    emb, grad = block_grads(numbers, columns, image_emb[...], match[...], text[...])
    grad_out[...] = grad
    acc = scale_of(numbers) * (acc_in[...] + jnp.dot(grad, emb, preferred_element_type=F32))
    acc_out[...] = acc
    dot = jnp.sum(image_emb[...].astype(F32) * acc, -1, keepdims=True)
    dot_out[...] = dot
    rows, width = acc.shape
    half, block = width // 2, rows // 4
    core = place[0] & 1
    other = pl.ds(pl.multiple_of((1 - core) * half, half), half)
    packet[:rows, :] = acc_out[:, other].astype(BF16)
    lines = []
    for slot in range(4):
        mine = slice(slot * block, (slot + 1) * block)
        flat = jnp.broadcast_to(dot[mine], (block, 128)).T[0:1, :]
        top = flat.astype(BF16).astype(F32)
        lines.append(jnp.concatenate([top, flat - top, jnp.zeros((1, half - 256), F32)], 1))
    lines.append(jnp.zeros((packet.shape[0] - rows - 4, half), F32))
    packet[rows:, :] = jnp.concatenate(lines, 0).astype(BF16)


def last_text_kernel(moves, numbers, grad, image_emb, out):
    out[...] = (scale_of(numbers) * inner_cols(grad[...], image_emb[...])).astype(out.dtype)
    moves.send(0)


def weight_kernel(moves, place, got, acc, dot, image_emb, inv, own_rows, core_rows, yh_rows, both_rows, weight, row_half, row_other, extra):
    rows, width = acc.shape
    half, quarter, block = width // 2, width // 4, rows // 4
    core = place[0] & 1
    own = pl.ds(pl.multiple_of(core * half, half), half)
    other = pl.ds(pl.multiple_of((1 - core) * half, half), half)
    for n in range(2):
        here = pl.ds(n * block, block)
        moves.push(acc.at[pl.ds((2 * n + 1) * block, block), own], 3, here)
        moves.push(acc.at[pl.ds(2 * n * block, block), other], 2, here)
    digits = got[rows:, :256].astype(F32)
    moves.need(5)
    projs = []
    for slot in range(4):
        mine = slice(slot * block, (slot + 1) * block)
        theirs = slice((slot ^ 1) * block, ((slot ^ 1) + 1) * block)
        kept = acc[mine, own] + got[theirs, :].astype(F32)
        if slot in (0, 2):
            row_half[slot // 2 * block : (slot // 2 + 1) * block, :] = kept
            if slot == 2:
                moves.send(1)
        line = digits[slot ^ 1 : (slot ^ 1) + 1, :]
        other_dot = jnp.broadcast_to(line[:, :128] + line[:, 128:], (block, 128)).T[:, 0:1]
        unit = image_emb[mine, own].astype(F32)
        projs.append(((kept - unit * (dot[mine, :] + other_dot)) * inv[mine, :]).astype(BF16))
    proj = jnp.concatenate(projs, 0)
    sensor = jnp.concatenate([own_rows[...], core_rows[...], yh_rows[...], both_rows[...]], 0)
    chunk = weight.shape[1]
    for side in range(2):
        product = inner_cols(proj[:, side * quarter : (side + 1) * quarter], sensor).astype(BF16)
        for m in range(quarter // chunk):
            at = side * (quarter // chunk) + m
            weight[at] = product[m * chunk : (m + 1) * chunk]
            moves.send(0, at)


def row_kernel(moves, place, row_half, row_other, extra, row_send, row_keep):
    block, half = row_half.shape[0] // 2, row_half.shape[1]
    core = place[0] & 1
    own = pl.ds(pl.multiple_of(core * half, half), half)
    other = pl.ds(pl.multiple_of((1 - core) * half, half), half)
    for n in range(3):
        moves.need(1 + n)
    for n, target in ((1, row_send), (0, row_keep)):
        here = slice(n * block, (n + 1) * block)
        target[:, own] = row_half[here, :].astype(target.dtype)
        target[:, other] = (row_other[here, :] + extra[here, :]).astype(target.dtype)
        moves.send(1 - n)


def sums_kernel(moves, text_2, below, far, text_m2, above, up, down):
    for n in range(3):
        moves.need(n)
    up[...] = (text_2[...].astype(F32) + below[...].astype(F32) + far[...].astype(F32)).astype(BF16)
    moves.send(0)
    moves.need(3)
    moves.need(4)
    down[...] = (text_m2[...].astype(F32) + above[...].astype(F32)).astype(BF16)
    moves.send(1)


def text_kernel(moves, text, own, near_below, near_above, up, down, out):
    for n in range(6):
        moves.need(n)
    total = own[...] + near_below[...].astype(F32) + near_above[...].astype(F32)
    total = total + up[...].astype(F32) + down[...].astype(F32)
    wide = text[...].astype(F32)
    inv = lax.rsqrt(jnp.sum(wide * wide, -1, keepdims=True) + 1e-06)
    unit = wide * inv
    out[...] = (total - unit * jnp.sum(unit * total, -1, keepdims=True)) * inv
    moves.send(0)


def sensor_kernel(moves, row_keep, row_got, inv, proj_weight, image_emb, out):
    rows = row_keep.shape[0]
    for n in range(3):
        moves.need(n)
    image_grad = row_keep[...] + row_got[...].astype(F32)
    unit = image_emb[:rows, :].astype(F32)
    dot = jnp.sum(unit * image_grad, -1, keepdims=True)
    proj_grad = ((image_grad - unit * dot) * inv[:rows, :]).astype(BF16)
    moves.need(3)
    out[...] = inner_rows(proj_grad, proj_weight[...]).astype(BF16)
    moves.send(0)


def chunk_kernel(moves, parts, out):
    total = parts[0].astype(F32)
    for n in range(1, parts.shape[0]):
        total = total + parts[n].astype(F32)
    turned = total.T
    count, rows, lanes = out.shape
    for n in range(count):
        at = 2 * rows * n
        out[n] = jnp.concatenate([turned[at : at + rows], turned[at + rows : at + 2 * rows]], 1).astype(BF16)
    moves.send(0)


def share_kernel(moves, parts, out):
    rows = parts.shape[1]
    for core in range(CORE):
        total = parts[core].astype(F32)
        for n in range(1, Z * YH):
            total = total + parts[n * CORE + core].astype(F32)
        total = total * (1.0 / DP)
        for n in range(DP):
            out[n, core * rows : (core + 1) * rows] = total
    moves.send(0)


def layout_kernel(moves, shares, out):
    rows, lanes = shares.shape[1] // 2, shares.shape[2]
    cols = lanes // 2
    for core in range(CORE):
        here = slice(core * rows, (core + 1) * rows)
        for pair in range(DP // 2):
            left, right = shares[2 * pair, here], shares[2 * pair + 1, here]
            at = core * DP * cols + pair * lanes
            out[:rows, at : at + lanes] = jnp.concatenate([left[:, :cols], right[:, :cols]], 1)
            out[rows:, at : at + lanes] = jnp.concatenate([left[:, cols:], right[:, cols:]], 1)
    moves.send(0)


def on_device(sensor_feats, text_embeds, proj_weight, matches, log_scale, logit_bias):
    sensor = sensor_feats[0]
    texts = text_embeds[0]
    rows = sensor.shape[0]
    feat, width = proj_weight.shape
    loop_index = lax.axis_index("loop")
    place = loop_index.reshape(1)

    slot = {0: texts}
    slot[1], slot[-1] = shift_z(texts, -1), shift_z(texts, 1)

    sensor_yh = swap_yh(sensor)
    match = matches.reshape(1, rows)
    match_yh = swap_yh(match)
    up, down, _, _ = lax.optimization_barrier((slot[1], slot[-1], sensor_yh, match_yh))
    slot[2], slot[-2] = shift_z(up, -1), shift_z(down, 1)
    sensor_later, sensor_yh_later, _, _, _ = lax.optimization_barrier((sensor, sensor_yh, match_yh, slot[1], slot[-1]))
    sensors = [sensor, swap_core(sensor_later), sensor_yh, swap_core(sensor_yh_later)]
    image_emb, image_inv, numbers = call(
        project_kernel,
        [jax.ShapeDtypeStruct(*s) for s in (((4 * rows, width), BF16), ((4 * rows, 1), F32), ((8, 128), F32))],
        {},
        proj_weight, *sensors, log_scale.reshape(1), logit_bias.reshape(1),
        far=(0,),
        packed=range(1, 5),
        far_out=(1,),
        cuts={0: CUT},
        loose=range(2, 5),
    )
    up, down, _ = lax.optimization_barrier((slot[2], slot[-2], image_emb))
    slot[3], slot[-3] = shift_z(up, -1), shift_z(down, 1)
    match_pair, _ = lax.optimization_barrier((jnp.concatenate([match, match_yh], 0), image_emb))
    match_both = swap_core(match_pair)
    match = [match, match_both[:1], match_yh, match_both[1:]]
    far, _ = lax.optimization_barrier((down, match_both))
    slot[4] = shift_z(far, 2)

    text_shape = jax.ShapeDtypeStruct((rows, width), BF16)
    acc_shape = jax.ShapeDtypeStruct((4 * rows, width), F32)
    keys = (0, 1, -1, 2, -2)
    match_rows, acc, text_0, text_1, text_m1, text_2, text_m2 = call(
        functools.partial(first_pairs_kernel, keys),
        [jax.ShapeDtypeStruct((4 * rows, 1), F32), acc_shape, jax.ShapeDtypeStruct((rows, width), F32)] + [text_shape] * 4,
        {},
        numbers, place, image_emb, *match, *(slot[k] for k in keys),
        packed=range(7, 12),
        far_out=range(2, 7),
    )
    text_far = {}
    for key in (-3, 3):
        acc, text_far[key] = call(
            functools.partial(pairs_kernel, (key,)),
            [acc_shape, text_shape],
            {5: 0},
            numbers, place, image_emb, match_rows, slot[key], acc,
            packed=(4,),
            far_out=(1,),
            loose=(4,),
        )
    text_3, text_m3 = text_far[3], text_far[-3]
    shapes = [((4 * rows, width), F32), ((4 * rows, 1), F32), ((4 * rows + 16, width // 2), BF16)]
    shapes.append(((4 * rows, rows), BF16))
    acc, dot, packet, last_grad = call(
        last_kernel,
        [jax.ShapeDtypeStruct(*s) for s in shapes],
        {5: 0},
        numbers, place, image_emb, match_rows, slot[4], acc,
    )

    got = swap_core(packet)
    weight_part, row_half, row_other, extra = call(
        weight_kernel,
        [jax.ShapeDtypeStruct((DP, width // 16, feat), BF16)] + [jax.ShapeDtypeStruct((2 * rows, width // 2), F32)] * 3,
        {},
        place, got, acc, dot, image_emb, image_inv, *sensors,
        far=(5,),
        far_out=(0, 1),
        pushed=(2, 3),
        sends=DP + 5,
    )
    last_grad, text_1, text_m1, text_3, text_m3, _ = lax.optimization_barrier(
        (last_grad, text_1, text_m1, text_3, text_m3, weight_part)
    )
    (text_4,) = call(
        last_text_kernel, [jax.ShapeDtypeStruct((rows, width), BF16)], {}, numbers, last_grad, image_emb, far_out=(0,)
    )
    shapes = [((rows, width), BF16), ((rows, width), F32)]
    row_send, row_keep = call(
        row_kernel,
        [jax.ShapeDtypeStruct(*s) for s in shapes],
        {},
        place, row_half, row_other, swap_core(extra),
        far=range(1, 4),
        far_out=(0, 1),
    )
    weight_part = lax.all_to_all(weight_part, "dp", 0, 0, tiled=True)

    per_loop = feat // LOOP
    block = (per_loop // 2, width // 8)
    (weight_chunks,) = call(
        chunk_kernel, [jax.ShapeDtypeStruct((LOOP,) + block, BF16)], {}, weight_part, far_out=(0,)
    )
    weight_part = lax.all_to_all(weight_chunks, "loop", 0, 0, tiled=True)
    (shares,) = call(
        share_kernel, [jax.ShapeDtypeStruct((DP, per_loop, width // 8), F32)], {}, weight_part, far_out=(0,)
    )

    from_below, from_above, far = shift_z(text_3, 1), shift_z(text_m3, -1), shift_z(text_4, 2)
    near_below, near_above = shift_z(text_1, 1), shift_z(text_m1, -1)
    row_got = swap_yh(row_send)
    from_below, from_above, far, near_below, near_above, row_got, _ = lax.optimization_barrier(
        (from_below, from_above, far, near_below, near_above, row_got, weight_chunks)
    )
    up, down = call(
        sums_kernel,
        [jax.ShapeDtypeStruct((rows, width), BF16)] * 2,
        {},
        text_2, from_below, far, text_m2, from_above,
        far=range(5),
        far_out=range(2),
        loose=(1, 2, 4),
    )
    up, down = shift_z(up, 2), shift_z(down, -2)

    (sensor_grad,) = call(
        sensor_kernel,
        [jax.ShapeDtypeStruct((rows, feat), BF16)],
        {},
        row_keep, row_got, image_inv, proj_weight, image_emb,
        far=range(4),
        far_out=(0,),
    )
    shares, _ = lax.optimization_barrier((shares, sensor_grad))
    up, down, _ = lax.optimization_barrier((up, down, shares))
    shares = lax.all_to_all(shares, "dp", 0, 0, tiled=True)
    (weight_grad,) = call(
        layout_kernel, [jax.ShapeDtypeStruct((per_loop, width), F32)], {}, shares, far_out=(0,)
    )
    (text_grad,) = call(
        text_kernel,
        [jax.ShapeDtypeStruct((rows, width), F32)],
        {},
        texts, text_0, near_below, near_above, up, down,
        far=range(6),
        far_out=(0,),
        loose=(4, 5),
    )
    return (sensor_grad[None], text_grad[None], weight_grad)


def solution(mesh):
    placed = (P("dp", "loop", None), P("dp", "loop", None), P(), P("dp", "loop"), P(), P())
    return jax.shard_map(
        on_device,
        mesh=mesh,
        in_specs=placed,
        out_specs=(P("dp", "loop", None), P("dp", "loop", None), P("loop", None)),
        check_vma=False,
    )
```
